32 devices in a mesh: groups: 2 (over y), rows: 8 (over z, x), sub: 2 (over core).
Axes of the slice: x: 2, y: 2, z: 4, core: 2. Of those that a mesh axis runs over, the one named last changes fastest.
Arguments:
- embeddings: bfloat16 [49152, 1024], P(('groups', 'rows', 'sub')), parts along dimension 0, may hold values from -100 to 100
- pair_blocks: int32 [2, 864], P(None, ('groups', 'rows', 'sub')), parts along dimension 1, may hold values from 0 to 95, as said below
- pair_count: int32 [32], P(('groups', 'rows', 'sub')), parts along dimension 0, may hold values from 6 to 27, as said below
Outputs:
- dup_weight: float32 [49152], P(('groups', 'rows', 'sub')), parts along dimension 0
- neighbour_mean: float32 [49152, 1024], P(('groups', 'rows', 'sub')), parts along dimension 0
The draws below stay inside these ranges and needn't reach their ends.
There are 2 independent parts, one for each index of `groups`. The reference program is written for one: setup_inputs(seed, part) draws one part's arguments, and reference() takes and returns one part's arrays. A program takes and returns all parts, laid end to end along the dimension named above; each array names one. Nothing has to cross between parts.
Inputs may be any that keep to these rules, and one draw needn't show every extreme that they name: `pair_blocks`: of device d's 27 slots (columns d * 27 onward) the first pair_count[d] hold every pair (i, j), i <= j, of blocks of one cluster with i among blocks d * 6 to d * 6 + 5, ordered by i and then j; clusters are runs of 1 to 7 consecutive blocks covering all 96 blocks. The other slots hold a pair (i, i) with i among the device's blocks. pair_count[d] is the number of such pairs of device d.
All inputs are finite; a program needn't handle non-finite values.
Results may differ from the reference program's by a relative error of at most 0.0015.
Values may be sent and summed in bfloat16 or wider, within the bound.
No kernel may reach another device: no remote copies, remote signals or barrier semaphores. Data moves between devices by JAX's collectives and lax.ppermute only.
A program may use at most 64 MiB of HBM per device.

```python
import jax
import jax.numpy as jnp
from jax import lax

D = 1024
BLK = 256
BLK_DEV = 6
DEVS = 16
BLOCKS = 96
ROWS = 24576
CLUSTER = 7
PMAX = 27
PAIRS = 432


def cluster_layout(key):
    positions = jnp.arange(BLOCKS, dtype=jnp.int32)
    lengths = jax.random.randint(key, (BLOCKS,), 1, CLUSTER + 1, dtype=jnp.int32)
    opening = jnp.cumsum(lengths) - lengths
    in_range = opening < BLOCKS
    starts = jnp.zeros((BLOCKS,), jnp.int32).at[jnp.where(in_range, opening, 0)].max(jnp.where(in_range, 1, 0).astype(jnp.int32))
    chosen = jax.random.randint(jax.random.fold_in(key, 11), (), 0, DEVS - 1, dtype=jnp.int32)
    forced_first = chosen * BLK_DEV
    within = (positions > forced_first) & (positions < forced_first + CLUSTER)
    starts = jnp.where(within, 0, starts)
    starts = jnp.where((positions == forced_first) | (positions == forced_first + CLUSTER) | (positions == 0), 1, starts)
    upcoming = jnp.where(starts == 1, positions, BLOCKS)
    upcoming = jnp.concatenate([upcoming[1:], jnp.full((1,), BLOCKS, jnp.int32)])
    span_sizes = (lax.cummin(upcoming, axis=0, reverse=True) - positions).reshape(DEVS, BLK_DEV)
    offsets = jnp.cumsum(span_sizes, axis=1) - span_sizes
    totals = jnp.sum(span_sizes, axis=1).astype(jnp.int32)
    slot_ids = jnp.arange(PMAX, dtype=jnp.int32)
    holder = jnp.sum((offsets[:, None, :] <= slot_ids[None, :, None]).astype(jnp.int32), axis=2) - 1
    slot_start = jnp.take_along_axis(offsets, holder, axis=1)
    first_block = jnp.arange(DEVS, dtype=jnp.int32)[:, None] * BLK_DEV + holder
    second_block = first_block + slot_ids[None, :] - slot_start
    alive = slot_ids[None, :] < totals[:, None]
    return (first_block, second_block, alive, totals)


def draw_pair_blocks(key, part):
    first_block, second_block, alive, totals = cluster_layout(key)
    key = jax.random.fold_in(key, 3)
    filler = jax.random.randint(key, (DEVS, PMAX), 0, BLK_DEV, dtype=jnp.int32) + jnp.arange(DEVS, dtype=jnp.int32)[:, None] * BLK_DEV
    first_block = jnp.where(alive, first_block, filler)
    second_block = jnp.where(alive, second_block, filler)
    return jnp.stack([first_block.reshape(-1), second_block.reshape(-1)]).astype(jnp.int32)


def draw_pair_count(key, part):
    first_block, second_block, alive, totals = cluster_layout(key)
    return totals


def draw_embeddings(key, part):
    key = jax.random.fold_in(key, 5)
    key_center, key_mix, key_noise, key_scale, key_column = jax.random.split(key, 5)
    group_rows = max(BLK // 8, 1)
    centers = jnp.clip(jax.random.normal(key_center, (ROWS // group_rows, D), jnp.float32), -5.0, 5.0)
    repeated = jnp.repeat(centers, group_rows, axis=0)
    mixing = jax.random.uniform(key_mix, (ROWS, 1), jnp.float32, 0.6, 2.0)
    noise = jnp.clip(jax.random.normal(key_noise, (ROWS, D), jnp.float32), -5.0, 5.0)
    row_scale = jnp.exp(jax.random.uniform(key_scale, (ROWS, 1), jnp.float32, jnp.log(0.3), jnp.log(3.0)))
    column_scale = jnp.exp(jax.random.uniform(key_column, (1, D), jnp.float32, jnp.log(0.5), jnp.log(2.0)))
    values = (mixing * repeated + noise) * row_scale * column_scale
    return values.astype(jnp.bfloat16)


def setup_inputs(seed: int = 0, part: int = 0) -> dict:
    key_of = jax.random.split(jax.random.key(seed), 4)
    part_splits = jax.random.split(jax.random.fold_in(key_of[3], part), 4)
    return {
        "embeddings": draw_embeddings(jax.random.fold_in(jax.random.fold_in(key_of[3], part), 71), part),
        "pair_blocks": draw_pair_blocks(jax.random.fold_in(jax.random.fold_in(key_of[3], part), 71), part),
        "pair_count": draw_pair_count(jax.random.fold_in(jax.random.fold_in(key_of[3], part), 71), part),
    }


TEMPER = 4.0

def inverse_norms(row_block):
    widened = row_block.astype(jnp.float32)
    return lax.rsqrt(lax.optimization_barrier(jnp.sum(widened * widened, axis=1)) + 1e-06)

def add_rows(totals, weight_sums, block_index, term, row_sum):
    row_start = (block_index * BLK).astype(jnp.int32)
    old_rows = lax.dynamic_slice_in_dim(totals, row_start, BLK, 0)
    totals = lax.dynamic_update_slice_in_dim(totals, old_rows + term, row_start, 0)
    old_sums = lax.dynamic_slice_in_dim(weight_sums, row_start, BLK, 0)
    weight_sums = lax.dynamic_update_slice_in_dim(weight_sums, old_sums + row_sum, row_start, 0)
    return (totals, weight_sums)

def reference(embeddings, pair_blocks, pair_count):
    inverse = inverse_norms(embeddings)
    slot_ids = jnp.arange(PAIRS, dtype=jnp.int32)
    alive = slot_ids % PMAX < pair_count[slot_ids // PMAX]
    ordering = jnp.argsort(jnp.where(alive, 0, 1).astype(jnp.int32), stable=True).astype(jnp.int32)
    live_count = jnp.sum(alive.astype(jnp.int32))
    totals = jnp.zeros(embeddings.shape, jnp.float32)
    weight_sums = jnp.zeros((embeddings.shape[0],), jnp.float32)

    def visit(step_index, running):
        slot_index = ordering[step_index]
        first_block = pair_blocks[0, slot_index].astype(jnp.int32)
        second_block = pair_blocks[1, slot_index].astype(jnp.int32)
        left_rows = lax.dynamic_slice_in_dim(embeddings, first_block * BLK, BLK, 0)
        right_rows = lax.dynamic_slice_in_dim(embeddings, second_block * BLK, BLK, 0)
        left_inv = lax.dynamic_slice_in_dim(inverse, first_block * BLK, BLK, 0)
        right_inv = lax.dynamic_slice_in_dim(inverse, second_block * BLK, BLK, 0)
        inner_prod = jnp.dot(left_rows, right_rows.T, preferred_element_type=jnp.float32)
        similar = inner_prod * left_inv[:, None] * right_inv[None, :]
        weight = jnp.exp(TEMPER * (similar - 1.0))
        packed = weight.astype(jnp.bfloat16)
        totals, weight_sums = add_rows(running[0], running[1], first_block, jnp.dot(packed, right_rows, preferred_element_type=jnp.float32), lax.optimization_barrier(jnp.sum(weight, axis=1)))
        factor = jnp.where(first_block != second_block, 1.0, 0.0).astype(jnp.float32)
        mirror_term = jnp.dot(packed.T, left_rows, preferred_element_type=jnp.float32) * factor
        return add_rows(totals, weight_sums, second_block, mirror_term, lax.optimization_barrier(jnp.sum(weight, axis=0)) * factor)
    totals, weight_sums = lax.fori_loop(0, live_count, visit, (totals, weight_sums))
    return (weight_sums, totals / weight_sums[:, None])
```

```python
import functools

import jax
import jax.numpy as jnp
import numpy as np
from jax import lax
from jax.experimental import pallas as pl
from jax.experimental.pallas import tpu as pltpu
from jax.sharding import PartitionSpec as P

BLK = 256
CLUSTER = 7
TEMPER = 4.0
EPS = 1e-06
LANES = 128
VMEM_LIMIT = 40 * 1024 * 1024

F32 = jnp.float32
BF16 = jnp.bfloat16

ODD, M_CHIP, T_CHIP, M_LINK, T_LINK = range(5)


def inverse_norm(rows):
    wide = rows.astype(F32)
    return lax.rsqrt(jnp.sum(wide * wide, axis=1, keepdims=True) + EPS)


def diagonal():
    return lax.broadcasted_iota(jnp.int32, (BLK, BLK), 0) == lax.broadcasted_iota(
        jnp.int32, (BLK, BLK), 1
    )


def to_row(column):
    return jnp.sum(jnp.where(diagonal(), column, 0.0), axis=0, keepdims=True)


def to_column(row):
    return jnp.sum(jnp.where(diagonal(), row, 0.0), axis=1, keepdims=True)


def store_sums(ref, column):
    row = to_row(column)
    ref[0, 0:1, :] = row[:, :LANES]
    ref[0, 1:2, :] = row[:, LANES:]


def load_sums(ref):
    return to_column(jnp.concatenate([ref[0, 0:1, :], ref[0, 1:2, :]], axis=1))


def weigh(rows, row_inv, others, other_inv):
    inner = lax.dot_general(rows, others, (((1,), (1,)), ((), ())), preferred_element_type=F32)
    weight = jnp.exp(inner * (TEMPER * row_inv) * other_inv - TEMPER)
    term = jnp.dot(weight.astype(BF16), others, preferred_element_type=F32)
    return jnp.sum(weight, axis=1, keepdims=True), term


def pair_cost(pairs, width):
    return pl.CostEstimate(
        flops=pairs * 4 * BLK * BLK * width,
        bytes_accessed=pairs * 2 * BLK * width,
        transcendentals=pairs * BLK * BLK,
    )


def local_kernel(blocks, counts, x_ref, acc_ref, sums_ref, inv_col, inv_row):
    step = pl.program_id(0)

    @pl.when(step == 0)
    def _():
        def norms(r, carry):
            inv = inverse_norm(x_ref[pl.ds(r * BLK, BLK), :])
            inv_col[pl.ds(r * BLK, BLK), :] = inv
            inv_row[r] = to_row(inv)
            return carry

        lax.fori_loop(0, blocks, norms, 0)

    first = jnp.int32(0)
    for r in range(blocks):
        ends = jnp.int32(r) + counts[r]
        first = jnp.where((ends <= step) & (r < step), ends, first)
    last = jnp.minimum(step + counts[step], blocks)
    rows = x_ref[pl.ds(step * BLK, BLK), :]
    row_inv = inv_col[pl.ds(step * BLK, BLK), :]
    for n in range(1, blocks + 1):

        @pl.when(last - first == n)
        def _(n=n):
            others = x_ref[pl.ds(pl.multiple_of(first * BLK, BLK), n * BLK), :]
            other_inv = jnp.concatenate([inv_row[first + k] for k in range(n)], axis=1)
            sums, term = weigh(rows, row_inv, others, other_inv)
            acc_ref[...] = term
            store_sums(sums_ref, sums)


def local_pairs(counts, x):
    length, width = x.shape
    blocks = length // BLK
    return pl.pallas_call(
        functools.partial(local_kernel, blocks),
        grid_spec=pltpu.PrefetchScalarGridSpec(
            num_scalar_prefetch=1,
            grid=(blocks,),
            in_specs=[pl.BlockSpec((length, width), lambda r, c: (0, 0))],
            out_specs=[
                pl.BlockSpec((BLK, width), lambda r, c: (r, 0)),
                pl.BlockSpec((1, 2, LANES), lambda r, c: (r, 0, 0)),
            ],
            scratch_shapes=[
                pltpu.VMEM((length, 1), F32),
                pltpu.VMEM((blocks, 1, BLK), F32),
            ],
        ),
        out_shape=[
            jax.ShapeDtypeStruct((length, width), F32),
            jax.ShapeDtypeStruct((blocks, 2, LANES), F32),
        ],
        compiler_params=pltpu.CompilerParams(vmem_limit_bytes=VMEM_LIMIT),
        cost_estimate=pair_cost(blocks * blocks // 2, width),
        name="local_pairs",
    )(counts, x)


def near_kernel(
    blocks, info, acc_ref, sums_in, x_ref, chip_ref, link_ref, out_ref, sums_ref, inv_row, inv_link
):
    step = pl.program_id(0)
    odd = info[ODD] == 1
    mine_chip, theirs_chip = info[M_CHIP], info[T_CHIP]
    mine_link, theirs_link = info[M_LINK], info[T_LINK]
    chip_first = jnp.where(odd, blocks - theirs_chip, 0)

    @pl.when(step == 0)
    def _():
        def norms(k, carry):
            place = chip_first + k
            rows = chip_ref[pl.ds(pl.multiple_of(place * BLK, BLK), BLK), :]
            inv_row[place] = to_row(inverse_norm(rows))
            return carry

        lax.fori_loop(0, theirs_chip, norms, 0)
        inv_link[...] = to_row(inverse_norm(link_ref[...]))

    from_head = step
    from_tail = blocks - 1 - step
    on_chip = jnp.where(odd, from_head, from_tail) < mine_chip
    on_link = jnp.where(odd, from_tail, from_head) < mine_link
    sums_ref[...] = sums_in[...]

    @pl.when(jnp.logical_not(on_chip | on_link))
    def _():
        out_ref[...] = acc_ref[...] * (1.0 / load_sums(sums_in))

    @pl.when(on_chip)
    def _():
        rows = x_ref[...]
        row_inv = inverse_norm(rows)
        out_ref[...] = acc_ref[...]

        def add(k, sums):
            place = chip_first + k
            others = chip_ref[pl.ds(pl.multiple_of(place * BLK, BLK), BLK), :]
            more, term = weigh(rows, row_inv, others, inv_row[place])
            out_ref[...] += term
            return sums + more

        sums = lax.fori_loop(0, theirs_chip, add, load_sums(sums_in))
        store_sums(sums_ref, sums)
        out_ref[...] = out_ref[...] * (1.0 / sums)

    @pl.when(on_link)
    def _():
        rows = x_ref[...]
        more, term = weigh(rows, inverse_norm(rows), link_ref[...], inv_link[...])
        sums = load_sums(sums_in) + more
        total = acc_ref[...] + term
        store_sums(sums_ref, sums)
        out_ref[...] = total * jnp.where(theirs_link == 1, 1.0 / sums, 1.0)


def near_pairs(info, acc, sums, x, chip_x, link_block):
    length, width = x.shape
    blocks = length // BLK
    row_spec = pl.BlockSpec((BLK, width), lambda r, c: (r, 0))
    sum_spec = pl.BlockSpec((1, 2, LANES), lambda r, c: (r, 0, 0))
    return pl.pallas_call(
        functools.partial(near_kernel, blocks),
        grid_spec=pltpu.PrefetchScalarGridSpec(
            num_scalar_prefetch=1,
            grid=(blocks,),
            in_specs=[
                row_spec,
                sum_spec,
                row_spec,
                pl.BlockSpec((length, width), lambda r, c: (0, 0)),
                pl.BlockSpec((BLK, width), lambda r, c: (0, 0)),
            ],
            out_specs=[row_spec, sum_spec],
            scratch_shapes=[
                pltpu.VMEM((blocks, 1, BLK), F32),
                pltpu.VMEM((1, BLK), F32),
            ],
        ),
        out_shape=[
            jax.ShapeDtypeStruct((length, width), F32),
            jax.ShapeDtypeStruct((blocks, 2, LANES), F32),
        ],
        compiler_params=pltpu.CompilerParams(vmem_limit_bytes=VMEM_LIMIT),
        cost_estimate=pair_cost(blocks * 2, width),
        name="near_pairs",
    )(info, acc, sums, x, chip_x, link_block)


def far_kernel(blocks, up, down, info, out_in, sums_in, x_ref, up_ref, down_ref, out_ref, sums_ref, inv_row):
    step = pl.program_id(0)
    for parity, mine, theirs, other_ref in ((0, down + 1, up, up_ref), (1, up + 1, down, down_ref)):

        @pl.when((info[ODD] == parity) & (step < mine))
        def _(theirs=theirs, other_ref=other_ref):
            @pl.when(step == 0)
            def _():
                for k in range(theirs):
                    inv_row[:, k * BLK : (k + 1) * BLK] = to_row(
                        inverse_norm(other_ref[k * BLK : (k + 1) * BLK, :])
                    )

            rows = x_ref[...]
            more, term = weigh(
                rows, inverse_norm(rows), other_ref[...], inv_row[:, : theirs * BLK]
            )
            sums = load_sums(sums_in) + more
            store_sums(sums_ref, sums)
            out_ref[...] = (out_in[...] + term) * (1.0 / sums)


def far_pairs(info, out, sums, x, up_blocks, down_blocks):
    length, width = x.shape
    blocks = length // BLK
    up, down = up_blocks.shape[0] // BLK, down_blocks.shape[0] // BLK

    def place(step, info):
        odd = info[ODD]
        mine = jnp.where(odd == 1, up + 1, down + 1)
        step = jnp.minimum(step, mine - 1)
        return jnp.where(odd == 1, blocks - 1 - step, step)

    row_spec = pl.BlockSpec((BLK, width), lambda s, c: (place(s, c), 0))
    sum_spec = pl.BlockSpec((1, 2, LANES), lambda s, c: (place(s, c), 0, 0))
    return pl.pallas_call(
        functools.partial(far_kernel, blocks, up, down),
        grid_spec=pltpu.PrefetchScalarGridSpec(
            num_scalar_prefetch=1,
            grid=(max(up, down) + 1,),
            in_specs=[
                row_spec,
                sum_spec,
                row_spec,
                pl.BlockSpec((up * BLK, width), lambda s, c: (0, 0)),
                pl.BlockSpec((down * BLK, width), lambda s, c: (0, 0)),
            ],
            out_specs=[row_spec, sum_spec],
            scratch_shapes=[pltpu.VMEM((1, max(up, down) * BLK), F32)],
        ),
        out_shape=[
            jax.ShapeDtypeStruct(out.shape, F32),
            jax.ShapeDtypeStruct(sums.shape, F32),
        ],
        input_output_aliases={1: 0, 2: 1},
        compiler_params=pltpu.CompilerParams(vmem_limit_bytes=VMEM_LIMIT),
        cost_estimate=pair_cost((up + 1) * (down + 1), width),
        name="far_pairs",
    )(info, out, sums, x, up_blocks, down_blocks)


def share_kernel(blocks, info, x_ref, link_ref, share_ref, acc, sums):
    step = pl.program_id(0)
    width = x_ref.shape[1]
    link = link_ref[...]

    @pl.when(step == 0)
    def _():
        acc[...] = jnp.zeros_like(acc)
        sums[...] = jnp.zeros_like(sums)

    @pl.when(step + 1 < info[M_LINK])
    def _():
        rows = x_ref[...]
        more, term = weigh(link, inverse_norm(link), rows, to_row(inverse_norm(rows)))
        acc[...] += term
        sums[...] += more

    @pl.when(step == blocks - 2)
    def _():
        share_ref[:, :width] = acc[...].astype(BF16)
        total = sums[...]
        high = total.astype(BF16)
        rest = total - high.astype(F32)
        middle = rest.astype(BF16)
        low = (rest - middle.astype(F32)).astype(BF16)
        lane = lax.broadcasted_iota(jnp.int32, (BLK, LANES), 1)
        parts = jnp.where(
            lane == 0,
            high.astype(F32),
            jnp.where(lane == 1, middle.astype(F32), jnp.where(lane == 2, low.astype(F32), 0.0)),
        )
        share_ref[:, width:] = parts.astype(BF16)


def share_of(info, x, link_block):
    length, width = x.shape
    blocks = length // BLK

    def place(step, info):
        step = jnp.minimum(step + 1, jnp.maximum(info[M_LINK] - 1, 1))
        return jnp.where(info[ODD] == 1, blocks - 1 - step, step)

    return pl.pallas_call(
        functools.partial(share_kernel, blocks),
        grid_spec=pltpu.PrefetchScalarGridSpec(
            num_scalar_prefetch=1,
            grid=(blocks - 1,),
            in_specs=[
                pl.BlockSpec((BLK, width), lambda s, c: (place(s, c), 0)),
                pl.BlockSpec((BLK, width), lambda s, c: (0, 0)),
            ],
            out_specs=pl.BlockSpec((BLK, width + LANES), lambda s, c: (0, 0)),
            scratch_shapes=[pltpu.VMEM((BLK, width), F32), pltpu.VMEM((BLK, 1), F32)],
        ),
        out_shape=jax.ShapeDtypeStruct((BLK, width + LANES), BF16),
        compiler_params=pltpu.CompilerParams(vmem_limit_bytes=VMEM_LIMIT),
        cost_estimate=pair_cost(blocks // 2, width),
        name="share_of_single",
    )(info, x, link_block)


def add_share_kernel(info, out_in, sums_in, share_ref, out_ref, sums_ref):
    width = out_ref.shape[1]
    gets = info[T_LINK] > 1

    @pl.when(gets)
    def _():
        sums = load_sums(sums_in) + jnp.sum(
            share_ref[:, width:].astype(F32), axis=1, keepdims=True
        )
        store_sums(sums_ref, sums)
        out_ref[...] = (out_in[...] + share_ref[:, :width].astype(F32)) * (1.0 / sums)

    @pl.when(jnp.logical_not(gets))
    def _():
        sums_ref[...] = sums_in[...]
        out_ref[...] = out_in[...]


def add_share(info, out, sums, share):
    length, width = out.shape
    blocks = length // BLK

    def place(info):
        return jnp.where(info[ODD] == 1, blocks - 1, 0)

    row_spec = pl.BlockSpec((BLK, width), lambda s, c: (place(c), 0))
    sum_spec = pl.BlockSpec((1, 2, LANES), lambda s, c: (place(c), 0, 0))
    return pl.pallas_call(
        add_share_kernel,
        grid_spec=pltpu.PrefetchScalarGridSpec(
            num_scalar_prefetch=1,
            grid=(1,),
            in_specs=[
                row_spec,
                sum_spec,
                pl.BlockSpec((BLK, width + LANES), lambda s, c: (0, 0)),
            ],
            out_specs=[row_spec, sum_spec],
        ),
        out_shape=[
            jax.ShapeDtypeStruct(out.shape, F32),
            jax.ShapeDtypeStruct(sums.shape, F32),
        ],
        input_output_aliases={1: 0, 2: 1},
        compiler_params=pltpu.CompilerParams(vmem_limit_bytes=VMEM_LIMIT),
        name="add_share",
    )(info, out, sums, share)


def per_device(embeddings, pair_blocks, pair_count):
    length, width = embeddings.shape
    blocks = length // BLK
    axes = ("rows", "sub")
    devices = lax.axis_size(axes)
    parity = lax.axis_index("sub").astype(jnp.int32)
    odd = parity == 1
    base = lax.axis_index(axes).astype(jnp.int32) * blocks
    edges = [(i, i + 1) for i in range(1, devices - 1, 2)]
    back = [(j, i) for i, j in edges]

    slots = jnp.arange(pair_blocks.shape[1], dtype=jnp.int32)
    named = jnp.where(slots < pair_count[0], pair_blocks[0] - base, -1)
    places = jnp.arange(blocks, dtype=jnp.int32)
    counts = jnp.sum((named[None, :] == places[:, None]).astype(jnp.int32), axis=1)
    tail_theirs = counts[blocks - 1] - 1
    tail_mine = jnp.sum((places + counts > blocks).astype(jnp.int32))
    head_theirs = lax.ppermute(
        tail_mine[None], axes, [(i, i + 1) for i in range(devices - 1)]
    )[0]
    head_mine = jnp.where(head_theirs > 0, counts[0], 0)

    edge_block = lax.dynamic_slice_in_dim(embeddings, parity * (length - BLK), BLK, 0)
    link_block = lax.ppermute(edge_block, axes, edges + back)
    chip_x = lax.ppermute(embeddings, "sub", [(0, 1), (1, 0)])
    acc, sums = local_pairs(counts, embeddings)

    mine_link = jnp.where(odd, tail_mine, head_mine)
    theirs_link = jnp.where(odd, tail_theirs, head_theirs)
    info = jnp.stack(
        [
            parity,
            jnp.where(odd, head_mine, tail_mine),
            jnp.where(odd, head_theirs, tail_theirs),
            mine_link,
            theirs_link,
        ]
    )
    below = jnp.where(odd, mine_link, theirs_link)
    above = jnp.where(odd, theirs_link, mine_link)

    def nothing(info, acc, sums, x, chip_x, link_block):
        return tuple(near_pairs(info, acc, sums, x, chip_x, link_block))

    def share(pairs, info, acc, sums, x, chip_x, link_block):
        arrived = lax.ppermute(share_of(info, x, link_block), axes, pairs)
        out, sums = near_pairs(info, acc, sums, x, chip_x, link_block)
        return tuple(add_share(info, out, sums, arrived))

    def further(up, down, info, acc, sums, x, chip_x, link_block):
        up_blocks = lax.ppermute(x[length - (up + 1) * BLK : length - BLK], axes, edges)
        down_blocks = lax.ppermute(x[BLK : (down + 1) * BLK], axes, back)
        out, sums = near_pairs(info, acc, sums, x, chip_x, link_block)
        return tuple(far_pairs(info, out, sums, x, up_blocks, down_blocks))

    table = np.zeros((CLUSTER, CLUSTER), np.int32)
    branches = [nothing, functools.partial(share, back), functools.partial(share, edges)]
    table[1, 2:] = 1
    table[2:, 1] = 2
    for up in range(1, CLUSTER - 2):
        for down in range(1, CLUSTER - 1 - up):
            if up + down + 2 <= CLUSTER:
                table[up + 1, down + 1] = len(branches)
                branches.append(functools.partial(further, up, down))
    which = jnp.asarray(table.reshape(-1))[below * CLUSTER + above]
    out, sums = lax.switch(which, branches, info, acc, sums, embeddings, chip_x, link_block)
    return sums.reshape(length), out


def solution(mesh):
    in_specs = (
        P(("groups", "rows", "sub"), None),
        P(None, ("groups", "rows", "sub")),
        P(("groups", "rows", "sub")),
    )
    out_specs = (P(("groups", "rows", "sub")), P(("groups", "rows", "sub"), None))
    return jax.shard_map(
        per_device, mesh=mesh, in_specs=in_specs, out_specs=out_specs, check_vma=False
    )
```

```python
import functools

import jax
import jax.numpy as jnp
from jax import lax
from jax.experimental import pallas as pl
from jax.experimental.pallas import tpu as pltpu
from jax.sharding import PartitionSpec as P

BLK = 256
TEMPER = 4.0
EPS = 1e-06
LANES = 128
VMEM_LIMIT = 16 * 1024 * 1024

F32 = jnp.float32
BF16 = jnp.bfloat16

ODD, MINE_CHIP, THEIRS_CHIP, MINE_LINK, THEIRS_LINK = range(5)

VMEM = pl.BlockSpec(memory_space=pltpu.VMEM)
SMEM = pl.BlockSpec(memory_space=pltpu.SMEM)
ANY = pl.BlockSpec(memory_space=pl.ANY)


def inverse_norm(rows):
    wide = rows.astype(F32)
    return lax.rsqrt(jnp.sum(wide * wide, axis=1, keepdims=True) + EPS)


def diagonal():
    return lax.broadcasted_iota(jnp.int32, (BLK, BLK), 0) == lax.broadcasted_iota(
        jnp.int32, (BLK, BLK), 1
    )


def to_row(column):
    return jnp.sum(jnp.where(diagonal(), column, 0.0), axis=0, keepdims=True)


def to_column(row):
    return jnp.sum(jnp.where(diagonal(), row, 0.0), axis=1, keepdims=True)


def store_sums(ref, place, column):
    row = to_row(column)
    ref[place, 0:1, :] = row[:, :LANES]
    ref[place, 1:2, :] = row[:, LANES:]


def load_sums(ref, place):
    return to_column(jnp.concatenate([ref[place, 0:1, :], ref[place, 1:2, :]], axis=1))


def block_of(ref, place):
    return ref[pl.ds(pl.multiple_of(place * BLK, BLK), BLK), :]


def weigh(rows, row_inv, others, other_inv):
    inner = lax.dot_general(rows, others, (((1,), (1,)), ((), ())), preferred_element_type=F32)
    weight = jnp.exp(inner * (TEMPER * row_inv) * other_inv - TEMPER)
    term = jnp.dot(weight.astype(BF16), others, preferred_element_type=F32)
    return jnp.sum(weight, axis=1, keepdims=True), term


def pair_cost(pairs, width):
    return pl.CostEstimate(
        flops=pairs * 4 * BLK * BLK * width,
        bytes_accessed=pairs * 2 * BLK * width,
        transcendentals=pairs * BLK * BLK,
    )


def params():
    return pltpu.CompilerParams(vmem_limit_bytes=VMEM_LIMIT)


def link_place(info, k, blocks):
    return jnp.where(info[ODD] == 1, blocks - 1 - k, k)


def local_kernel(blocks, start, stop, counts, x_ref, *refs):
    acc_ref, sums_ref, inv_row = refs[-3:]

    def norms(r, carry):
        inv_row[r] = to_row(inverse_norm(block_of(x_ref, r)))
        return carry

    lax.fori_loop(0, blocks, norms, 0)

    def visit(step, carry):
        first = jnp.int32(0)
        for r in range(blocks):
            ends = jnp.int32(r) + counts[r]
            first = jnp.where((ends <= step) & (r < step), ends, first)
        last = jnp.minimum(step + counts[step], blocks)
        rows = block_of(x_ref, step)
        row_inv = to_column(inv_row[step])
        place = pl.ds(pl.multiple_of(step * BLK, BLK), BLK)
        sums, term = weigh(rows, row_inv, block_of(x_ref, first), inv_row[first])
        acc_ref[place, :] = term

        def add(k, sums):
            more, term = weigh(rows, row_inv, block_of(x_ref, k), inv_row[k])
            acc_ref[place, :] += term
            return sums + more

        store_sums(sums_ref, step, lax.fori_loop(first + 1, last, add, sums))
        return carry

    lax.fori_loop(start, stop, visit, 0)


def local_pairs(counts, x, start, stop, before=(), after=()):
    length, width = x.shape
    blocks = length // BLK
    n = 2 + len(after)
    return pl.pallas_call(
        functools.partial(local_kernel, blocks, start, stop),
        in_specs=[SMEM, VMEM] + [ANY] * len(after) + [VMEM] * len(before),
        out_specs=[VMEM, VMEM],
        out_shape=[
            jax.ShapeDtypeStruct((length, width), F32),
            jax.ShapeDtypeStruct((blocks, 2, LANES), F32),
        ],
        scratch_shapes=[pltpu.VMEM((blocks, 1, BLK), F32)],
        input_output_aliases={n + k: k for k in range(len(before))},
        compiler_params=params(),
        cost_estimate=pair_cost((stop - start) * blocks // 2, width),
        name="local_pairs",
    )(counts, x, *after, *before)


def payload_kernel(blocks, slot, info, x_ref, link_ref, out_ref, sums_ref, acc):
    mine, theirs = info[MINE_LINK], info[THEIRS_LINK]
    shares = (mine >= 5) & (theirs >= slot - 2)

    @pl.when(jnp.logical_not(shares))
    def _():
        out_ref[...] = block_of(x_ref, link_place(info, slot - 1, blocks))
        sums_ref[...] = jnp.zeros_like(sums_ref)

    @pl.when(shares)
    def _():
        link = link_ref[...]
        link_inv = inverse_norm(link)
        acc[...] = jnp.zeros_like(acc)

        def add(k, sums):
            others = block_of(x_ref, link_place(info, k, blocks))
            more, term = weigh(link, link_inv, others, to_row(inverse_norm(others)))
            acc[...] += term
            return sums + more

        store_sums(sums_ref, 0, lax.fori_loop(2, mine, add, jnp.zeros((BLK, 1), F32)))
        out_ref[...] = acc[...].astype(BF16)


def payload(slot, info, x, link_block):
    length, width = x.shape
    return pl.pallas_call(
        functools.partial(payload_kernel, length // BLK, slot),
        in_specs=[SMEM, VMEM, VMEM],
        out_specs=[VMEM, VMEM],
        out_shape=[
            jax.ShapeDtypeStruct((BLK, width), BF16),
            jax.ShapeDtypeStruct((1, 2, LANES), F32),
        ],
        scratch_shapes=[pltpu.VMEM((BLK, width), F32)],
        compiler_params=params(),
        cost_estimate=pair_cost(2, width),
        name="payload",
    )(info, x, link_block)


def finish(acc_ref, place, sums):
    acc_ref[place, :] = acc_ref[place, :] * (1.0 / sums)


def near_kernel(
    blocks, info, x_ref, chip_ref, one_ref, two_ref, acc_in, sums_in, acc_ref, sums_ref, out_ref, inv_row, sem
):
    odd = info[ODD] == 1
    mine_chip, theirs_chip = info[MINE_CHIP], info[THEIRS_CHIP]
    mine_link, theirs_link = info[MINE_LINK], info[THEIRS_LINK]
    chip_first = jnp.where(odd, blocks - theirs_chip, 0)

    def norms(k, carry):
        inv_row[k] = to_row(inverse_norm(block_of(chip_ref, chip_first + k)))
        return carry

    lax.fori_loop(0, theirs_chip, norms, 0)

    def copy_out(r):
        place = pl.ds(pl.multiple_of(r * BLK, BLK), BLK)
        return pltpu.make_async_copy(acc_ref.at[place, :], out_ref.at[place, :], sem.at[r])

    def is_chip(r):
        return jnp.where(odd, r, blocks - 1 - r) < mine_chip

    def is_link(r):
        return jnp.where(odd, blocks - 1 - r, r) < mine_link

    def is_done(r):
        return jnp.logical_not(is_link(r)) | (theirs_link <= 2)

    def visit(r, carry):
        place = pl.ds(pl.multiple_of(r * BLK, BLK), BLK)

        @pl.when(is_chip(r))
        def _():
            rows = block_of(x_ref, r)
            row_inv = inverse_norm(rows)

            def add(k, sums):
                more, term = weigh(rows, row_inv, block_of(chip_ref, chip_first + k), inv_row[k])
                acc_ref[place, :] += term
                return sums + more

            store_sums(sums_ref, r, lax.fori_loop(0, theirs_chip, add, load_sums(sums_ref, r)))

        for other_ref, least in ((one_ref, 1), (two_ref, 2)):

            @pl.when(is_link(r) & (theirs_link >= least))
            def _(other_ref=other_ref):
                rows = block_of(x_ref, r)
                others = other_ref[...]
                more, term = weigh(
                    rows, inverse_norm(rows), others, to_row(inverse_norm(others))
                )
                acc_ref[place, :] += term
                store_sums(sums_ref, r, load_sums(sums_ref, r) + more)

        @pl.when(is_done(r))
        def _():
            finish(acc_ref, place, load_sums(sums_ref, r))
            copy_out(r).start()

        return carry

    lax.fori_loop(0, blocks, visit, 0)

    def wait(r, carry):
        @pl.when(is_done(r))
        def _():
            copy_out(r).wait()

        return carry

    lax.fori_loop(0, blocks, wait, 0)


def near_pairs(info, x, chip_x, one, two, acc, sums):
    length, width = x.shape
    blocks = length // BLK
    return pl.pallas_call(
        functools.partial(near_kernel, blocks),
        in_specs=[SMEM] + [VMEM] * 6,
        out_specs=[VMEM, VMEM, ANY],
        out_shape=[
            jax.ShapeDtypeStruct((length, width), F32),
            jax.ShapeDtypeStruct((blocks, 2, LANES), F32),
            jax.ShapeDtypeStruct((length, width), F32),
        ],
        scratch_shapes=[pltpu.VMEM((blocks, 1, BLK), F32), pltpu.SemaphoreType.DMA((blocks,))],
        input_output_aliases={5: 0, 6: 1},
        compiler_params=params(),
        cost_estimate=pair_cost(12, width),
        name="near_pairs",
    )(info, x, chip_x, one, two, acc, sums)


def far_kernel(
    blocks, slot, info, x_ref, got_ref, got_sums, acc_in, sums_in, out_in, acc_ref, sums_ref, out_ref, sem
):
    mine, theirs = info[MINE_LINK], info[THEIRS_LINK]
    is_block = (theirs == slot) | (theirs == 4)
    shared = slot - 3
    is_share = (theirs >= 5) & (mine > shared)

    def place_of(k):
        return pl.ds(pl.multiple_of(link_place(info, k, blocks) * BLK, BLK), BLK)

    def copy_out(k):
        return pltpu.make_async_copy(
            acc_ref.at[place_of(k), :], out_ref.at[place_of(k), :], sem.at[k]
        )

    @pl.when(is_block)
    def _():
        others = got_ref[...]
        other_inv = to_row(inverse_norm(others))

        def visit(k, carry):
            r = link_place(info, k, blocks)
            place = place_of(k)
            rows = block_of(x_ref, r)
            more, term = weigh(rows, inverse_norm(rows), others, other_inv)
            sums = load_sums(sums_ref, r) + more
            store_sums(sums_ref, r, sums)
            last = theirs == slot
            acc_ref[place, :] = (acc_ref[place, :] + term) * jnp.where(last, 1.0 / sums, 1.0)

            @pl.when(last)
            def _():
                copy_out(k).start()

            return carry

        lax.fori_loop(0, mine, visit, 0)

        @pl.when(theirs == slot)
        def _():
            def wait(k, carry):
                copy_out(k).wait()
                return carry

            lax.fori_loop(0, mine, wait, 0)

    @pl.when(is_share)
    def _():
        r = link_place(info, shared, blocks)
        place = place_of(shared)
        sums = load_sums(sums_ref, r) + load_sums(got_sums, 0)
        store_sums(sums_ref, r, sums)
        acc_ref[place, :] = (acc_ref[place, :] + got_ref[...].astype(F32)) * (1.0 / sums)
        copy_out(shared).start()
        copy_out(shared).wait()


def far_pairs(slot, info, x, got, got_sums, acc, sums, out):
    length, width = x.shape
    blocks = length // BLK
    return pl.pallas_call(
        functools.partial(far_kernel, blocks, slot),
        in_specs=[SMEM] + [VMEM] * 5 + [ANY],
        out_specs=[VMEM, VMEM, ANY],
        out_shape=[
            jax.ShapeDtypeStruct((length, width), F32),
            jax.ShapeDtypeStruct((blocks, 2, LANES), F32),
            jax.ShapeDtypeStruct((length, width), F32),
        ],
        scratch_shapes=[pltpu.SemaphoreType.DMA((blocks,))],
        input_output_aliases={4: 0, 5: 1, 6: 2},
        compiler_params=params(),
        cost_estimate=pair_cost(4, width),
        name="far_pairs",
    )(info, x, got, got_sums, acc, sums, out)


def per_device(embeddings, pair_blocks, pair_count):
    length, width = embeddings.shape
    blocks = length // BLK
    axes = ("rows", "sub")
    devices = lax.axis_size(axes)
    parity = lax.axis_index("sub").astype(jnp.int32)
    odd = parity == 1
    base = lax.axis_index(axes).astype(jnp.int32) * blocks
    edges = [(i, i + 1) for i in range(1, devices - 1, 2)]
    edges += [(j, i) for i, j in edges]

    def over_link(array):
        return lax.ppermute(array, axes, edges)

    def edge_block(k):
        start = jnp.where(odd, length - (k + 1) * BLK, k * BLK)
        return lax.dynamic_slice_in_dim(embeddings, start, BLK, 0)

    one = over_link(edge_block(0))
    two = over_link(edge_block(1))
    chip_x = lax.ppermute(embeddings, "sub", [(0, 1), (1, 0)])

    slots = jnp.arange(pair_blocks.shape[1], dtype=jnp.int32)
    named = jnp.where(slots < pair_count[0], pair_blocks[0] - base, -1)
    places = jnp.arange(blocks, dtype=jnp.int32)
    counts = jnp.sum((named[None, :] == places[:, None]).astype(jnp.int32), axis=1)
    tail_theirs = counts[blocks - 1] - 1
    tail_mine = jnp.sum((places + counts > blocks).astype(jnp.int32))
    head_theirs = lax.ppermute(
        tail_mine[None], axes, [(i, i + 1) for i in range(devices - 1)]
    )[0]
    head_mine = jnp.where(head_theirs > 0, counts[0], 0)
    info = jnp.stack(
        [
            parity,
            jnp.where(odd, head_mine, tail_mine),
            jnp.where(odd, head_theirs, tail_theirs),
            jnp.where(odd, tail_mine, head_mine),
            jnp.where(odd, tail_theirs, head_theirs),
        ]
    )

    half = blocks // 2
    acc, sums = local_pairs(counts, embeddings, 0, half)
    third, third_sums = payload(3, info, embeddings, one)
    got_third = over_link(third)
    acc, sums = local_pairs(counts, embeddings, half, blocks, (acc, sums), (third_sums,))
    fourth, fourth_sums = payload(4, info, embeddings, two)
    got_fourth = over_link(fourth)
    got_sums = over_link(jnp.concatenate([third_sums, fourth_sums]))
    acc, sums, out = near_pairs(info, embeddings, chip_x, one, two, acc, sums)
    acc, sums, out = far_pairs(3, info, embeddings, got_third, got_sums[:1], acc, sums, out)
    acc, sums, out = far_pairs(4, info, embeddings, got_fourth, got_sums[1:], acc, sums, out)
    return sums.reshape(length), out


def solution(mesh):
    in_specs = (
        P(("groups", "rows", "sub"), None),
        P(None, ("groups", "rows", "sub")),
        P(("groups", "rows", "sub")),
    )
    out_specs = (P(("groups", "rows", "sub")), P(("groups", "rows", "sub"), None))
    return jax.shard_map(
        per_device, mesh=mesh, in_specs=in_specs, out_specs=out_specs, check_vma=False
    )
```

```python
import functools

import jax
import jax.numpy as jnp
from jax import lax
from jax.experimental import pallas as pl
from jax.experimental.pallas import tpu as pltpu
from jax.sharding import PartitionSpec as P

BLK = 256
EXTRA = 16
TEMPER = 4.0
EPS = 1e-06
LANES = 128
MIB = 1024 * 1024

F32 = jnp.float32
BF16 = jnp.bfloat16

ODD, MINE_CHIP, THEIRS_CHIP, MINE_LINK, THEIRS_LINK = range(5)

VMEM = pl.BlockSpec(memory_space=pltpu.VMEM)
SMEM = pl.BlockSpec(memory_space=pltpu.SMEM)
ANY = pl.BlockSpec(memory_space=pl.ANY)


def diagonal():
    return lax.broadcasted_iota(jnp.int32, (BLK, BLK), 0) == lax.broadcasted_iota(
        jnp.int32, (BLK, BLK), 1
    )


def to_row(column):
    return jnp.sum(jnp.where(diagonal(), column, 0.0), axis=0, keepdims=True)


def to_column(row):
    return jnp.sum(jnp.where(diagonal(), row, 0.0), axis=1, keepdims=True)


def inverse_norm(rows):
    wide = rows.astype(F32)
    return lax.rsqrt(jnp.sum(wide * wide, axis=1, keepdims=True) + EPS)


def inverse_row(rows):
    column = inverse_norm(rows)
    return jnp.concatenate(
        [to_row(column[k : k + BLK]) for k in range(0, rows.shape[0], BLK)], axis=1
    )


def store_row(ref, place, row):
    ref[place, 0:1, :] = row[:, :LANES]
    ref[place, 1:2, :] = row[:, LANES:]


def load_row(ref, place):
    return jnp.concatenate([ref[place, 0:1, :], ref[place, 1:2, :]], axis=1)


def span(place, n=1):
    return pl.ds(pl.multiple_of(place * BLK, BLK), n * BLK)


def product(rows, others):
    return lax.dot_general(rows, others, (((1,), (1,)), ((), ())), preferred_element_type=F32)


def weights(inner, row_inv, other_inv):
    return jnp.exp(inner * (TEMPER * row_inv) * other_inv - TEMPER)


def total(weight, others):
    return jnp.dot(weight.astype(BF16), others, preferred_element_type=F32)


def by_threes(count, body):
    threes = lax.div(count, 3)
    rest = count - 3 * threes

    def step(k, carry):
        body(3, 3 * k)
        return carry

    lax.fori_loop(0, threes, step, 0)
    for n in (1, 2):

        @pl.when(rest == n)
        def _(n=n):
            body(n, 3 * threes)


def pair_cost(pairs, width):
    return pl.CostEstimate(
        flops=pairs * 4 * BLK * BLK * width,
        bytes_accessed=pairs * 2 * BLK * width,
        transcendentals=pairs * BLK * BLK,
    )


def params(mib):
    return pltpu.CompilerParams(vmem_limit_bytes=mib * MIB)


def link_place(info, k, blocks):
    return jnp.where(info[ODD] == 1, blocks - 1 - k, k)


def link_low(info, first, n, blocks):
    return jnp.where(info[ODD] == 1, blocks - first - n, first)


def prep_kernel(blocks, meta, pairs, live, x_hbm, counts, x_ref, pay_ref, sem):
    copy = pltpu.make_async_copy(x_hbm, x_ref, sem)
    copy.start()
    for r in range(blocks + 2):
        counts[r] = 0

    def count(s, carry):
        r = pairs[0, s] - meta[1]
        counts[r] = counts[r] + 1
        return carry

    lax.fori_loop(0, live[0], count, 0)
    tail = jnp.int32(0)
    for r in range(blocks):
        tail += jnp.where(r + counts[r] > blocks, 1, 0)
    counts[blocks] = tail
    pay_ref[BLK:, :] = jnp.full((EXTRA, x_ref.shape[1]), tail.astype(F32)).astype(BF16)
    copy.wait()
    pay_ref[:BLK, :] = x_ref[span(jnp.where(meta[0] == 1, blocks - 1, 0)), :]


def prepare(meta, pair_blocks, pair_count, x):
    length, width = x.shape
    blocks = length // BLK
    return pl.pallas_call(
        functools.partial(prep_kernel, blocks),
        in_specs=[SMEM, SMEM, SMEM, ANY],
        out_specs=[SMEM, VMEM, VMEM],
        out_shape=[
            jax.ShapeDtypeStruct((blocks + 2,), jnp.int32),
            jax.ShapeDtypeStruct((length, width), BF16),
            jax.ShapeDtypeStruct((BLK + EXTRA, width), BF16),
        ],
        scratch_shapes=[pltpu.SemaphoreType.DMA],
        compiler_params=params(8),
        cost_estimate=pl.CostEstimate(
            flops=0, bytes_accessed=2 * length * width, transcendentals=0
        ),
        name="prepare",
    )(meta, pair_blocks, pair_count, x)


def local_kernel(blocks, meta, counts, x_ref, acc_ref, sums_ref, pay_ref):
    pay_ref[...] = x_ref[span(jnp.where(meta[0] == 1, blocks - 2, 1)), :]

    def visit(first, left):
        size = jnp.minimum(counts[first], blocks - first)
        for n in range(1, blocks + 1):

            @pl.when((left == 0) & (size == n))
            def _(n=n):
                rows = x_ref[span(first, n), :]
                inner = product(rows, rows)
                squares = [
                    jnp.where(
                        diagonal(), inner[k * BLK : (k + 1) * BLK, k * BLK : (k + 1) * BLK], 0.0
                    )
                    for k in range(n)
                ]
                row_inv = jnp.concatenate(
                    [lax.rsqrt(jnp.sum(s, axis=1, keepdims=True) + EPS) for s in squares], axis=0
                )
                other_inv = jnp.concatenate(
                    [lax.rsqrt(jnp.sum(s, axis=0, keepdims=True) + EPS) for s in squares], axis=1
                )
                weight = weights(inner, row_inv, other_inv)
                sums = jnp.sum(weight, axis=0, keepdims=True)
                acc_ref[span(first, n), :] = total(weight, rows)
                for k in range(n):
                    store_row(sums_ref, first + k, sums[:, k * BLK : (k + 1) * BLK])

        return jnp.where(left == 0, size, left) - 1

    lax.fori_loop(0, blocks, visit, jnp.int32(0))


def local_pairs(meta, counts, x):
    length, width = x.shape
    blocks = length // BLK
    return pl.pallas_call(
        functools.partial(local_kernel, blocks),
        in_specs=[SMEM, SMEM, VMEM],
        out_specs=[VMEM, VMEM, VMEM],
        out_shape=[
            jax.ShapeDtypeStruct((length, width), F32),
            jax.ShapeDtypeStruct((blocks, 2, LANES), F32),
            jax.ShapeDtypeStruct((BLK, width), BF16),
        ],
        compiler_params=params(24),
        cost_estimate=pair_cost(blocks * blocks, width),
        name="local_pairs",
    )(meta, counts, x)


def write_payload(blocks, slot, info, x_ref, link_ref, pay_ref, acc):
    mine, theirs = info[MINE_LINK], info[THEIRS_LINK]
    shares = (mine >= 5) & (theirs >= slot - 2)

    @pl.when(jnp.logical_not(shares))
    def _():
        pay_ref[:BLK, :] = x_ref[span(link_place(info, slot - 1, blocks)), :]
        pay_ref[BLK:, :] = jnp.zeros((EXTRA, x_ref.shape[1]), BF16)

    for n in range(3, blocks - 1):

        @pl.when(shares & (mine == n + 2))
        def _(n=n):
            link = link_ref[:BLK, :]
            others = x_ref[span(link_low(info, 2, n, blocks), n), :]
            weight = weights(product(link, others), inverse_norm(link), inverse_row(others))
            pay_ref[:BLK, :] = total(weight, others).astype(BF16)
            sums = to_row(jnp.sum(weight, axis=1, keepdims=True))
            high = sums.astype(BF16)
            rest = sums - high.astype(F32)
            middle = rest.astype(BF16)
            low = (rest - middle.astype(F32)).astype(BF16)
            place = lax.broadcasted_iota(jnp.int32, (EXTRA, BLK), 0)
            parts = jnp.where(
                place == 0,
                high.astype(F32),
                jnp.where(
                    place == 1, middle.astype(F32), jnp.where(place == 2, low.astype(F32), 0.0)
                ),
            )
            pay_ref[BLK:, :BLK] = parts.astype(BF16)
            pay_ref[BLK:, BLK:] = jnp.zeros((EXTRA, x_ref.shape[1] - BLK), BF16)


def third_kernel(blocks, meta, counts, chip_counts, x_ref, link_ref, pay_ref, info):
    odd = meta[0] == 1
    told = jnp.max(link_ref[BLK:, :LANES].astype(F32)).astype(jnp.int32)
    head_theirs = jnp.where(odd, chip_counts[blocks], told)
    head_mine = jnp.where(head_theirs > 0, counts[0], 0)
    tail_mine = counts[blocks]
    tail_theirs = counts[blocks - 1] - 1
    info[ODD] = meta[0]
    info[MINE_CHIP] = jnp.where(odd, head_mine, tail_mine)
    info[THEIRS_CHIP] = jnp.where(odd, head_theirs, tail_theirs)
    info[MINE_LINK] = jnp.where(odd, tail_mine, head_mine)
    info[THEIRS_LINK] = jnp.where(odd, tail_theirs, head_theirs)
    write_payload(blocks, 3, info, x_ref, link_ref, pay_ref, None)


def third_payload(meta, counts, chip_counts, x, link_block, after):
    length, width = x.shape
    blocks = length // BLK

    def kernel(meta, counts, chip_counts, x_ref, link_ref, after_ref, pay_ref, info):
        third_kernel(blocks, meta, counts, chip_counts, x_ref, link_ref, pay_ref, info)

    return pl.pallas_call(
        kernel,
        in_specs=[SMEM, SMEM, SMEM, VMEM, VMEM, ANY],
        out_specs=[VMEM, SMEM],
        out_shape=[
            jax.ShapeDtypeStruct((BLK + EXTRA, width), BF16),
            jax.ShapeDtypeStruct((8,), jnp.int32),
        ],
        compiler_params=params(8),
        cost_estimate=pair_cost(2, width),
        name="third_payload",
    )(meta, counts, chip_counts, x, link_block, after)


def fourth_payload(info, x, link_block, after):
    length, width = x.shape
    blocks = length // BLK

    def kernel(info, x_ref, link_ref, after_ref, pay_ref):
        write_payload(blocks, 4, info, x_ref, link_ref, pay_ref, None)

    return pl.pallas_call(
        kernel,
        in_specs=[SMEM, VMEM, VMEM, ANY],
        out_specs=VMEM,
        out_shape=jax.ShapeDtypeStruct((BLK + EXTRA, width), BF16),
        compiler_params=params(8),
        cost_estimate=pair_cost(2, width),
        name="fourth_payload",
    )(info, x, link_block, after)


def copy_out(acc_ref, out_ref, sem, r):
    return pltpu.make_async_copy(acc_ref.at[span(r), :], out_ref.at[span(r), :], sem.at[r])


def finish(acc_ref, sums_ref, out_ref, sem, r):
    acc_ref[span(r), :] = acc_ref[span(r), :] * (1.0 / to_column(load_row(sums_ref, r)))
    copy_out(acc_ref, out_ref, sem, r).start()


def each(blocks, chosen, body):
    def step(r, carry):
        @pl.when(chosen(r))
        def _():
            body(r)

        return carry

    lax.fori_loop(0, blocks, step, 0)


def chip_kernel(blocks, info, x_ref, chip_ref, acc_in, sums_in, acc_ref, sums_ref, out_ref, sem):
    odd = info[ODD] == 1
    mine, theirs = info[MINE_CHIP], info[THEIRS_CHIP]
    mine_link = info[MINE_LINK]
    low = jnp.where(odd, 0, blocks - mine)
    low_theirs = jnp.where(odd, blocks - theirs, 0)

    def is_done(r):
        return jnp.where(odd, blocks - 1 - r, r) >= mine_link

    def add(r, n, first):
        rows = x_ref[span(r), :]
        others = chip_ref[span(low_theirs + first, n), :]
        weight = weights(product(rows, others), inverse_norm(rows), inverse_row(others))
        acc_ref[span(r), :] += total(weight, others)
        more = to_row(jnp.sum(weight, axis=1, keepdims=True))
        store_row(sums_ref, r, load_row(sums_ref, r) + more)

    def visit(r):
        @pl.when((r >= low) & (r < low + mine))
        def _():
            by_threes(theirs, functools.partial(add, r))

        finish(acc_ref, sums_ref, out_ref, sem, r)

    each(blocks, is_done, visit)
    each(blocks, is_done, lambda r: copy_out(acc_ref, out_ref, sem, r).wait())


def link_kernel(
    blocks, slots, info, x_ref, *refs
):
    got_refs = refs[: len(slots)]
    acc_in, sums_in, out_in, acc_ref, sums_ref, out_ref, sem = refs[len(slots) :]
    mine, theirs = info[MINE_LINK], info[THEIRS_LINK]

    for slot, got_ref in zip(slots, got_refs):
        uses = theirs >= slot
        if slot > 2:
            uses = uses & (theirs <= 4)

        @pl.when(uses)
        def _(got_ref=got_ref):
            others = got_ref[:BLK, :]
            other_inv = inverse_row(others)

            def add(n, first):
                low = link_low(info, first, n, blocks)
                rows = x_ref[span(low, n), :]
                weight = weights(product(rows, others), inverse_norm(rows), other_inv)
                acc_ref[span(low, n), :] += total(weight, others)
                sums = jnp.sum(weight, axis=1, keepdims=True)
                for k in range(n):
                    more = to_row(sums[k * BLK : (k + 1) * BLK])
                    store_row(sums_ref, low + k, load_row(sums_ref, low + k) + more)

            by_threes(mine, add)

        if slot > 2:

            @pl.when((theirs >= 5) & (mine >= slot - 2))
            def _(slot=slot, got_ref=got_ref):
                r = link_place(info, slot - 3, blocks)
                acc_ref[span(r), :] += got_ref[:BLK, :].astype(F32)
                more = jnp.sum(got_ref[BLK:, :BLK].astype(F32), axis=0, keepdims=True)
                store_row(sums_ref, r, load_row(sums_ref, r) + more)

    def is_done(r):
        k = jnp.where(info[ODD] == 1, blocks - 1 - r, r)
        last = jnp.where(theirs >= 5, k + 3, jnp.maximum(theirs, 2))
        now = last == slots[0]
        for slot in slots[1:]:
            now = now | (last == slot)
        return (k < mine) & now

    each(blocks, is_done, functools.partial(finish, acc_ref, sums_ref, out_ref, sem))
    each(blocks, is_done, lambda r: copy_out(acc_ref, out_ref, sem, r).wait())


def totals_shapes(x):
    length, width = x.shape
    return [
        jax.ShapeDtypeStruct((length, width), F32),
        jax.ShapeDtypeStruct((length // BLK, 2, LANES), F32),
        jax.ShapeDtypeStruct((length, width), F32),
    ]


def chip_pairs(info, x, chip_x, acc, sums):
    length, width = x.shape
    blocks = length // BLK
    return pl.pallas_call(
        functools.partial(chip_kernel, blocks),
        in_specs=[SMEM] + [VMEM] * 4,
        out_specs=[VMEM, VMEM, ANY],
        out_shape=totals_shapes(x),
        scratch_shapes=[pltpu.SemaphoreType.DMA((blocks,))],
        input_output_aliases={3: 0, 4: 1},
        compiler_params=params(8),
        cost_estimate=pair_cost(12, width),
        name="chip_pairs",
    )(info, x, chip_x, acc, sums)


def link_pairs(slots, info, x, got, acc, sums, out):
    length, width = x.shape
    blocks = length // BLK
    n = len(slots)
    return pl.pallas_call(
        functools.partial(link_kernel, blocks, slots),
        in_specs=[SMEM] + [VMEM] * (3 + n) + [ANY],
        out_specs=[VMEM, VMEM, ANY],
        out_shape=totals_shapes(x),
        scratch_shapes=[pltpu.SemaphoreType.DMA((blocks,))],
        input_output_aliases={2 + n: 0, 3 + n: 1, 4 + n: 2},
        compiler_params=params(8),
        cost_estimate=pair_cost(6 * n, width),
        name="link_pairs",
    )(info, x, *got, acc, sums, out)


def per_device(embeddings, pair_blocks, pair_count):
    length, width = embeddings.shape
    blocks = length // BLK
    axes = ("rows", "sub")
    devices = lax.axis_size(axes)
    parity = lax.axis_index("sub").astype(jnp.int32)
    base = lax.axis_index(axes).astype(jnp.int32) * blocks
    edges = [(i, i + 1) for i in range(1, devices - 1, 2)]
    edges += [(j, i) for i, j in edges]

    def over_link(array):
        return lax.ppermute(array, axes, edges)

    def over_chip(array):
        return lax.ppermute(array, "sub", [(0, 1), (1, 0)])

    chip_x = over_chip(embeddings)
    meta = jnp.stack([parity, base])
    counts, x, first = prepare(meta, pair_blocks, pair_count, embeddings)
    one = over_link(first)
    chip_counts = over_chip(counts)
    acc, sums, second = local_pairs(meta, counts, x)
    two = over_link(second)
    third, info = third_payload(meta, counts, chip_counts, x, one, second)
    three = over_link(third)
    acc, sums, out = chip_pairs(info, x, chip_x, acc, sums)
    fourth = fourth_payload(info, x, two, sums)
    four = over_link(fourth)
    acc, sums, out = link_pairs((1, 2), info, x, (one, two), acc, sums, out)
    acc, sums, out = link_pairs((3,), info, x, (three,), acc, sums, out)
    acc, sums, out = link_pairs((4,), info, x, (four,), acc, sums, out)
    return sums.reshape(length), out


def solution(mesh):
    in_specs = (
        P(("groups", "rows", "sub"), None),
        P(None, ("groups", "rows", "sub")),
        P(("groups", "rows", "sub")),
    )
    out_specs = (P(("groups", "rows", "sub")), P(("groups", "rows", "sub"), None))
    return jax.shard_map(
        per_device, mesh=mesh, in_specs=in_specs, out_specs=out_specs, check_vma=False
    )
```

```python
import functools

import jax
import jax.numpy as jnp
from jax import lax
from jax.experimental import pallas as pl
from jax.experimental.pallas import tpu as pltpu
from jax.sharding import PartitionSpec as P

BLK = 256
EXTRA = 16
TEMPER = 4.0
EPS = 1e-06
LANES = 128
MIB = 1024 * 1024

F32 = jnp.float32
BF16 = jnp.bfloat16

ODD, MINE_CHIP, THEIRS_CHIP, MINE_LINK, THEIRS_LINK = range(5)

VMEM = pl.BlockSpec(memory_space=pltpu.VMEM)
SMEM = pl.BlockSpec(memory_space=pltpu.SMEM)
ANY = pl.BlockSpec(memory_space=pl.ANY)
HBM = pl.BlockSpec(memory_space=pltpu.HBM)


def diagonal():
    return lax.broadcasted_iota(jnp.int32, (BLK, BLK), 0) == lax.broadcasted_iota(
        jnp.int32, (BLK, BLK), 1
    )


def to_row(column):
    return jnp.sum(jnp.where(diagonal(), column, 0.0), axis=0, keepdims=True)


def to_column(row):
    return jnp.sum(jnp.where(diagonal(), row, 0.0), axis=1, keepdims=True)


def inverse_norm(rows):
    wide = rows.astype(F32)
    return lax.rsqrt(jnp.sum(wide * wide, axis=1, keepdims=True) + EPS)


def store_row(ref, place, row):
    ref[place, 0:1, :] = row[:, :LANES]
    ref[place, 1:2, :] = row[:, LANES:]


def load_row(ref, place):
    return jnp.concatenate([ref[place, 0:1, :], ref[place, 1:2, :]], axis=1)


def span(place, n=1):
    return pl.ds(pl.multiple_of(place * BLK, BLK), n * BLK)


def product(rows, others):
    return lax.dot_general(rows, others, (((1,), (1,)), ((), ())), preferred_element_type=F32)


def weights(inner, row_inv, other_inv):
    return jnp.exp(inner * (TEMPER * row_inv) * other_inv - TEMPER)


def total(weight, others):
    return jnp.dot(weight.astype(BF16), others, preferred_element_type=F32)


def scaled(weight, flags):
    return jnp.concatenate(
        [
            jnp.concatenate(
                [
                    weight[a * BLK : (a + 1) * BLK, b * BLK : (b + 1) * BLK] * flag
                    for b, flag in enumerate(row)
                ],
                axis=1,
            )
            for a, row in enumerate(flags)
        ],
        axis=0,
    )


def flag(condition):
    return jnp.where(condition, 1.0, 0.0).astype(F32)


def pair_cost(pairs, width):
    return pl.CostEstimate(
        flops=pairs * 4 * BLK * BLK * width,
        bytes_accessed=pairs * 2 * BLK * width,
        transcendentals=pairs * BLK * BLK,
    )


def params(mib):
    return pltpu.CompilerParams(vmem_limit_bytes=mib * MIB)


def link_place(info, k, blocks):
    return jnp.where(info[ODD] == 1, blocks - 1 - k, k)


def prep_kernel(blocks, axes, pairs_hbm, live_hbm, x_hbm, counts, x_ref, pay_ref, pairs, live, sem):
    odd = lax.axis_index("sub") == 1
    base = lax.axis_index(axes) * blocks
    edge = jnp.where(odd, blocks - 1, 0)
    copies = [
        pltpu.make_async_copy(pairs_hbm, pairs, sem.at[0]),
        pltpu.make_async_copy(live_hbm, live, sem.at[1]),
        pltpu.make_async_copy(x_hbm.at[span(edge), :], pay_ref.at[:BLK, :], sem.at[2]),
        pltpu.make_async_copy(x_hbm, x_ref, sem.at[3]),
    ]
    for copy in copies:
        copy.start()
    for r in range(blocks):
        counts[r] = 0
    copies[0].wait()
    copies[1].wait()

    def count(s, carry):
        r = pairs[0, s] - base
        counts[r] = counts[r] + 1
        return carry

    lax.fori_loop(0, live[0], count, 0)
    tail = jnp.int32(0)
    start = jnp.int32(0)
    for r in range(blocks):
        tail += jnp.where(r + counts[r] > blocks, 1, 0)
        if r:
            start = jnp.where(r - 1 + counts[r - 1] == r, r, start)
        counts[blocks + 1 + r] = start
    counts[blocks] = tail
    pay_ref[BLK:, :] = jnp.full((EXTRA, x_ref.shape[1]), tail.astype(F32)).astype(BF16)
    copies[2].wait()
    copies[3].wait()


def prepare(axes, pair_blocks, pair_count, x):
    length, width = x.shape
    blocks = length // BLK
    return pl.pallas_call(
        functools.partial(prep_kernel, blocks, axes),
        in_specs=[HBM] * 3,
        out_specs=[SMEM, VMEM, VMEM],
        out_shape=[
            jax.ShapeDtypeStruct((2 * blocks + 1,), jnp.int32),
            jax.ShapeDtypeStruct((length, width), BF16),
            jax.ShapeDtypeStruct((BLK + EXTRA, width), BF16),
        ],
        scratch_shapes=[
            pltpu.SMEM(pair_blocks.shape, jnp.int32),
            pltpu.SMEM(pair_count.shape, jnp.int32),
            pltpu.SemaphoreType.DMA((4,)),
        ],
        compiler_params=params(56),
        cost_estimate=pl.CostEstimate(
            flops=0, bytes_accessed=2 * length * width, transcendentals=0
        ),
        name="prepare",
    )(pair_blocks, pair_count, x)


def local_kernel(blocks, counts, x_ref, acc_ref, sums_ref, inv_ref, pay_ref, inv_row):
    odd = lax.axis_index("sub") == 1
    pay_ref[...] = x_ref[span(jnp.where(odd, blocks - 2, 1)), :]
    half = blocks // 2

    def norms(r, carry):
        inv = inverse_norm(x_ref[span(r), :])
        inv_ref[span(r), :] = inv
        inv_row[r] = to_row(inv)
        return carry

    lax.fori_loop(0, blocks, norms, 0)

    def visit(k, carry):
        turn = lax.rem(k, half)
        row = lax.div(k, half) * 2
        col = lax.rem(lax.div(k, half) + turn, half) * 2
        same = [
            [counts[blocks + 1 + row + a] == counts[blocks + 1 + col + b] for b in range(2)]
            for a in range(2)
        ]

        @pl.when(same[0][0] | same[0][1] | same[1][0] | same[1][1])
        def _():
            rows = x_ref[span(row, 2), :]
            others = x_ref[span(col, 2), :]
            other_inv = jnp.concatenate([inv_row[col], inv_row[col + 1]], axis=1)
            weight = weights(product(rows, others), inv_ref[span(row, 2), :], other_inv)
            weight = scaled(weight, [[flag(s) for s in line] for line in same])
            term = total(weight, others)
            acc_ref[span(row, 2), :] = jnp.where(turn == 0, term, acc_ref[span(row, 2), :] + term)
            sums = jnp.sum(weight, axis=1, keepdims=True)
            for a in range(2):
                more = to_row(sums[a * BLK : (a + 1) * BLK])
                before = load_row(sums_ref, row + a)
                store_row(sums_ref, row + a, jnp.where(turn == 0, more, before + more))

        return carry

    lax.fori_loop(0, half * half, visit, 0)


def local_pairs(counts, x):
    length, width = x.shape
    blocks = length // BLK
    return pl.pallas_call(
        functools.partial(local_kernel, blocks),
        in_specs=[SMEM, VMEM],
        out_specs=[VMEM] * 4,
        out_shape=[
            jax.ShapeDtypeStruct((length, width), F32),
            jax.ShapeDtypeStruct((blocks, 2, LANES), F32),
            jax.ShapeDtypeStruct((length, 1), F32),
            jax.ShapeDtypeStruct((BLK, width), BF16),
        ],
        scratch_shapes=[pltpu.VMEM((blocks, 1, BLK), F32)],
        compiler_params=params(12),
        cost_estimate=pair_cost(blocks * blocks, width),
        name="local_pairs",
    )(counts, x)


def write_payload(blocks, slot, info, x_ref, link_ref, pay_ref, acc):
    mine, theirs = info[MINE_LINK], info[THEIRS_LINK]
    shares = (mine >= 5) & (theirs >= slot - 2)

    @pl.when(jnp.logical_not(shares))
    def _():
        pay_ref[:BLK, :] = x_ref[span(link_place(info, slot - 1, blocks)), :]
        pay_ref[BLK:, :] = jnp.zeros((EXTRA, x_ref.shape[1]), BF16)

    @pl.when(shares)
    def _():
        link = link_ref[:BLK, :]
        link_inv = inverse_norm(link)
        acc[...] = jnp.zeros_like(acc)

        def add(k, sums):
            others = x_ref[span(link_place(info, k, blocks)), :]
            weight = weights(product(link, others), link_inv, to_row(inverse_norm(others)))
            acc[...] += total(weight, others)
            return sums + to_row(jnp.sum(weight, axis=1, keepdims=True))

        sums = lax.fori_loop(2, mine, add, jnp.zeros((1, BLK), F32))
        pay_ref[:BLK, :] = acc[...].astype(BF16)
        high = sums.astype(BF16)
        rest = sums - high.astype(F32)
        middle = rest.astype(BF16)
        low = (rest - middle.astype(F32)).astype(BF16)
        place = lax.broadcasted_iota(jnp.int32, (EXTRA, BLK), 0)
        parts = jnp.where(
            place == 0,
            high.astype(F32),
            jnp.where(place == 1, middle.astype(F32), jnp.where(place == 2, low.astype(F32), 0.0)),
        )
        pay_ref[BLK:, :BLK] = parts.astype(BF16)
        pay_ref[BLK:, BLK:] = jnp.zeros((EXTRA, x_ref.shape[1] - BLK), BF16)


def third_kernel(blocks, counts, chip_counts, x_ref, link_ref, pay_ref, info, acc):
    odd = lax.axis_index("sub") == 1
    told = jnp.max(link_ref[BLK:, :LANES].astype(F32)).astype(jnp.int32)
    head_theirs = jnp.where(odd, chip_counts[blocks], told)
    head_mine = jnp.where(head_theirs > 0, counts[0], 0)
    tail_mine = counts[blocks]
    tail_theirs = counts[blocks - 1] - 1
    info[ODD] = jnp.where(odd, 1, 0)
    info[MINE_CHIP] = jnp.where(odd, head_mine, tail_mine)
    info[THEIRS_CHIP] = jnp.where(odd, head_theirs, tail_theirs)
    info[MINE_LINK] = jnp.where(odd, tail_mine, head_mine)
    info[THEIRS_LINK] = jnp.where(odd, tail_theirs, head_theirs)
    write_payload(blocks, 3, info, x_ref, link_ref, pay_ref, acc)


def third_payload(counts, chip_counts, x, link_block, after):
    length, width = x.shape
    blocks = length // BLK

    def kernel(counts, chip_counts, x_ref, link_ref, after_ref, pay_ref, info, acc):
        third_kernel(blocks, counts, chip_counts, x_ref, link_ref, pay_ref, info, acc)

    return pl.pallas_call(
        kernel,
        in_specs=[SMEM, SMEM, VMEM, VMEM, ANY],
        out_specs=[VMEM, SMEM],
        out_shape=[
            jax.ShapeDtypeStruct((BLK + EXTRA, width), BF16),
            jax.ShapeDtypeStruct((8,), jnp.int32),
        ],
        scratch_shapes=[pltpu.VMEM((BLK, width), F32)],
        compiler_params=params(8),
        cost_estimate=pair_cost(2, width),
        name="third_payload",
    )(counts, chip_counts, x, link_block, after)


def fourth_payload(info, x, link_block, after):
    length, width = x.shape
    blocks = length // BLK

    def kernel(info, x_ref, link_ref, after_ref, pay_ref, acc):
        write_payload(blocks, 4, info, x_ref, link_ref, pay_ref, acc)

    return pl.pallas_call(
        kernel,
        in_specs=[SMEM, VMEM, VMEM, ANY],
        out_specs=VMEM,
        out_shape=jax.ShapeDtypeStruct((BLK + EXTRA, width), BF16),
        scratch_shapes=[pltpu.VMEM((BLK, width), F32)],
        compiler_params=params(8),
        cost_estimate=pair_cost(2, width),
        name="fourth_payload",
    )(info, x, link_block, after)


def copy_out(acc_ref, out_ref, sem, r):
    return pltpu.make_async_copy(acc_ref.at[span(r), :], out_ref.at[span(r), :], sem.at[r])


def finish(acc_ref, sums_ref, out_ref, sem, r):
    acc_ref[span(r), :] = acc_ref[span(r), :] * (1.0 / to_column(load_row(sums_ref, r)))
    copy_out(acc_ref, out_ref, sem, r).start()


def each(blocks, chosen, body):
    def step(r, carry):
        @pl.when(chosen(r))
        def _():
            body(r)

        return carry

    lax.fori_loop(0, blocks, step, 0)


def add_tile(acc_ref, sums_ref, row, weight, others):
    acc_ref[span(row, 2), :] += total(weight, others)
    sums = jnp.sum(weight, axis=1, keepdims=True)
    for a in range(2):
        more = to_row(sums[a * BLK : (a + 1) * BLK])
        store_row(sums_ref, row + a, load_row(sums_ref, row + a) + more)


def chip_kernel(
    blocks, info, x_ref, inv_ref, chip_ref, acc_in, sums_in, acc_ref, sums_ref, out_ref, inv_row, sem
):
    odd = info[ODD] == 1
    mine, theirs = info[MINE_CHIP], info[THEIRS_CHIP]
    mine_link = info[MINE_LINK]

    def is_done(r):
        return jnp.where(odd, blocks - 1 - r, r) >= mine_link

    def column(n):
        col = jnp.where(odd, blocks - 2 - 2 * n, 2 * n)
        for b in range(2):
            inv_row[b] = to_row(inverse_norm(chip_ref[span(col + b), :]))
        theirs_ok = [jnp.where(odd, blocks - 1 - col - b, col + b) < theirs for b in range(2)]

        def tile(m, carry):
            row = jnp.where(odd, 2 * m, blocks - 2 - 2 * m)
            mine_ok = [jnp.where(odd, row + a, blocks - 1 - row - a) < mine for a in range(2)]
            others = chip_ref[span(col, 2), :]
            other_inv = jnp.concatenate([inv_row[0], inv_row[1]], axis=1)
            weight = weights(
                product(x_ref[span(row, 2), :], others), inv_ref[span(row, 2), :], other_inv
            )
            weight = scaled(weight, [[flag(p & q) for q in theirs_ok] for p in mine_ok])
            add_tile(acc_ref, sums_ref, row, weight, others)
            return carry

        lax.fori_loop(0, lax.div(mine + 1, 2), tile, 0)

    def columns(n, carry):
        column(n)
        return carry

    lax.fori_loop(0, lax.div(theirs + 1, 2), columns, 0)
    each(blocks, is_done, functools.partial(finish, acc_ref, sums_ref, out_ref, sem))
    each(blocks, is_done, lambda r: copy_out(acc_ref, out_ref, sem, r).wait())


def link_kernel(blocks, slots, info, x_ref, inv_ref, *refs):
    got_refs = refs[: len(slots)]
    acc_in, sums_in, out_in, acc_ref, sums_ref, out_ref, sem = refs[len(slots) :]
    mine, theirs = info[MINE_LINK], info[THEIRS_LINK]
    odd = info[ODD] == 1

    for slot, got_ref in zip(slots, got_refs):
        uses = theirs >= slot
        if slot > 2:
            uses = uses & (theirs <= 4)

        @pl.when(uses)
        def _(got_ref=got_ref):
            other_inv = to_row(inverse_norm(got_ref[:BLK, :]))

            def tile(m, carry):
                row = jnp.where(odd, blocks - 2 - 2 * m, 2 * m)
                mine_ok = [jnp.where(odd, blocks - 1 - row - a, row + a) < mine for a in range(2)]
                others = got_ref[:BLK, :]
                weight = weights(
                    product(x_ref[span(row, 2), :], others), inv_ref[span(row, 2), :], other_inv
                )
                weight = scaled(weight, [[flag(p)] for p in mine_ok])
                add_tile(acc_ref, sums_ref, row, weight, others)
                return carry

            lax.fori_loop(0, lax.div(mine + 1, 2), tile, 0)

        if slot > 2:

            @pl.when((theirs >= 5) & (mine >= slot - 2))
            def _(slot=slot, got_ref=got_ref):
                r = link_place(info, slot - 3, blocks)
                acc_ref[span(r), :] += got_ref[:BLK, :].astype(F32)
                more = jnp.sum(got_ref[BLK:, :BLK].astype(F32), axis=0, keepdims=True)
                store_row(sums_ref, r, load_row(sums_ref, r) + more)

    def is_done(r):
        k = jnp.where(odd, blocks - 1 - r, r)
        last = jnp.where(theirs >= 5, k + 3, jnp.maximum(theirs, 2))
        now = last == slots[0]
        for slot in slots[1:]:
            now = now | (last == slot)
        return (k < mine) & now

    each(blocks, is_done, functools.partial(finish, acc_ref, sums_ref, out_ref, sem))
    each(blocks, is_done, lambda r: copy_out(acc_ref, out_ref, sem, r).wait())


def totals_shapes(x):
    length, width = x.shape
    return [
        jax.ShapeDtypeStruct((length, width), F32),
        jax.ShapeDtypeStruct((length // BLK, 2, LANES), F32),
        jax.ShapeDtypeStruct((length, width), F32),
    ]


def chip_pairs(info, x, inv, chip_x, acc, sums):
    length, width = x.shape
    blocks = length // BLK
    return pl.pallas_call(
        functools.partial(chip_kernel, blocks),
        in_specs=[SMEM] + [VMEM] * 5,
        out_specs=[VMEM, VMEM, ANY],
        out_shape=totals_shapes(x),
        scratch_shapes=[pltpu.VMEM((2, 1, BLK), F32), pltpu.SemaphoreType.DMA((blocks,))],
        input_output_aliases={4: 0, 5: 1},
        compiler_params=params(8),
        cost_estimate=pair_cost(12, width),
        name="chip_pairs",
    )(info, x, inv, chip_x, acc, sums)


def link_pairs(slots, info, x, inv, got, acc, sums, out):
    length, width = x.shape
    blocks = length // BLK
    n = len(slots)
    return pl.pallas_call(
        functools.partial(link_kernel, blocks, slots),
        in_specs=[SMEM] + [VMEM] * (4 + n) + [ANY],
        out_specs=[VMEM, VMEM, ANY],
        out_shape=totals_shapes(x),
        scratch_shapes=[pltpu.SemaphoreType.DMA((blocks,))],
        input_output_aliases={3 + n: 0, 4 + n: 1, 5 + n: 2},
        compiler_params=params(8),
        cost_estimate=pair_cost(6 * n, width),
        name="link_pairs",
    )(info, x, inv, *got, acc, sums, out)


def per_device(embeddings, pair_blocks, pair_count):
    length, width = embeddings.shape
    blocks = length // BLK
    axes = ("rows", "sub")
    devices = lax.axis_size(axes)
    edges = [(i, i + 1) for i in range(1, devices - 1, 2)]
    edges += [(j, i) for i, j in edges]

    def over_link(array):
        return lax.ppermute(array, axes, edges)

    def over_chip(array):
        return lax.ppermute(array, "sub", [(0, 1), (1, 0)])

    counts, x, first = prepare(axes, pair_blocks, pair_count, embeddings)
    one = over_link(first)
    chip_x = over_chip(embeddings)
    chip_counts = over_chip(counts)
    acc, sums, inv, second = local_pairs(counts, x)
    two = over_link(second)
    third, info = third_payload(counts, chip_counts, x, one, second)
    three = over_link(third)
    acc, sums, out = chip_pairs(info, x, inv, chip_x, acc, sums)
    fourth = fourth_payload(info, x, two, sums)
    four = over_link(fourth)
    acc, sums, out = link_pairs((1, 2), info, x, inv, (one, two), acc, sums, out)
    acc, sums, out = link_pairs((3,), info, x, inv, (three,), acc, sums, out)
    acc, sums, out = link_pairs((4,), info, x, inv, (four,), acc, sums, out)
    return sums.reshape(length), out


def solution(mesh):
    in_specs = (
        P(("groups", "rows", "sub"), None),
        P(None, ("groups", "rows", "sub")),
        P(("groups", "rows", "sub")),
    )
    out_specs = (P(("groups", "rows", "sub")), P(("groups", "rows", "sub"), None))
    return jax.shard_map(
        per_device, mesh=mesh, in_specs=in_specs, out_specs=out_specs, check_vma=False
    )
```

```python
import functools

import jax
import jax.numpy as jnp
from jax import lax
from jax.experimental import pallas as pl
from jax.experimental.pallas import tpu as pltpu
from jax.sharding import PartitionSpec as P

BLK = 256
EXTRA = 16
TEMPER = 4.0
EPS = 1e-06
LANES = 128
MIB = 1024 * 1024

F32 = jnp.float32
BF16 = jnp.bfloat16

ODD, MINE_CHIP, THEIRS_CHIP, MINE_LINK, THEIRS_LINK = range(5)

VMEM = pl.BlockSpec(memory_space=pltpu.VMEM)
SMEM = pl.BlockSpec(memory_space=pltpu.SMEM)
ANY = pl.BlockSpec(memory_space=pl.ANY)
HBM = pl.BlockSpec(memory_space=pltpu.HBM)


def diagonal():
    return lax.broadcasted_iota(jnp.int32, (BLK, BLK), 0) == lax.broadcasted_iota(
        jnp.int32, (BLK, BLK), 1
    )


def to_row(column):
    return jnp.sum(jnp.where(diagonal(), column, 0.0), axis=0, keepdims=True)


def to_column(row):
    return jnp.sum(jnp.where(diagonal(), row, 0.0), axis=1, keepdims=True)


def inverse_norm(rows):
    wide = rows.astype(F32)
    return lax.rsqrt(jnp.sum(wide * wide, axis=1, keepdims=True) + EPS)


def store_row(ref, place, row):
    ref[pl.ds(2 * place, 1), :] = row[:, :LANES]
    ref[pl.ds(2 * place + 1, 1), :] = row[:, LANES:]


def load_row(ref, place):
    return jnp.concatenate([ref[pl.ds(2 * place, 1), :], ref[pl.ds(2 * place + 1, 1), :]], axis=1)


def span(place, n=1):
    return pl.ds(pl.multiple_of(place * BLK, BLK), n * BLK)


def product(rows, others):
    return lax.dot_general(rows, others, (((1,), (1,)), ((), ())), preferred_element_type=F32)


def weights(inner, row_inv, other_inv):
    return jnp.exp(inner * (TEMPER * row_inv) * other_inv - TEMPER)


def total(weight, others):
    return jnp.dot(weight.astype(BF16), others, preferred_element_type=F32)


def scaled(weight, flags):
    return jnp.concatenate(
        [
            jnp.concatenate(
                [
                    weight[a * BLK : (a + 1) * BLK, b * BLK : (b + 1) * BLK] * flag
                    for b, flag in enumerate(row)
                ],
                axis=1,
            )
            for a, row in enumerate(flags)
        ],
        axis=0,
    )


def flag(condition):
    return jnp.where(condition, 1.0, 0.0).astype(F32)


def pair_cost(pairs, width):
    return pl.CostEstimate(
        flops=pairs * 4 * BLK * BLK * width,
        bytes_accessed=pairs * 2 * BLK * width,
        transcendentals=pairs * BLK * BLK,
    )


def params(mib):
    return pltpu.CompilerParams(vmem_limit_bytes=mib * MIB)


def link_place(info, k, blocks):
    return jnp.where(info[ODD] == 1, blocks - 1 - k, k)


def prep_kernel(blocks, axes, pairs_hbm, live_hbm, x_hbm, counts, pay_ref, pairs, live, sem):
    odd = lax.axis_index("sub") == 1
    base = lax.axis_index(axes) * blocks
    edge = jnp.where(odd, blocks - 1, 0)
    copies = [
        pltpu.make_async_copy(pairs_hbm, pairs, sem.at[0]),
        pltpu.make_async_copy(live_hbm, live, sem.at[1]),
        pltpu.make_async_copy(x_hbm.at[span(edge), :], pay_ref.at[:BLK, :], sem.at[2]),
    ]
    for copy in copies:
        copy.start()
    for r in range(blocks):
        counts[r] = 0
    copies[0].wait()
    copies[1].wait()

    def count(s, carry):
        r = pairs[0, s] - base
        counts[r] = counts[r] + 1
        return carry

    lax.fori_loop(0, live[0], count, 0)
    tail = jnp.int32(0)
    start = jnp.int32(0)
    for r in range(blocks):
        tail += jnp.where(r + counts[r] > blocks, 1, 0)
        if r:
            start = jnp.where(r - 1 + counts[r - 1] == r, r, start)
        counts[blocks + 1 + r] = start
    counts[blocks] = tail
    pay_ref[BLK:, :] = jnp.full((EXTRA, pay_ref.shape[1]), tail.astype(F32)).astype(BF16)
    copies[2].wait()


def prepare(axes, pair_blocks, pair_count, x):
    length, width = x.shape
    blocks = length // BLK
    return pl.pallas_call(
        functools.partial(prep_kernel, blocks, axes),
        in_specs=[HBM] * 3,
        out_specs=[SMEM, VMEM],
        out_shape=[
            jax.ShapeDtypeStruct((2 * blocks + 1,), jnp.int32),
            jax.ShapeDtypeStruct((BLK + EXTRA, width), BF16),
        ],
        scratch_shapes=[
            pltpu.SMEM(pair_blocks.shape, jnp.int32),
            pltpu.SMEM(pair_count.shape, jnp.int32),
            pltpu.SemaphoreType.DMA((3,)),
        ],
        compiler_params=params(56),
        cost_estimate=pl.CostEstimate(
            flops=0, bytes_accessed=4 * BLK * width, transcendentals=0
        ),
        name="prepare",
    )(pair_blocks, pair_count, x)


def same_clusters(counts, blocks, row, col):
    return [
        [counts[blocks + 1 + row + a] == counts[blocks + 1 + col + b] for b in range(2)]
        for a in range(2)
    ]


def local_tile(x_ref, inv_ref, inv_row, row, col, same):
    others = x_ref[span(col, 2), :]
    other_inv = jnp.concatenate([inv_row[col], inv_row[col + 1]], axis=1)
    weight = weights(product(x_ref[span(row, 2), :], others), inv_ref[span(row, 2), :], other_inv)
    weight = scaled(weight, [[flag(s) for s in line] for line in same])
    return weight, others


def diagonal_kernel(blocks, counts, x_ref, acc_ref, sums_ref, inv_ref, inv_row, pay_ref):
    odd = lax.axis_index("sub") == 1
    pay_ref[...] = x_ref[span(jnp.where(odd, blocks - 2, 1)), :]

    def norms(r, carry):
        inv = inverse_norm(x_ref[span(r), :])
        inv_ref[span(r), :] = inv
        inv_row[r] = to_row(inv)
        return carry

    lax.fori_loop(0, blocks, norms, 0)

    def visit(k, carry):
        row = 2 * k
        same = same_clusters(counts, blocks, row, row)
        weight, others = local_tile(x_ref, inv_ref, inv_row, row, row, same)
        acc_ref[span(row, 2), :] = total(weight, others)
        sums = jnp.sum(weight, axis=1, keepdims=True)
        for a in range(2):
            store_row(sums_ref, row + a, to_row(sums[a * BLK : (a + 1) * BLK]))
        return carry

    lax.fori_loop(0, blocks // 2, visit, 0)


def rest_kernel(blocks, counts, x_ref, inv_ref, inv_row, acc_in, sums_in, acc_ref, sums_ref):
    half = blocks // 2

    def visit(k, carry):
        row = lax.div(k, half - 1) * 2
        col = lax.rem(lax.div(k, half - 1) + 1 + lax.rem(k, half - 1), half) * 2
        same = same_clusters(counts, blocks, row, col)

        @pl.when(same[0][0] | same[0][1] | same[1][0] | same[1][1])
        def _():
            weight, others = local_tile(x_ref, inv_ref, inv_row, row, col, same)
            add_tile(acc_ref, sums_ref, row, weight, others)

        return carry

    lax.fori_loop(0, half * (half - 1), visit, 0)


def diagonal_pairs(counts, x):
    length, width = x.shape
    blocks = length // BLK
    return pl.pallas_call(
        functools.partial(diagonal_kernel, blocks),
        in_specs=[SMEM, VMEM],
        out_specs=[VMEM] * 5,
        out_shape=[
            jax.ShapeDtypeStruct((length, width), F32),
            jax.ShapeDtypeStruct((2 * blocks, LANES), F32),
            jax.ShapeDtypeStruct((length, 1), F32),
            jax.ShapeDtypeStruct((blocks, 1, BLK), F32),
            jax.ShapeDtypeStruct((BLK, width), BF16),
        ],
        compiler_params=params(12),
        cost_estimate=pair_cost(2 * blocks, width),
        name="diagonal_pairs",
    )(counts, x)


def rest_pairs(counts, x, inv, inv_row, acc, sums, after):
    length, width = x.shape
    blocks = length // BLK

    def kernel(counts, x_ref, inv_ref, inv_row, after_ref, *refs):
        rest_kernel(blocks, counts, x_ref, inv_ref, inv_row, *refs)

    return pl.pallas_call(
        kernel,
        in_specs=[SMEM, VMEM, VMEM, VMEM, ANY, VMEM, VMEM],
        out_specs=[VMEM] * 2,
        out_shape=totals_shapes(x)[:2],
        input_output_aliases={5: 0, 6: 1},
        compiler_params=params(12),
        cost_estimate=pair_cost(blocks * blocks - 2 * blocks, width),
        name="rest_pairs",
    )(counts, x, inv, inv_row, after, acc, sums)


def write_payload(blocks, slot, info, x_ref, link_ref, pay_ref, acc):
    mine, theirs = info[MINE_LINK], info[THEIRS_LINK]
    shares = (mine >= 5) & (theirs >= slot - 2)

    @pl.when(jnp.logical_not(shares))
    def _():
        pay_ref[:BLK, :] = x_ref[span(link_place(info, slot - 1, blocks)), :]
        pay_ref[BLK:, :] = jnp.zeros((EXTRA, x_ref.shape[1]), BF16)

    @pl.when(shares)
    def _():
        link = link_ref[:BLK, :]
        link_inv = inverse_norm(link)
        acc[...] = jnp.zeros_like(acc)

        def add(k, sums):
            others = x_ref[span(link_place(info, k, blocks)), :]
            weight = weights(product(link, others), link_inv, to_row(inverse_norm(others)))
            acc[...] += total(weight, others)
            return sums + to_row(jnp.sum(weight, axis=1, keepdims=True))

        sums = lax.fori_loop(2, mine, add, jnp.zeros((1, BLK), F32))
        pay_ref[:BLK, :] = acc[...].astype(BF16)
        high = sums.astype(BF16)
        rest = sums - high.astype(F32)
        middle = rest.astype(BF16)
        low = (rest - middle.astype(F32)).astype(BF16)
        place = lax.broadcasted_iota(jnp.int32, (EXTRA, BLK), 0)
        parts = jnp.where(
            place == 0,
            high.astype(F32),
            jnp.where(place == 1, middle.astype(F32), jnp.where(place == 2, low.astype(F32), 0.0)),
        )
        pay_ref[BLK:, :BLK] = parts.astype(BF16)
        pay_ref[BLK:, BLK:] = jnp.zeros((EXTRA, x_ref.shape[1] - BLK), BF16)


def third_kernel(blocks, axes, counts, chip_pairs, x_ref, link_ref, pay_ref, info, acc):
    odd = lax.axis_index("sub") == 1
    base = lax.axis_index(axes) * blocks
    slots = chip_pairs.shape[1]
    listed = lax.fori_loop(
        0, slots, lambda s, n: n + jnp.where(chip_pairs[1, s] == base, 1, 0), jnp.int32(0)
    )
    told = jnp.max(link_ref[BLK:, :LANES].astype(F32)).astype(jnp.int32)
    head_theirs = jnp.where(odd, listed, told)
    head_mine = jnp.where(head_theirs > 0, counts[0], 0)
    tail_mine = counts[blocks]
    tail_theirs = counts[blocks - 1] - 1
    info[ODD] = jnp.where(odd, 1, 0)
    info[MINE_CHIP] = jnp.where(odd, head_mine, tail_mine)
    info[THEIRS_CHIP] = jnp.where(odd, head_theirs, tail_theirs)
    info[MINE_LINK] = jnp.where(odd, tail_mine, head_mine)
    info[THEIRS_LINK] = jnp.where(odd, tail_theirs, head_theirs)
    write_payload(blocks, 3, info, x_ref, link_ref, pay_ref, acc)


def third_payload(axes, counts, chip_pairs, x, link_block, after):
    length, width = x.shape
    blocks = length // BLK

    def kernel(counts, chip_pairs, x_ref, link_ref, after_ref, pay_ref, info, acc):
        third_kernel(blocks, axes, counts, chip_pairs, x_ref, link_ref, pay_ref, info, acc)

    return pl.pallas_call(
        kernel,
        in_specs=[SMEM, SMEM, VMEM, VMEM, ANY],
        out_specs=[VMEM, SMEM],
        out_shape=[
            jax.ShapeDtypeStruct((BLK + EXTRA, width), BF16),
            jax.ShapeDtypeStruct((8,), jnp.int32),
        ],
        scratch_shapes=[pltpu.VMEM((BLK, width), F32)],
        compiler_params=params(8),
        cost_estimate=pair_cost(2, width),
        name="third_payload",
    )(counts, chip_pairs, x, link_block, after)


def fourth_payload(info, x, link_block, after):
    length, width = x.shape
    blocks = length // BLK

    def kernel(info, x_ref, link_ref, after_ref, pay_ref, acc):
        write_payload(blocks, 4, info, x_ref, link_ref, pay_ref, acc)

    return pl.pallas_call(
        kernel,
        in_specs=[SMEM, VMEM, VMEM, ANY],
        out_specs=VMEM,
        out_shape=jax.ShapeDtypeStruct((BLK + EXTRA, width), BF16),
        scratch_shapes=[pltpu.VMEM((BLK, width), F32)],
        compiler_params=params(8),
        cost_estimate=pair_cost(2, width),
        name="fourth_payload",
    )(info, x, link_block, after)


def copy_out(acc_ref, out_ref, sem, r):
    return pltpu.make_async_copy(acc_ref.at[span(r), :], out_ref.at[span(r), :], sem.at[r])


def finish(acc_ref, sums_ref, out_ref, sem, r):
    acc_ref[span(r), :] = acc_ref[span(r), :] * (1.0 / to_column(load_row(sums_ref, r)))
    copy_out(acc_ref, out_ref, sem, r).start()


def each(blocks, chosen, body):
    def step(r, carry):
        @pl.when(chosen(r))
        def _():
            body(r)

        return carry

    lax.fori_loop(0, blocks, step, 0)


def add_tile(acc_ref, sums_ref, row, weight, others):
    acc_ref[span(row, 2), :] += total(weight, others)
    sums = jnp.sum(weight, axis=1, keepdims=True)
    for a in range(2):
        more = to_row(sums[a * BLK : (a + 1) * BLK])
        store_row(sums_ref, row + a, load_row(sums_ref, row + a) + more)


def chip_kernel(
    blocks, info, x_ref, inv_ref, chip_ref, acc_in, sums_in, acc_ref, sums_ref, out_ref, inv_row, sem
):
    odd = info[ODD] == 1
    mine, theirs = info[MINE_CHIP], info[THEIRS_CHIP]
    mine_link = info[MINE_LINK]

    def is_done(r):
        return jnp.where(odd, blocks - 1 - r, r) >= mine_link

    def column(n):
        col = jnp.where(odd, blocks - 2 - 2 * n, 2 * n)
        for b in range(2):
            inv_row[b] = to_row(inverse_norm(chip_ref[span(col + b), :]))
        theirs_ok = [jnp.where(odd, blocks - 1 - col - b, col + b) < theirs for b in range(2)]

        def tile(m, carry):
            row = jnp.where(odd, 2 * m, blocks - 2 - 2 * m)
            mine_ok = [jnp.where(odd, row + a, blocks - 1 - row - a) < mine for a in range(2)]
            others = chip_ref[span(col, 2), :]
            other_inv = jnp.concatenate([inv_row[0], inv_row[1]], axis=1)
            weight = weights(
                product(x_ref[span(row, 2), :], others), inv_ref[span(row, 2), :], other_inv
            )
            weight = scaled(weight, [[flag(p & q) for q in theirs_ok] for p in mine_ok])
            add_tile(acc_ref, sums_ref, row, weight, others)
            return carry

        lax.fori_loop(0, lax.div(mine + 1, 2), tile, 0)

    def columns(n, carry):
        column(n)
        return carry

    lax.fori_loop(0, lax.div(theirs + 1, 2), columns, 0)
    each(blocks, is_done, functools.partial(finish, acc_ref, sums_ref, out_ref, sem))
    each(blocks, is_done, lambda r: copy_out(acc_ref, out_ref, sem, r).wait())


def link_kernel(blocks, slots, info, x_ref, inv_ref, *refs):
    got_refs = refs[: len(slots)]
    acc_in, sums_in, out_in, acc_ref, sums_ref, out_ref, *dup_ref, sem = refs[len(slots) :]
    mine, theirs = info[MINE_LINK], info[THEIRS_LINK]
    odd = info[ODD] == 1

    for slot, got_ref in zip(slots, got_refs):
        uses = theirs >= slot
        if slot > 2:
            uses = uses & (theirs <= 4)

        @pl.when(uses)
        def _(got_ref=got_ref):
            other_inv = to_row(inverse_norm(got_ref[:BLK, :]))

            def tile(m, carry):
                row = jnp.where(odd, blocks - 2 - 2 * m, 2 * m)
                mine_ok = [jnp.where(odd, blocks - 1 - row - a, row + a) < mine for a in range(2)]
                others = got_ref[:BLK, :]
                weight = weights(
                    product(x_ref[span(row, 2), :], others), inv_ref[span(row, 2), :], other_inv
                )
                weight = scaled(weight, [[flag(p)] for p in mine_ok])
                add_tile(acc_ref, sums_ref, row, weight, others)
                return carry

            lax.fori_loop(0, lax.div(mine + 1, 2), tile, 0)

        if slot > 2:

            @pl.when((theirs >= 5) & (mine >= slot - 2))
            def _(slot=slot, got_ref=got_ref):
                r = link_place(info, slot - 3, blocks)
                acc_ref[span(r), :] += got_ref[:BLK, :].astype(F32)
                more = jnp.sum(got_ref[BLK:, :BLK].astype(F32), axis=0, keepdims=True)
                store_row(sums_ref, r, load_row(sums_ref, r) + more)

    def is_done(r):
        k = jnp.where(odd, blocks - 1 - r, r)
        last = jnp.where(theirs >= 5, k + 3, jnp.maximum(theirs, 2))
        now = last == slots[0]
        for slot in slots[1:]:
            now = now | (last == slot)
        return (k < mine) & now

    dup_copies = [pltpu.make_async_copy(sums_ref, ref, sem.at[blocks]) for ref in dup_ref]
    for copy in dup_copies:
        copy.start()
    each(blocks, is_done, functools.partial(finish, acc_ref, sums_ref, out_ref, sem))
    each(blocks, is_done, lambda r: copy_out(acc_ref, out_ref, sem, r).wait())
    for copy in dup_copies:
        copy.wait()


def totals_shapes(x):
    length, width = x.shape
    return [
        jax.ShapeDtypeStruct((length, width), F32),
        jax.ShapeDtypeStruct((2 * length // BLK, LANES), F32),
        jax.ShapeDtypeStruct((length, width), F32),
    ]


def chip_pairs(info, x, inv, chip_x, acc, sums):
    length, width = x.shape
    blocks = length // BLK
    return pl.pallas_call(
        functools.partial(chip_kernel, blocks),
        in_specs=[SMEM] + [VMEM] * 5,
        out_specs=[VMEM, VMEM, ANY],
        out_shape=totals_shapes(x),
        scratch_shapes=[pltpu.VMEM((2, 1, BLK), F32), pltpu.SemaphoreType.DMA((blocks,))],
        input_output_aliases={4: 0, 5: 1},
        compiler_params=params(8),
        cost_estimate=pair_cost(12, width),
        name="chip_pairs",
    )(info, x, inv, chip_x, acc, sums)


def link_pairs(slots, info, x, inv, got, acc, sums, out, last=False):
    length, width = x.shape
    blocks = length // BLK
    n = len(slots)
    return pl.pallas_call(
        functools.partial(link_kernel, blocks, slots),
        in_specs=[SMEM] + [VMEM] * (4 + n) + [ANY],
        out_specs=[VMEM, VMEM, ANY] + [ANY] * last,
        out_shape=totals_shapes(x) + totals_shapes(x)[1:2] * last,
        scratch_shapes=[pltpu.SemaphoreType.DMA((blocks + 1,))],
        input_output_aliases={3 + n: 0, 4 + n: 1, 5 + n: 2},
        compiler_params=params(8),
        cost_estimate=pair_cost(6 * n, width),
        name="link_pairs",
    )(info, x, inv, *got, acc, sums, out)


def per_device(embeddings, pair_blocks, pair_count):
    length, width = embeddings.shape
    blocks = length // BLK
    axes = ("rows", "sub")
    devices = lax.axis_size(axes)
    edges = [(i, i + 1) for i in range(1, devices - 1, 2)]
    edges += [(j, i) for i, j in edges]

    def over_link(array):
        return lax.ppermute(array, axes, edges)

    def over_chip(array):
        return lax.ppermute(array, "sub", [(0, 1), (1, 0)])

    x = embeddings
    counts, first = prepare(axes, pair_blocks, pair_count, x)
    one = over_link(first)
    chip_x = over_chip(x)
    chip_list = over_chip(pair_blocks)
    acc, sums, inv, inv_row, second = diagonal_pairs(counts, x)
    two = over_link(second)
    acc, sums = rest_pairs(counts, x, inv, inv_row, acc, sums, second)
    third, info = third_payload(axes, counts, chip_list, x, one, sums)
    three = over_link(third)
    acc, sums, out = chip_pairs(info, x, inv, chip_x, acc, sums)
    fourth = fourth_payload(info, x, two, sums)
    four = over_link(fourth)
    acc, sums, out = link_pairs((1, 2), info, x, inv, (one, two), acc, sums, out)
    acc, sums, out = link_pairs((3,), info, x, inv, (three,), acc, sums, out)
    acc, sums, out, dup = link_pairs((4,), info, x, inv, (four,), acc, sums, out, last=True)
    return dup.reshape(length), out


def solution(mesh):
    in_specs = (
        P(("groups", "rows", "sub"), None),
        P(None, ("groups", "rows", "sub")),
        P(("groups", "rows", "sub")),
    )
    out_specs = (P(("groups", "rows", "sub")), P(("groups", "rows", "sub"), None))
    return jax.shard_map(
        per_device, mesh=mesh, in_specs=in_specs, out_specs=out_specs, check_vma=False
    )
```

```python
import functools

import jax
import jax.numpy as jnp
from jax import lax
from jax.experimental import pallas as pl
from jax.experimental.pallas import tpu as pltpu
from jax.sharding import PartitionSpec as P

BLK = 256
EXTRA = 16
TEMPER = 4.0
EPS = 1e-06
LANES = 128
MIB = 1024 * 1024

F32 = jnp.float32
BF16 = jnp.bfloat16

ODD, MINE_CHIP, THEIRS_CHIP, MINE_LINK, THEIRS_LINK = range(5)

VMEM = pl.BlockSpec(memory_space=pltpu.VMEM)
SMEM = pl.BlockSpec(memory_space=pltpu.SMEM)
ANY = pl.BlockSpec(memory_space=pl.ANY)
HBM = pl.BlockSpec(memory_space=pltpu.HBM)


def diagonal():
    return lax.broadcasted_iota(jnp.int32, (BLK, BLK), 0) == lax.broadcasted_iota(
        jnp.int32, (BLK, BLK), 1
    )


def to_row(column):
    return jnp.sum(jnp.where(diagonal(), column, 0.0), axis=0, keepdims=True)


def to_column(row):
    return jnp.sum(jnp.where(diagonal(), row, 0.0), axis=1, keepdims=True)


def inverse_norm(rows):
    wide = rows.astype(F32)
    return lax.rsqrt(jnp.sum(wide * wide, axis=1, keepdims=True) + EPS)


def store_row(ref, place, row):
    ref[pl.ds(2 * place, 1), :] = row[:, :LANES]
    ref[pl.ds(2 * place + 1, 1), :] = row[:, LANES:]


def load_row(ref, place):
    return jnp.concatenate([ref[pl.ds(2 * place, 1), :], ref[pl.ds(2 * place + 1, 1), :]], axis=1)


def span(place, n=1):
    return pl.ds(pl.multiple_of(place * BLK, BLK), n * BLK)


def product(rows, others):
    return lax.dot_general(rows, others, (((1,), (1,)), ((), ())), preferred_element_type=F32)


def weights(inner, row_inv, other_inv):
    return jnp.exp(inner * (TEMPER * row_inv) * other_inv - TEMPER)


def total(weight, others):
    return jnp.dot(weight.astype(BF16), others, preferred_element_type=F32)


def scaled(weight, flags):
    return jnp.concatenate(
        [
            jnp.concatenate(
                [
                    weight[a * BLK : (a + 1) * BLK, b * BLK : (b + 1) * BLK] * flag
                    for b, flag in enumerate(row)
                ],
                axis=1,
            )
            for a, row in enumerate(flags)
        ],
        axis=0,
    )


def flag(condition):
    return jnp.where(condition, 1.0, 0.0).astype(F32)


def pair_cost(pairs, width):
    return pl.CostEstimate(
        flops=pairs * BLK * BLK * width // 64, bytes_accessed=BLK * width, transcendentals=0
    )


def params(mib):
    return pltpu.CompilerParams(vmem_limit_bytes=mib * MIB)


def link_place(info, k, blocks):
    return jnp.where(info[ODD] == 1, blocks - 1 - k, k)


def prep_kernel(blocks, axes, pairs_hbm, live_hbm, x_hbm, counts, pay_ref, pairs, live, sem):
    odd = lax.axis_index("sub") == 1
    base = lax.axis_index(axes) * blocks
    edge = jnp.where(odd, blocks - 1, 0)
    copies = [
        pltpu.make_async_copy(pairs_hbm, pairs, sem.at[0]),
        pltpu.make_async_copy(live_hbm, live, sem.at[1]),
        pltpu.make_async_copy(x_hbm.at[span(edge), :], pay_ref.at[:BLK, :], sem.at[2]),
    ]
    for copy in copies:
        copy.start()
    for r in range(blocks):
        counts[r] = 0
    copies[0].wait()
    copies[1].wait()

    def count(s, carry):
        r = pairs[0, s] - base
        counts[r] = counts[r] + 1
        return carry

    lax.fori_loop(0, live[0], count, 0)
    tail = jnp.int32(0)
    start = jnp.int32(0)
    for r in range(blocks):
        tail += jnp.where(r + counts[r] > blocks, 1, 0)
        if r:
            start = jnp.where(r - 1 + counts[r - 1] == r, r, start)
        counts[blocks + 1 + r] = start
    counts[blocks] = tail
    pay_ref[BLK:, :] = jnp.full((EXTRA, pay_ref.shape[1]), tail.astype(F32)).astype(BF16)
    copies[2].wait()


def prepare(axes, pair_blocks, pair_count, x):
    length, width = x.shape
    blocks = length // BLK
    return pl.pallas_call(
        functools.partial(prep_kernel, blocks, axes),
        in_specs=[HBM] * 3,
        out_specs=[SMEM, VMEM],
        out_shape=[
            jax.ShapeDtypeStruct((2 * blocks + 1,), jnp.int32),
            jax.ShapeDtypeStruct((BLK + EXTRA, width), BF16),
        ],
        scratch_shapes=[
            pltpu.SMEM(pair_blocks.shape, jnp.int32),
            pltpu.SMEM(pair_count.shape, jnp.int32),
            pltpu.SemaphoreType.DMA((3,)),
        ],
        compiler_params=params(56),
        cost_estimate=pl.CostEstimate(
            flops=0, bytes_accessed=4 * BLK * width, transcendentals=0
        ),
        name="prepare",
    )(pair_blocks, pair_count, x)


def same_clusters(counts, blocks, row, col):
    return [
        [counts[blocks + 1 + row + a] == counts[blocks + 1 + col + b] for b in range(2)]
        for a in range(2)
    ]


def local_tile(x_ref, inv_ref, inv_row, row, col, same):
    others = x_ref[span(col, 2), :]
    other_inv = jnp.concatenate([inv_row[col], inv_row[col + 1]], axis=1)
    weight = weights(product(x_ref[span(row, 2), :], others), inv_ref[span(row, 2), :], other_inv)
    weight = scaled(weight, [[flag(s) for s in line] for line in same])
    return weight, others


def diagonal_kernel(blocks, counts, after, x_ref, acc_ref, sums_ref, inv_ref, inv_row, pay_ref):
    odd = lax.axis_index("sub") == 1
    pay_ref[...] = x_ref[span(jnp.where(odd, blocks - 2, 1)), :]

    def norms(r, carry):
        inv = inverse_norm(x_ref[span(r), :])
        inv_ref[span(r), :] = inv
        inv_row[r] = to_row(inv)
        return carry

    lax.fori_loop(0, blocks, norms, 0)

    def visit(k, carry):
        row = 2 * k
        same = same_clusters(counts, blocks, row, row)
        weight, others = local_tile(x_ref, inv_ref, inv_row, row, row, same)
        acc_ref[span(row, 2), :] = total(weight, others)
        sums = jnp.sum(weight, axis=1, keepdims=True)
        for a in range(2):
            store_row(sums_ref, row + a, to_row(sums[a * BLK : (a + 1) * BLK]))
        return carry

    lax.fori_loop(0, blocks // 2, visit, 0)


def rest_kernel(blocks, counts, x_ref, inv_ref, inv_row, acc_in, sums_in, acc_ref, sums_ref):
    half = blocks // 2

    def visit(k, carry):
        row = lax.div(k, half - 1) * 2
        col = lax.rem(lax.div(k, half - 1) + 1 + lax.rem(k, half - 1), half) * 2
        same = same_clusters(counts, blocks, row, col)

        @pl.when(same[0][0] | same[0][1] | same[1][0] | same[1][1])
        def _():
            weight, others = local_tile(x_ref, inv_ref, inv_row, row, col, same)
            add_tile(acc_ref, sums_ref, row, weight, others)

        return carry

    lax.fori_loop(0, half * (half - 1), visit, 0)


def diagonal_pairs(counts, x, after):
    length, width = x.shape
    blocks = length // BLK
    return pl.pallas_call(
        functools.partial(diagonal_kernel, blocks),
        in_specs=[SMEM, SMEM, VMEM],
        out_specs=[VMEM] * 5,
        out_shape=[
            jax.ShapeDtypeStruct((length, width), F32),
            jax.ShapeDtypeStruct((2 * blocks, LANES), F32),
            jax.ShapeDtypeStruct((length, 1), F32),
            jax.ShapeDtypeStruct((blocks, 1, BLK), F32),
            jax.ShapeDtypeStruct((BLK, width), BF16),
        ],
        compiler_params=params(12),
        cost_estimate=pair_cost(2 * blocks, width),
        name="diagonal_pairs",
    )(counts, after, x)


def rest_pairs(counts, x, inv, inv_row, acc, sums, after):
    length, width = x.shape
    blocks = length // BLK

    def kernel(counts, x_ref, inv_ref, inv_row, after, *refs):
        rest_kernel(blocks, counts, x_ref, inv_ref, inv_row, *refs)

    return pl.pallas_call(
        kernel,
        in_specs=[SMEM, VMEM, VMEM, VMEM, SMEM, VMEM, VMEM],
        out_specs=[VMEM] * 2,
        out_shape=totals_shapes(x)[:2],
        input_output_aliases={5: 0, 6: 1},
        compiler_params=params(12),
        cost_estimate=pair_cost(blocks * blocks - 2 * blocks, width),
        name="rest_pairs",
    )(counts, x, inv, inv_row, after, acc, sums)


def write_payload(blocks, slot, info, x_ref, link_ref, pay_ref, acc):
    mine, theirs = info[MINE_LINK], info[THEIRS_LINK]
    shares = (mine >= 5) & (theirs >= slot - 2)

    @pl.when(jnp.logical_not(shares))
    def _():
        pay_ref[:BLK, :] = x_ref[span(link_place(info, slot - 1, blocks)), :]
        pay_ref[BLK:, :] = jnp.zeros((EXTRA, x_ref.shape[1]), BF16)

    @pl.when(shares)
    def _():
        link = link_ref[:BLK, :]
        link_inv = inverse_norm(link)
        acc[...] = jnp.zeros_like(acc)

        def add(k, sums):
            others = x_ref[span(link_place(info, k, blocks)), :]
            weight = weights(product(link, others), link_inv, to_row(inverse_norm(others)))
            acc[...] += total(weight, others)
            return sums + to_row(jnp.sum(weight, axis=1, keepdims=True))

        sums = lax.fori_loop(2, mine, add, jnp.zeros((1, BLK), F32))
        pay_ref[:BLK, :] = acc[...].astype(BF16)
        high = sums.astype(BF16)
        rest = sums - high.astype(F32)
        middle = rest.astype(BF16)
        low = (rest - middle.astype(F32)).astype(BF16)
        place = lax.broadcasted_iota(jnp.int32, (EXTRA, BLK), 0)
        parts = jnp.where(
            place == 0,
            high.astype(F32),
            jnp.where(place == 1, middle.astype(F32), jnp.where(place == 2, low.astype(F32), 0.0)),
        )
        pay_ref[BLK:, :BLK] = parts.astype(BF16)
        pay_ref[BLK:, BLK:] = jnp.zeros((EXTRA, x_ref.shape[1] - BLK), BF16)


def third_kernel(blocks, axes, counts, chip_pairs, x_ref, link_ref, pay_ref, info, acc):
    odd = lax.axis_index("sub") == 1
    base = lax.axis_index(axes) * blocks
    slots = chip_pairs.shape[1]
    listed = lax.fori_loop(
        0, slots, lambda s, n: n + jnp.where(chip_pairs[1, s] == base, 1, 0), jnp.int32(0)
    )
    told = jnp.max(link_ref[BLK:, :LANES].astype(F32)).astype(jnp.int32)
    head_theirs = jnp.where(odd, listed, told)
    head_mine = jnp.where(head_theirs > 0, counts[0], 0)
    tail_mine = counts[blocks]
    tail_theirs = counts[blocks - 1] - 1
    info[ODD] = jnp.where(odd, 1, 0)
    info[MINE_CHIP] = jnp.where(odd, head_mine, tail_mine)
    info[THEIRS_CHIP] = jnp.where(odd, head_theirs, tail_theirs)
    info[MINE_LINK] = jnp.where(odd, tail_mine, head_mine)
    info[THEIRS_LINK] = jnp.where(odd, tail_theirs, head_theirs)
    write_payload(blocks, 3, info, x_ref, link_ref, pay_ref, acc)


def third_payload(axes, counts, chip_pairs, x, link_block, after):
    length, width = x.shape
    blocks = length // BLK

    def kernel(counts, chip_pairs, x_ref, link_ref, after_ref, pay_ref, info, acc):
        third_kernel(blocks, axes, counts, chip_pairs, x_ref, link_ref, pay_ref, info, acc)

    return pl.pallas_call(
        kernel,
        in_specs=[SMEM, SMEM, VMEM, VMEM, ANY],
        out_specs=[VMEM, SMEM],
        out_shape=[
            jax.ShapeDtypeStruct((BLK + EXTRA, width), BF16),
            jax.ShapeDtypeStruct((8,), jnp.int32),
        ],
        scratch_shapes=[pltpu.VMEM((BLK, width), F32)],
        compiler_params=params(8),
        cost_estimate=pair_cost(2, width),
        name="third_payload",
    )(counts, chip_pairs, x, link_block, after)


def fourth_payload(info, x, link_block, after):
    length, width = x.shape
    blocks = length // BLK

    def kernel(info, x_ref, link_ref, after_ref, pay_ref, acc):
        write_payload(blocks, 4, info, x_ref, link_ref, pay_ref, acc)

    return pl.pallas_call(
        kernel,
        in_specs=[SMEM, VMEM, VMEM, ANY],
        out_specs=VMEM,
        out_shape=jax.ShapeDtypeStruct((BLK + EXTRA, width), BF16),
        scratch_shapes=[pltpu.VMEM((BLK, width), F32)],
        compiler_params=params(8),
        cost_estimate=pair_cost(2, width),
        name="fourth_payload",
    )(info, x, link_block, after)


def copy_out(acc_ref, out_ref, sem, r):
    return pltpu.make_async_copy(acc_ref.at[span(r), :], out_ref.at[span(r), :], sem.at[r])


def finish(acc_ref, sums_ref, out_ref, sem, r):
    acc_ref[span(r), :] = acc_ref[span(r), :] * (1.0 / to_column(load_row(sums_ref, r)))
    copy_out(acc_ref, out_ref, sem, r).start()


def each(blocks, chosen, body):
    def step(r, carry):
        @pl.when(chosen(r))
        def _():
            body(r)

        return carry

    lax.fori_loop(0, blocks, step, 0)


def add_tile(acc_ref, sums_ref, row, weight, others):
    acc_ref[span(row, 2), :] += total(weight, others)
    sums = jnp.sum(weight, axis=1, keepdims=True)
    for a in range(2):
        more = to_row(sums[a * BLK : (a + 1) * BLK])
        store_row(sums_ref, row + a, load_row(sums_ref, row + a) + more)


def chip_kernel(
    blocks,
    info,
    x_ref,
    inv_ref,
    chip_ref,
    after_ref,
    acc_in,
    sums_in,
    acc_ref,
    sums_ref,
    out_ref,
    inv_row,
    sem,
):
    odd = info[ODD] == 1
    mine, theirs = info[MINE_CHIP], info[THEIRS_CHIP]
    mine_link = info[MINE_LINK]

    def is_done(r):
        return jnp.where(odd, blocks - 1 - r, r) >= mine_link

    def column(n):
        col = jnp.where(odd, blocks - 2 - 2 * n, 2 * n)
        for b in range(2):
            inv_row[b] = to_row(inverse_norm(chip_ref[span(col + b), :]))
        theirs_ok = [jnp.where(odd, blocks - 1 - col - b, col + b) < theirs for b in range(2)]

        def tile(m, carry):
            row = jnp.where(odd, 2 * m, blocks - 2 - 2 * m)
            mine_ok = [jnp.where(odd, row + a, blocks - 1 - row - a) < mine for a in range(2)]
            others = chip_ref[span(col, 2), :]
            other_inv = jnp.concatenate([inv_row[0], inv_row[1]], axis=1)
            weight = weights(
                product(x_ref[span(row, 2), :], others), inv_ref[span(row, 2), :], other_inv
            )
            weight = scaled(weight, [[flag(p & q) for q in theirs_ok] for p in mine_ok])
            add_tile(acc_ref, sums_ref, row, weight, others)
            return carry

        lax.fori_loop(0, lax.div(mine + 1, 2), tile, 0)

    def columns(n, carry):
        column(n)
        return carry

    lax.fori_loop(0, lax.div(theirs + 1, 2), columns, 0)
    each(blocks, is_done, functools.partial(finish, acc_ref, sums_ref, out_ref, sem))
    each(blocks, is_done, lambda r: copy_out(acc_ref, out_ref, sem, r).wait())


def link_kernel(blocks, slots, info, x_ref, inv_ref, *refs):
    got_refs = refs[: len(slots)]
    acc_in, sums_in, out_in, acc_ref, sums_ref, out_ref, *dup_ref, side, inv_row, sem = refs[
        len(slots) :
    ]
    mine, theirs = info[MINE_LINK], info[THEIRS_LINK]
    odd = info[ODD] == 1

    uses = theirs >= slots[0]
    if slots[0] > 2:
        uses = uses & (theirs <= 4)

    @pl.when(uses)
    def _():
        for k, got_ref in enumerate(got_refs):
            block = got_ref[:BLK, :]
            side[k * BLK : (k + 1) * BLK, :] = block
            inv_row[:, k * BLK : (k + 1) * BLK] = to_row(inverse_norm(block))

        def tile(m, carry):
            row = jnp.where(odd, blocks - 2 - 2 * m, 2 * m)
            mine_ok = [jnp.where(odd, blocks - 1 - row - a, row + a) < mine for a in range(2)]
            others = side[...]
            weight = weights(
                product(x_ref[span(row, 2), :], others), inv_ref[span(row, 2), :], inv_row[...]
            )
            weight = scaled(weight, [[flag(p & (theirs >= q)) for q in slots] for p in mine_ok])
            add_tile(acc_ref, sums_ref, row, weight, others)
            return carry

        lax.fori_loop(0, lax.div(mine + 1, 2), tile, 0)

    if slots[0] > 2:
        slot = slots[0]

        @pl.when((theirs >= 5) & (mine >= slot - 2))
        def _():
            r = link_place(info, slot - 3, blocks)
            acc_ref[span(r), :] += got_refs[0][:BLK, :].astype(F32)
            more = jnp.sum(got_refs[0][BLK:, :BLK].astype(F32), axis=0, keepdims=True)
            store_row(sums_ref, r, load_row(sums_ref, r) + more)

    def is_done(r):
        k = jnp.where(odd, blocks - 1 - r, r)
        last = jnp.where(theirs >= 5, k + 3, jnp.maximum(theirs, 2))
        now = last == slots[0]
        for slot in slots[1:]:
            now = now | (last == slot)
        return (k < mine) & now

    dup_copies = [pltpu.make_async_copy(sums_ref, ref, sem.at[blocks]) for ref in dup_ref]
    for copy in dup_copies:
        copy.start()
    each(blocks, is_done, functools.partial(finish, acc_ref, sums_ref, out_ref, sem))
    each(blocks, is_done, lambda r: copy_out(acc_ref, out_ref, sem, r).wait())
    for copy in dup_copies:
        copy.wait()


def totals_shapes(x):
    length, width = x.shape
    return [
        jax.ShapeDtypeStruct((length, width), F32),
        jax.ShapeDtypeStruct((2 * length // BLK, LANES), F32),
        jax.ShapeDtypeStruct((length, width), F32),
    ]


def chip_pairs(info, x, inv, chip_x, acc, sums, after):
    length, width = x.shape
    blocks = length // BLK
    return pl.pallas_call(
        functools.partial(chip_kernel, blocks),
        in_specs=[SMEM] + [VMEM] * 3 + [ANY] + [VMEM] * 2,
        out_specs=[VMEM, VMEM, ANY],
        out_shape=totals_shapes(x),
        scratch_shapes=[pltpu.VMEM((2, 1, BLK), F32), pltpu.SemaphoreType.DMA((blocks,))],
        input_output_aliases={5: 0, 6: 1},
        compiler_params=params(8),
        cost_estimate=pair_cost(12, width),
        name="chip_pairs",
    )(info, x, inv, chip_x, after, acc, sums)


def link_pairs(slots, info, x, inv, got, acc, sums, out, last=False):
    length, width = x.shape
    blocks = length // BLK
    n = len(slots)
    return pl.pallas_call(
        functools.partial(link_kernel, blocks, slots),
        in_specs=[SMEM] + [VMEM] * (4 + n) + [ANY],
        out_specs=[VMEM, VMEM, ANY] + [ANY] * last,
        out_shape=totals_shapes(x) + totals_shapes(x)[1:2] * last,
        scratch_shapes=[
            pltpu.VMEM((n * BLK, width), BF16),
            pltpu.VMEM((1, n * BLK), F32),
            pltpu.SemaphoreType.DMA((blocks + 1,)),
        ],
        input_output_aliases={3 + n: 0, 4 + n: 1, 5 + n: 2},
        compiler_params=params(8),
        cost_estimate=pair_cost(6 * n, width),
        name="link_pairs",
    )(info, x, inv, *got, acc, sums, out)


def per_device(embeddings, pair_blocks, pair_count):
    length, width = embeddings.shape
    blocks = length // BLK
    axes = ("rows", "sub")
    devices = lax.axis_size(axes)
    edges = [(i, i + 1) for i in range(1, devices - 1, 2)]
    edges += [(j, i) for i, j in edges]

    def over_link(array):
        return lax.ppermute(array, axes, edges)

    def over_chip(array):
        return lax.ppermute(array, "sub", [(0, 1), (1, 0)])

    x = embeddings
    counts, first = prepare(axes, pair_blocks, pair_count, x)
    one = over_link(first)
    chip_x = over_chip(x)
    chip_list = over_chip(pair_blocks)
    acc, sums, inv, inv_row, second = diagonal_pairs(counts, x, chip_list)
    two = over_link(second)
    third, info = third_payload(axes, counts, chip_list, x, one, second)
    three = over_link(third)
    acc, sums = rest_pairs(counts, x, inv, inv_row, acc, sums, info)
    fourth = fourth_payload(info, x, two, sums)
    four = over_link(fourth)
    acc, sums, out = chip_pairs(info, x, inv, chip_x, acc, sums, fourth)
    acc, sums, out = link_pairs((1, 2), info, x, inv, (one, two), acc, sums, out)
    acc, sums, out = link_pairs((3,), info, x, inv, (three,), acc, sums, out)
    acc, sums, out, dup = link_pairs((4,), info, x, inv, (four,), acc, sums, out, last=True)
    return dup.reshape(length), out


def solution(mesh):
    in_specs = (
        P(("groups", "rows", "sub"), None),
        P(None, ("groups", "rows", "sub")),
        P(("groups", "rows", "sub")),
    )
    out_specs = (P(("groups", "rows", "sub")), P(("groups", "rows", "sub"), None))
    return jax.shard_map(
        per_device, mesh=mesh, in_specs=in_specs, out_specs=out_specs, check_vma=False
    )
```

```python
import functools

import jax
import jax.numpy as jnp
from jax import lax
from jax.experimental import pallas as pl
from jax.experimental.pallas import tpu as pltpu
from jax.sharding import PartitionSpec as P

BLK = 256
EXTRA = 16
TEMPER = 4.0
LOG2_E = 1.4426950408889634
NEVER = 1e30
EPS = 1e-06
LANES = 128
MIB = 1024 * 1024

F32 = jnp.float32
BF16 = jnp.bfloat16

ODD, MINE_CHIP, THEIRS_CHIP, MINE_LINK, THEIRS_LINK = range(5)

VMEM = pl.BlockSpec(memory_space=pltpu.VMEM)
SMEM = pl.BlockSpec(memory_space=pltpu.SMEM)
ANY = pl.BlockSpec(memory_space=pl.ANY)
HBM = pl.BlockSpec(memory_space=pltpu.HBM)


def diagonal():
    return lax.broadcasted_iota(jnp.int32, (BLK, BLK), 0) == lax.broadcasted_iota(
        jnp.int32, (BLK, BLK), 1
    )


def to_row(column):
    return jnp.sum(jnp.where(diagonal(), column, 0.0), axis=0, keepdims=True)


def to_column(row):
    return jnp.sum(jnp.where(diagonal(), row, 0.0), axis=1, keepdims=True)


def inverse_norm(rows):
    wide = rows.astype(F32)
    return lax.rsqrt(jnp.sum(wide * wide, axis=1, keepdims=True) + EPS)


def store_row(ref, place, row):
    ref[pl.ds(2 * place, 1), :] = row[:, :LANES]
    ref[pl.ds(2 * place + 1, 1), :] = row[:, LANES:]


def load_row(ref, place):
    return jnp.concatenate([ref[pl.ds(2 * place, 1), :], ref[pl.ds(2 * place + 1, 1), :]], axis=1)


def span(place, n=1):
    return pl.ds(pl.multiple_of(place * BLK, BLK), n * BLK)


def product(rows, others):
    return lax.dot_general(rows, others, (((1,), (1,)), ((), ())), preferred_element_type=F32)


def weights(inner, row_inv, other_inv, used=None):
    scaled = inner * (TEMPER * LOG2_E * row_inv) * other_inv
    if used is None:
        return jnp.exp2(scaled - TEMPER * LOG2_E)
    return jnp.concatenate(
        [
            jnp.concatenate(
                [
                    jnp.exp2(
                        scaled[a * BLK : (a + 1) * BLK, b * BLK : (b + 1) * BLK]
                        - jnp.where(use, TEMPER * LOG2_E, NEVER)
                    )
                    for b, use in enumerate(line)
                ],
                axis=1,
            )
            for a, line in enumerate(used)
        ],
        axis=0,
    )


def total(weight, others):
    return jnp.dot(weight.astype(BF16), others, preferred_element_type=F32)


def pair_cost(pairs, width):
    return pl.CostEstimate(
        flops=pairs * BLK * BLK * width // 64, bytes_accessed=BLK * width, transcendentals=0
    )


def params(mib):
    return pltpu.CompilerParams(vmem_limit_bytes=mib * MIB)


def link_place(info, k, blocks):
    return jnp.where(info[ODD] == 1, blocks - 1 - k, k)


def prep_kernel(blocks, axes, pairs_hbm, live_hbm, x_hbm, counts, pay_ref, pairs, live, sem):
    odd = lax.axis_index("sub") == 1
    base = lax.axis_index(axes) * blocks
    edge = jnp.where(odd, blocks - 1, 0)
    copies = [
        pltpu.make_async_copy(pairs_hbm, pairs, sem.at[0]),
        pltpu.make_async_copy(live_hbm, live, sem.at[1]),
        pltpu.make_async_copy(x_hbm.at[span(edge), :], pay_ref.at[:BLK, :], sem.at[2]),
    ]
    for copy in copies:
        copy.start()
    for r in range(blocks):
        counts[r] = 0
    copies[0].wait()
    copies[1].wait()

    def count(s, carry):
        r = pairs[0, s] - base
        counts[r] = counts[r] + 1
        return carry

    lax.fori_loop(0, live[0], count, 0)
    tail = jnp.int32(0)
    start = jnp.int32(0)
    for r in range(blocks):
        tail += jnp.where(r + counts[r] > blocks, 1, 0)
        if r:
            start = jnp.where(r - 1 + counts[r - 1] == r, r, start)
        counts[blocks + 1 + r] = start
    counts[blocks] = tail
    pay_ref[BLK:, :] = jnp.full((EXTRA, pay_ref.shape[1]), tail.astype(F32)).astype(BF16)
    copies[2].wait()


def prepare(axes, pair_blocks, pair_count, x):
    length, width = x.shape
    blocks = length // BLK
    return pl.pallas_call(
        functools.partial(prep_kernel, blocks, axes),
        in_specs=[HBM] * 3,
        out_specs=[SMEM, VMEM],
        out_shape=[
            jax.ShapeDtypeStruct((2 * blocks + 1,), jnp.int32),
            jax.ShapeDtypeStruct((BLK + EXTRA, width), BF16),
        ],
        scratch_shapes=[
            pltpu.SMEM(pair_blocks.shape, jnp.int32),
            pltpu.SMEM(pair_count.shape, jnp.int32),
            pltpu.SemaphoreType.DMA((3,)),
        ],
        compiler_params=params(56),
        cost_estimate=pl.CostEstimate(
            flops=0, bytes_accessed=4 * BLK * width, transcendentals=0
        ),
        name="prepare",
    )(pair_blocks, pair_count, x)


def same_clusters(counts, blocks, row, col):
    return [
        [counts[blocks + 1 + row + a] == counts[blocks + 1 + col + b] for b in range(2)]
        for a in range(2)
    ]


def local_tile(x_ref, inv_ref, inv_row, row, col, same):
    others = x_ref[span(col, 2), :]
    other_inv = jnp.concatenate([inv_row[col], inv_row[col + 1]], axis=1)
    inner = product(x_ref[span(row, 2), :], others)
    return weights(inner, inv_ref[span(row, 2), :], other_inv, same), others


def diagonal_kernel(blocks, counts, after, x_ref, acc_ref, sums_ref, inv_ref, inv_row, pay_ref):
    odd = lax.axis_index("sub") == 1
    pay_ref[...] = x_ref[span(jnp.where(odd, blocks - 2, 1)), :]

    def norms(r, carry):
        inv = inverse_norm(x_ref[span(r), :])
        inv_ref[span(r), :] = inv
        inv_row[r] = to_row(inv)
        return carry

    lax.fori_loop(0, blocks, norms, 0)

    def visit(k, carry):
        row = 2 * k
        same = same_clusters(counts, blocks, row, row)
        weight, others = local_tile(x_ref, inv_ref, inv_row, row, row, same)
        acc_ref[span(row, 2), :] = total(weight, others)
        sums = jnp.sum(weight, axis=1, keepdims=True)
        for a in range(2):
            store_row(sums_ref, row + a, to_row(sums[a * BLK : (a + 1) * BLK]))
        return carry

    lax.fori_loop(0, blocks // 2, visit, 0)


def rest_kernel(blocks, counts, x_ref, inv_ref, inv_row, acc_in, sums_in, acc_ref, sums_ref):
    half = blocks // 2

    def visit(k, carry):
        row = lax.div(k, half - 1) * 2
        col = lax.rem(lax.div(k, half - 1) + 1 + lax.rem(k, half - 1), half) * 2
        same = same_clusters(counts, blocks, row, col)

        @pl.when(same[0][0] | same[0][1] | same[1][0] | same[1][1])
        def _():
            weight, others = local_tile(x_ref, inv_ref, inv_row, row, col, same)
            add_tile(acc_ref, sums_ref, row, weight, others)

        return carry

    lax.fori_loop(0, half * (half - 1), visit, 0)


def diagonal_pairs(counts, x, after):
    length, width = x.shape
    blocks = length // BLK
    return pl.pallas_call(
        functools.partial(diagonal_kernel, blocks),
        in_specs=[SMEM, SMEM, VMEM],
        out_specs=[VMEM] * 5,
        out_shape=[
            jax.ShapeDtypeStruct((length, width), F32),
            jax.ShapeDtypeStruct((2 * blocks, LANES), F32),
            jax.ShapeDtypeStruct((length, 1), F32),
            jax.ShapeDtypeStruct((blocks, 1, BLK), F32),
            jax.ShapeDtypeStruct((BLK, width), BF16),
        ],
        compiler_params=params(12),
        cost_estimate=pair_cost(2 * blocks, width),
        name="diagonal_pairs",
    )(counts, after, x)


def rest_pairs(counts, x, inv, inv_row, acc, sums):
    length, width = x.shape
    blocks = length // BLK

    return pl.pallas_call(
        functools.partial(rest_kernel, blocks),
        in_specs=[SMEM] + [VMEM] * 5,
        out_specs=[VMEM] * 2,
        out_shape=totals_shapes(x)[:2],
        input_output_aliases={4: 0, 5: 1},
        compiler_params=params(12),
        cost_estimate=pair_cost(blocks * blocks - 2 * blocks, width),
        name="rest_pairs",
    )(counts, x, inv, inv_row, acc, sums)


def write_payload(blocks, slot, info, x_ref, link_ref, pay_ref, acc):
    mine, theirs = info[MINE_LINK], info[THEIRS_LINK]
    shares = (mine >= 5) & (theirs >= slot - 2)

    @pl.when(jnp.logical_not(shares))
    def _():
        pay_ref[:BLK, :] = x_ref[span(link_place(info, slot - 1, blocks)), :]
        pay_ref[BLK:, :] = jnp.zeros((EXTRA, x_ref.shape[1]), BF16)

    @pl.when(shares)
    def _():
        link = link_ref[:BLK, :]
        link_inv = inverse_norm(link)
        acc[...] = jnp.zeros_like(acc)

        def add(k, sums):
            others = x_ref[span(link_place(info, k, blocks)), :]
            weight = weights(product(link, others), link_inv, to_row(inverse_norm(others)))
            acc[...] += total(weight, others)
            return sums + to_row(jnp.sum(weight, axis=1, keepdims=True))

        sums = lax.fori_loop(2, mine, add, jnp.zeros((1, BLK), F32))
        pay_ref[:BLK, :] = acc[...].astype(BF16)
        high = sums.astype(BF16)
        rest = sums - high.astype(F32)
        middle = rest.astype(BF16)
        low = (rest - middle.astype(F32)).astype(BF16)
        place = lax.broadcasted_iota(jnp.int32, (EXTRA, BLK), 0)
        parts = jnp.where(
            place == 0,
            high.astype(F32),
            jnp.where(place == 1, middle.astype(F32), jnp.where(place == 2, low.astype(F32), 0.0)),
        )
        pay_ref[BLK:, :BLK] = parts.astype(BF16)
        pay_ref[BLK:, BLK:] = jnp.zeros((EXTRA, x_ref.shape[1] - BLK), BF16)


def third_kernel(blocks, axes, counts, chip_pairs, x_ref, link_ref, pay_ref, info, acc):
    odd = lax.axis_index("sub") == 1
    base = lax.axis_index(axes) * blocks
    slots = chip_pairs.shape[1]
    listed = lax.fori_loop(
        0, slots, lambda s, n: n + jnp.where(chip_pairs[1, s] == base, 1, 0), jnp.int32(0)
    )
    told = jnp.max(link_ref[BLK:, :LANES].astype(F32)).astype(jnp.int32)
    head_theirs = jnp.where(odd, listed, told)
    head_mine = jnp.where(head_theirs > 0, counts[0], 0)
    tail_mine = counts[blocks]
    tail_theirs = counts[blocks - 1] - 1
    info[ODD] = jnp.where(odd, 1, 0)
    info[MINE_CHIP] = jnp.where(odd, head_mine, tail_mine)
    info[THEIRS_CHIP] = jnp.where(odd, head_theirs, tail_theirs)
    info[MINE_LINK] = jnp.where(odd, tail_mine, head_mine)
    info[THEIRS_LINK] = jnp.where(odd, tail_theirs, head_theirs)
    write_payload(blocks, 3, info, x_ref, link_ref, pay_ref, acc)


def third_payload(axes, counts, chip_pairs, x, link_block, after):
    length, width = x.shape
    blocks = length // BLK

    def kernel(counts, chip_pairs, x_ref, link_ref, after_ref, pay_ref, info, acc):
        third_kernel(blocks, axes, counts, chip_pairs, x_ref, link_ref, pay_ref, info, acc)

    return pl.pallas_call(
        kernel,
        in_specs=[SMEM, SMEM, VMEM, VMEM, ANY],
        out_specs=[VMEM, SMEM],
        out_shape=[
            jax.ShapeDtypeStruct((BLK + EXTRA, width), BF16),
            jax.ShapeDtypeStruct((8,), jnp.int32),
        ],
        scratch_shapes=[pltpu.VMEM((BLK, width), F32)],
        compiler_params=params(8),
        cost_estimate=pair_cost(2, width),
        name="third_payload",
    )(counts, chip_pairs, x, link_block, after)


def fourth_payload(info, x, link_block, after):
    length, width = x.shape
    blocks = length // BLK

    def kernel(info, x_ref, link_ref, after_ref, pay_ref, acc):
        write_payload(blocks, 4, info, x_ref, link_ref, pay_ref, acc)

    return pl.pallas_call(
        kernel,
        in_specs=[SMEM, VMEM, VMEM, ANY],
        out_specs=VMEM,
        out_shape=jax.ShapeDtypeStruct((BLK + EXTRA, width), BF16),
        scratch_shapes=[pltpu.VMEM((BLK, width), F32)],
        compiler_params=params(8),
        cost_estimate=pair_cost(2, width),
        name="fourth_payload",
    )(info, x, link_block, after)


def copy_out(acc_ref, out_ref, sem, r):
    return pltpu.make_async_copy(acc_ref.at[span(r), :], out_ref.at[span(r), :], sem.at[r])


def finish(acc_ref, sums_ref, out_ref, sem, r):
    acc_ref[span(r), :] = acc_ref[span(r), :] * (1.0 / to_column(load_row(sums_ref, r)))
    copy_out(acc_ref, out_ref, sem, r).start()


def each(blocks, chosen, body):
    def step(r, carry):
        @pl.when(chosen(r))
        def _():
            body(r)

        return carry

    lax.fori_loop(0, blocks, step, 0)


def add_tile(acc_ref, sums_ref, row, weight, others):
    acc_ref[span(row, 2), :] += total(weight, others)
    sums = jnp.sum(weight, axis=1, keepdims=True)
    for a in range(2):
        more = to_row(sums[a * BLK : (a + 1) * BLK])
        store_row(sums_ref, row + a, load_row(sums_ref, row + a) + more)


def chip_kernel(
    blocks,
    info,
    x_ref,
    inv_ref,
    chip_ref,
    after_ref,
    acc_in,
    sums_in,
    acc_ref,
    sums_ref,
    out_ref,
    inv_row,
    sem,
):
    odd = info[ODD] == 1
    mine, theirs = info[MINE_CHIP], info[THEIRS_CHIP]
    mine_link = info[MINE_LINK]

    def is_done(r):
        return jnp.where(odd, blocks - 1 - r, r) >= mine_link

    def column(n):
        col = jnp.where(odd, blocks - 2 - 2 * n, 2 * n)
        for b in range(2):
            inv_row[b] = to_row(inverse_norm(chip_ref[span(col + b), :]))
        theirs_ok = [jnp.where(odd, blocks - 1 - col - b, col + b) < theirs for b in range(2)]

        def tile(m, carry):
            row = jnp.where(odd, 2 * m, blocks - 2 - 2 * m)
            mine_ok = [jnp.where(odd, row + a, blocks - 1 - row - a) < mine for a in range(2)]
            others = chip_ref[span(col, 2), :]
            other_inv = jnp.concatenate([inv_row[0], inv_row[1]], axis=1)
            used = [[p & q for q in theirs_ok] for p in mine_ok]
            inner = product(x_ref[span(row, 2), :], others)
            weight = weights(inner, inv_ref[span(row, 2), :], other_inv, used)
            add_tile(acc_ref, sums_ref, row, weight, others)
            return carry

        lax.fori_loop(0, lax.div(mine + 1, 2), tile, 0)

    def columns(n, carry):
        column(n)
        return carry

    lax.fori_loop(0, lax.div(theirs + 1, 2), columns, 0)
    each(blocks, is_done, functools.partial(finish, acc_ref, sums_ref, out_ref, sem))
    each(blocks, is_done, lambda r: copy_out(acc_ref, out_ref, sem, r).wait())


def link_kernel(blocks, slots, info, x_ref, inv_ref, *refs):
    got_refs = refs[: len(slots)]
    acc_in, sums_in, out_in, acc_ref, sums_ref, out_ref, *dup_ref, side, inv_row, sem = refs[
        len(slots) :
    ]
    mine, theirs = info[MINE_LINK], info[THEIRS_LINK]
    odd = info[ODD] == 1

    uses = theirs >= slots[0]
    if slots[0] > 2:
        uses = uses & (theirs <= 4)

    @pl.when(uses)
    def _():
        for k, got_ref in enumerate(got_refs):
            block = got_ref[:BLK, :]
            side[k * BLK : (k + 1) * BLK, :] = block
            inv_row[:, k * BLK : (k + 1) * BLK] = to_row(inverse_norm(block))

        def tile(m, carry):
            row = jnp.where(odd, blocks - 2 - 2 * m, 2 * m)
            mine_ok = [jnp.where(odd, blocks - 1 - row - a, row + a) < mine for a in range(2)]
            others = side[...]
            used = [[p & (theirs >= q) for q in slots] for p in mine_ok]
            inner = product(x_ref[span(row, 2), :], others)
            weight = weights(inner, inv_ref[span(row, 2), :], inv_row[...], used)
            add_tile(acc_ref, sums_ref, row, weight, others)
            return carry

        lax.fori_loop(0, lax.div(mine + 1, 2), tile, 0)

    if slots[0] > 2:
        slot = slots[0]

        @pl.when((theirs >= 5) & (mine >= slot - 2))
        def _():
            r = link_place(info, slot - 3, blocks)
            acc_ref[span(r), :] += got_refs[0][:BLK, :].astype(F32)
            more = jnp.sum(got_refs[0][BLK:, :BLK].astype(F32), axis=0, keepdims=True)
            store_row(sums_ref, r, load_row(sums_ref, r) + more)

    def is_done(r):
        k = jnp.where(odd, blocks - 1 - r, r)
        last = jnp.where(theirs >= 5, k + 3, jnp.maximum(theirs, 2))
        now = last == slots[0]
        for slot in slots[1:]:
            now = now | (last == slot)
        return (k < mine) & now

    dup_copies = [pltpu.make_async_copy(sums_ref, ref, sem.at[blocks]) for ref in dup_ref]
    for copy in dup_copies:
        copy.start()
    each(blocks, is_done, functools.partial(finish, acc_ref, sums_ref, out_ref, sem))
    each(blocks, is_done, lambda r: copy_out(acc_ref, out_ref, sem, r).wait())
    for copy in dup_copies:
        copy.wait()


def totals_shapes(x):
    length, width = x.shape
    return [
        jax.ShapeDtypeStruct((length, width), F32),
        jax.ShapeDtypeStruct((2 * length // BLK, LANES), F32),
        jax.ShapeDtypeStruct((length, width), F32),
    ]


def chip_pairs(info, x, inv, chip_x, acc, sums, after):
    length, width = x.shape
    blocks = length // BLK
    return pl.pallas_call(
        functools.partial(chip_kernel, blocks),
        in_specs=[SMEM] + [VMEM] * 3 + [ANY] + [VMEM] * 2,
        out_specs=[VMEM, VMEM, ANY],
        out_shape=totals_shapes(x),
        scratch_shapes=[pltpu.VMEM((2, 1, BLK), F32), pltpu.SemaphoreType.DMA((blocks,))],
        input_output_aliases={5: 0, 6: 1},
        compiler_params=params(8),
        cost_estimate=pair_cost(12, width),
        name="chip_pairs",
    )(info, x, inv, chip_x, after, acc, sums)


def link_pairs(slots, info, x, inv, got, acc, sums, out, last=False):
    length, width = x.shape
    blocks = length // BLK
    n = len(slots)
    return pl.pallas_call(
        functools.partial(link_kernel, blocks, slots),
        in_specs=[SMEM] + [VMEM] * (4 + n) + [ANY],
        out_specs=[VMEM, VMEM, ANY] + [ANY] * last,
        out_shape=totals_shapes(x) + totals_shapes(x)[1:2] * last,
        scratch_shapes=[
            pltpu.VMEM((n * BLK, width), BF16),
            pltpu.VMEM((1, n * BLK), F32),
            pltpu.SemaphoreType.DMA((blocks + 1,)),
        ],
        input_output_aliases={3 + n: 0, 4 + n: 1, 5 + n: 2},
        compiler_params=params(8),
        cost_estimate=pair_cost(6 * n, width),
        name="link_pairs",
    )(info, x, inv, *got, acc, sums, out)


def per_device(embeddings, pair_blocks, pair_count):
    length, width = embeddings.shape
    blocks = length // BLK
    axes = ("rows", "sub")
    devices = lax.axis_size(axes)
    edges = [(i, i + 1) for i in range(1, devices - 1, 2)]
    edges += [(j, i) for i, j in edges]

    def over_link(array):
        return lax.ppermute(array, axes, edges)

    def over_chip(array):
        return lax.ppermute(array, "sub", [(0, 1), (1, 0)])

    x = embeddings
    counts, first = prepare(axes, pair_blocks, pair_count, x)
    one = over_link(first)
    chip_x = over_chip(x)
    chip_list = over_chip(pair_blocks)
    acc, sums, inv, inv_row, second = diagonal_pairs(counts, x, chip_list)
    two = over_link(second)
    acc, sums = rest_pairs(counts, x, inv, inv_row, acc, sums)
    third, info = third_payload(axes, counts, chip_list, x, one, sums)
    three = over_link(third)
    fourth = fourth_payload(info, x, two, third)
    four = over_link(fourth)
    acc, sums, out = chip_pairs(info, x, inv, chip_x, acc, sums, fourth)
    acc, sums, out = link_pairs((1, 2), info, x, inv, (one, two), acc, sums, out)
    acc, sums, out = link_pairs((3,), info, x, inv, (three,), acc, sums, out)
    acc, sums, out, dup = link_pairs((4,), info, x, inv, (four,), acc, sums, out, last=True)
    return dup.reshape(length), out


def solution(mesh):
    in_specs = (
        P(("groups", "rows", "sub"), None),
        P(None, ("groups", "rows", "sub")),
        P(("groups", "rows", "sub")),
    )
    out_specs = (P(("groups", "rows", "sub")), P(("groups", "rows", "sub"), None))
    return jax.shard_map(
        per_device, mesh=mesh, in_specs=in_specs, out_specs=out_specs, check_vma=False
    )
```

```python
import functools

import jax
import jax.numpy as jnp
from jax import lax
from jax.experimental import pallas as pl
from jax.experimental.pallas import tpu as pltpu
from jax.sharding import PartitionSpec as P

BLK = 256
EXTRA = 16
TEMPER = 4.0
LOG2_E = 1.4426950408889634
NEVER = 1e30
EPS = 1e-06
LANES = 128
MIB = 1024 * 1024

F32 = jnp.float32
BF16 = jnp.bfloat16

ODD, MINE_CHIP, THEIRS_CHIP, MINE_LINK, THEIRS_LINK = range(5)

VMEM = pl.BlockSpec(memory_space=pltpu.VMEM)
SMEM = pl.BlockSpec(memory_space=pltpu.SMEM)
ANY = pl.BlockSpec(memory_space=pl.ANY)
HBM = pl.BlockSpec(memory_space=pltpu.HBM)


def diagonal():
    return lax.broadcasted_iota(jnp.int32, (BLK, BLK), 0) == lax.broadcasted_iota(
        jnp.int32, (BLK, BLK), 1
    )


def to_row(column):
    return jnp.sum(jnp.where(diagonal(), column, 0.0), axis=0, keepdims=True)


def to_column(row):
    return jnp.sum(jnp.where(diagonal(), row, 0.0), axis=1, keepdims=True)


def inverse_norm(rows):
    wide = rows.astype(F32)
    return lax.rsqrt(jnp.sum(wide * wide, axis=1, keepdims=True) + EPS)


def store_row(ref, place, row):
    ref[pl.ds(2 * place, 1), :] = row[:, :LANES]
    ref[pl.ds(2 * place + 1, 1), :] = row[:, LANES:]


def load_row(ref, place):
    return jnp.concatenate([ref[pl.ds(2 * place, 1), :], ref[pl.ds(2 * place + 1, 1), :]], axis=1)


def span(place, n=1):
    return pl.ds(pl.multiple_of(place * BLK, BLK), n * BLK)


def product(rows, others):
    return lax.dot_general(rows, others, (((1,), (1,)), ((), ())), preferred_element_type=F32)


def weights(inner, row_inv, other_inv, used=None):
    scaled = inner * (TEMPER * LOG2_E * row_inv) * other_inv
    if used is None:
        return jnp.exp2(scaled - TEMPER * LOG2_E)
    return jnp.concatenate(
        [
            jnp.concatenate(
                [
                    jnp.exp2(
                        scaled[a * BLK : (a + 1) * BLK, b * BLK : (b + 1) * BLK]
                        - jnp.where(use, TEMPER * LOG2_E, NEVER)
                    )
                    for b, use in enumerate(line)
                ],
                axis=1,
            )
            for a, line in enumerate(used)
        ],
        axis=0,
    )


def total(weight, others):
    return jnp.dot(weight.astype(BF16), others, preferred_element_type=F32)


def pair_cost(pairs, width):
    return pl.CostEstimate(
        flops=pairs * BLK * BLK * width // 64, bytes_accessed=BLK * width, transcendentals=0
    )


def params(mib):
    return pltpu.CompilerParams(vmem_limit_bytes=mib * MIB)


def link_place(info, k, blocks):
    return jnp.where(info[ODD] == 1, blocks - 1 - k, k)


def prep_kernel(
    blocks, axes, pairs_hbm, live_hbm, x_hbm, counts, one_ref, two_ref, pairs, live, sem
):
    odd = lax.axis_index("sub") == 1
    base = lax.axis_index(axes) * blocks
    edges = jnp.where(odd, blocks - 1, 0), jnp.where(odd, blocks - 2, 1)
    copies = [
        pltpu.make_async_copy(pairs_hbm, pairs, sem.at[0]),
        pltpu.make_async_copy(live_hbm, live, sem.at[1]),
        pltpu.make_async_copy(x_hbm.at[span(edges[0]), :], one_ref.at[:BLK, :], sem.at[2]),
        pltpu.make_async_copy(x_hbm.at[span(edges[1]), :], two_ref, sem.at[3]),
    ]
    for copy in copies:
        copy.start()
    for r in range(blocks):
        counts[r] = 0
    copies[0].wait()
    copies[1].wait()

    def count(s, carry):
        r = pairs[0, s] - base
        counts[r] = counts[r] + 1
        return carry

    lax.fori_loop(0, live[0], count, 0)
    tail = jnp.int32(0)
    start = jnp.int32(0)
    for r in range(blocks):
        tail += jnp.where(r + counts[r] > blocks, 1, 0)
        if r:
            start = jnp.where(r - 1 + counts[r - 1] == r, r, start)
        counts[blocks + 1 + r] = start
    counts[blocks] = tail
    one_ref[BLK:, :] = jnp.full((EXTRA, one_ref.shape[1]), tail.astype(F32)).astype(BF16)
    copies[2].wait()
    copies[3].wait()


def prepare(axes, pair_blocks, pair_count, x):
    length, width = x.shape
    blocks = length // BLK
    return pl.pallas_call(
        functools.partial(prep_kernel, blocks, axes),
        in_specs=[HBM] * 3,
        out_specs=[SMEM, VMEM, VMEM],
        out_shape=[
            jax.ShapeDtypeStruct((2 * blocks + 1,), jnp.int32),
            jax.ShapeDtypeStruct((BLK + EXTRA, width), BF16),
            jax.ShapeDtypeStruct((BLK, width), BF16),
        ],
        scratch_shapes=[
            pltpu.SMEM(pair_blocks.shape, jnp.int32),
            pltpu.SMEM(pair_count.shape, jnp.int32),
            pltpu.SemaphoreType.DMA((4,)),
        ],
        compiler_params=params(56),
        cost_estimate=pl.CostEstimate(
            flops=0, bytes_accessed=4 * BLK * width, transcendentals=0
        ),
        name="prepare",
    )(pair_blocks, pair_count, x)


def same_clusters(counts, blocks, row, col):
    return [
        [counts[blocks + 1 + row + a] == counts[blocks + 1 + col + b] for b in range(2)]
        for a in range(2)
    ]


def local_tile(x_ref, inv_ref, inv_row, row, col, same):
    others = x_ref[span(col, 2), :]
    other_inv = jnp.concatenate([inv_row[col], inv_row[col + 1]], axis=1)
    inner = product(x_ref[span(row, 2), :], others)
    return weights(inner, inv_ref[span(row, 2), :], other_inv, same), others


def local_kernel(blocks, counts, after, x_ref, acc_ref, sums_ref, inv_ref, inv_row):
    half = blocks // 2

    def norms(r, carry):
        inv = inverse_norm(x_ref[span(r), :])
        inv_ref[span(r), :] = inv
        inv_row[r] = to_row(inv)
        return carry

    lax.fori_loop(0, blocks, norms, 0)

    def diagonal_tile(k, carry):
        row = 2 * k
        same = same_clusters(counts, blocks, row, row)
        weight, others = local_tile(x_ref, inv_ref, inv_row, row, row, same)
        acc_ref[span(row, 2), :] = total(weight, others)
        sums = jnp.sum(weight, axis=1, keepdims=True)
        for a in range(2):
            store_row(sums_ref, row + a, to_row(sums[a * BLK : (a + 1) * BLK]))
        return carry

    lax.fori_loop(0, half, diagonal_tile, 0)

    def other_tile(k, carry):
        row = lax.div(k, half - 1) * 2
        col = lax.rem(lax.div(k, half - 1) + 1 + lax.rem(k, half - 1), half) * 2
        same = same_clusters(counts, blocks, row, col)

        @pl.when(same[0][0] | same[0][1] | same[1][0] | same[1][1])
        def _():
            weight, others = local_tile(x_ref, inv_ref, inv_row, row, col, same)
            add_tile(acc_ref, sums_ref, row, weight, others)

        return carry

    lax.fori_loop(0, half * (half - 1), other_tile, 0)


def local_pairs(counts, x, after):
    length, width = x.shape
    blocks = length // BLK
    return pl.pallas_call(
        functools.partial(local_kernel, blocks),
        in_specs=[SMEM, SMEM, VMEM],
        out_specs=[VMEM] * 3,
        out_shape=totals_shapes(x)[:2] + [jax.ShapeDtypeStruct((length, 1), F32)],
        scratch_shapes=[pltpu.VMEM((blocks, 1, BLK), F32)],
        compiler_params=params(12),
        cost_estimate=pair_cost(blocks * blocks, width),
        name="local_pairs",
    )(counts, after, x)


def write_payload(blocks, slot, info, x_ref, link_ref, pay_ref, sums_ref, acc):
    mine, theirs = info[MINE_LINK], info[THEIRS_LINK]
    shares = (mine >= 5) & (theirs >= slot - 2)

    @pl.when(jnp.logical_not(shares))
    def _():
        pay_ref[...] = x_ref[span(link_place(info, slot - 1, blocks)), :]
        store_row(sums_ref, slot - 3, jnp.zeros((1, BLK), F32))

    @pl.when(shares)
    def _():
        link = link_ref[:BLK, :]
        link_inv = inverse_norm(link)
        acc[...] = jnp.zeros_like(acc)

        def add(k, sums):
            others = x_ref[span(link_place(info, k, blocks)), :]
            weight = weights(product(link, others), link_inv, to_row(inverse_norm(others)))
            acc[...] += total(weight, others)
            return sums + to_row(jnp.sum(weight, axis=1, keepdims=True))

        sums = lax.fori_loop(2, mine, add, jnp.zeros((1, BLK), F32))
        pay_ref[...] = acc[...].astype(BF16)
        store_row(sums_ref, slot - 3, sums)


def third_kernel(
    blocks, axes, counts, chip_pairs, x_ref, link_ref, pay_ref, sums_ref, info, acc
):
    odd = lax.axis_index("sub") == 1
    base = lax.axis_index(axes) * blocks
    slots = chip_pairs.shape[1]
    listed = lax.fori_loop(
        0, slots, lambda s, n: n + jnp.where(chip_pairs[1, s] == base, 1, 0), jnp.int32(0)
    )
    told = jnp.max(link_ref[BLK:, :LANES].astype(F32)).astype(jnp.int32)
    head_theirs = jnp.where(odd, listed, told)
    head_mine = jnp.where(head_theirs > 0, counts[0], 0)
    tail_mine = counts[blocks]
    tail_theirs = counts[blocks - 1] - 1
    info[ODD] = jnp.where(odd, 1, 0)
    info[MINE_CHIP] = jnp.where(odd, head_mine, tail_mine)
    info[THEIRS_CHIP] = jnp.where(odd, head_theirs, tail_theirs)
    info[MINE_LINK] = jnp.where(odd, tail_mine, head_mine)
    info[THEIRS_LINK] = jnp.where(odd, tail_theirs, head_theirs)
    store_row(sums_ref, 1, jnp.zeros((1, BLK), F32))
    write_payload(blocks, 3, info, x_ref, link_ref, pay_ref, sums_ref, acc)


def third_payload(axes, counts, chip_pairs, x, link_block, after):
    length, width = x.shape
    blocks = length // BLK

    def kernel(counts, chip_pairs, x_ref, link_ref, after_ref, *refs):
        third_kernel(blocks, axes, counts, chip_pairs, x_ref, link_ref, *refs)

    return pl.pallas_call(
        kernel,
        in_specs=[SMEM, SMEM, VMEM, VMEM, ANY],
        out_specs=[VMEM, VMEM, SMEM],
        out_shape=[
            jax.ShapeDtypeStruct((BLK, width), BF16),
            jax.ShapeDtypeStruct((4, LANES), F32),
            jax.ShapeDtypeStruct((8,), jnp.int32),
        ],
        scratch_shapes=[pltpu.VMEM((BLK, width), F32)],
        compiler_params=params(8),
        cost_estimate=pair_cost(2, width),
        name="third_payload",
    )(counts, chip_pairs, x, link_block, after)


def fourth_payload(info, x, link_block, sums):
    length, width = x.shape
    blocks = length // BLK

    def kernel(info, x_ref, link_ref, sums_in, pay_ref, sums_ref, acc):
        write_payload(blocks, 4, info, x_ref, link_ref, pay_ref, sums_ref, acc)

    return pl.pallas_call(
        kernel,
        in_specs=[SMEM, VMEM, VMEM, VMEM],
        out_specs=[VMEM, VMEM],
        out_shape=[
            jax.ShapeDtypeStruct((BLK, width), BF16),
            jax.ShapeDtypeStruct((4, LANES), F32),
        ],
        input_output_aliases={3: 1},
        scratch_shapes=[pltpu.VMEM((BLK, width), F32)],
        compiler_params=params(8),
        cost_estimate=pair_cost(2, width),
        name="fourth_payload",
    )(info, x, link_block, sums)


def copy_out(acc_ref, out_ref, sem, r):
    return pltpu.make_async_copy(acc_ref.at[span(r), :], out_ref.at[span(r), :], sem.at[r])


def finish(acc_ref, sums_ref, out_ref, sem, r):
    acc_ref[span(r), :] = acc_ref[span(r), :] * (1.0 / to_column(load_row(sums_ref, r)))
    copy_out(acc_ref, out_ref, sem, r).start()


def each(blocks, chosen, body):
    def step(r, carry):
        @pl.when(chosen(r))
        def _():
            body(r)

        return carry

    lax.fori_loop(0, blocks, step, 0)


def add_tile(acc_ref, sums_ref, row, weight, others, tall=2):
    acc_ref[span(row, tall), :] += total(weight, others)
    sums = jnp.sum(weight, axis=1, keepdims=True)
    for a in range(tall):
        more = to_row(sums[a * BLK : (a + 1) * BLK])
        store_row(sums_ref, row + a, load_row(sums_ref, row + a) + more)


def chip_kernel(
    blocks,
    info,
    x_ref,
    inv_ref,
    chip_ref,
    after_ref,
    acc_in,
    sums_in,
    acc_ref,
    sums_ref,
    out_ref,
    inv_row,
    sem,
):
    odd = info[ODD] == 1
    mine, theirs = info[MINE_CHIP], info[THEIRS_CHIP]
    mine_link = info[MINE_LINK]

    def is_done(r):
        return jnp.where(odd, blocks - 1 - r, r) >= mine_link

    def column(n):
        col = jnp.where(odd, blocks - 2 - 2 * n, 2 * n)
        for b in range(2):
            inv_row[b] = to_row(inverse_norm(chip_ref[span(col + b), :]))
        theirs_ok = [jnp.where(odd, blocks - 1 - col - b, col + b) < theirs for b in range(2)]

        def tile(m, carry):
            row = jnp.where(odd, 2 * m, blocks - 2 - 2 * m)
            mine_ok = [jnp.where(odd, row + a, blocks - 1 - row - a) < mine for a in range(2)]
            others = chip_ref[span(col, 2), :]
            other_inv = jnp.concatenate([inv_row[0], inv_row[1]], axis=1)
            used = [[p & q for q in theirs_ok] for p in mine_ok]
            inner = product(x_ref[span(row, 2), :], others)
            weight = weights(inner, inv_ref[span(row, 2), :], other_inv, used)
            add_tile(acc_ref, sums_ref, row, weight, others)
            return carry

        lax.fori_loop(0, lax.div(mine + 1, 2), tile, 0)

    def columns(n, carry):
        column(n)
        return carry

    lax.fori_loop(0, lax.div(theirs + 1, 2), columns, 0)
    each(blocks, is_done, functools.partial(finish, acc_ref, sums_ref, out_ref, sem))
    each(blocks, is_done, lambda r: copy_out(acc_ref, out_ref, sem, r).wait())


def link_kernel(blocks, slots, info, x_ref, inv_ref, got_sums, *refs):
    got_refs = refs[: len(slots)]
    tall = 4 if slots == (4,) else 2
    acc_in, sums_in, out_in, acc_ref, sums_ref, out_ref, *dup_ref, side, inv_row, sem = refs[
        len(slots) :
    ]
    mine, theirs = info[MINE_LINK], info[THEIRS_LINK]
    odd = info[ODD] == 1

    uses = theirs >= slots[0]
    if slots[0] > 2:
        uses = uses & (theirs <= 4)

    @pl.when(uses)
    def _():
        for k, got_ref in enumerate(got_refs):
            block = got_ref[:BLK, :]
            side[k * BLK : (k + 1) * BLK, :] = block
            inv_row[:, k * BLK : (k + 1) * BLK] = to_row(inverse_norm(block))

        def tile(m, carry):
            row = jnp.where(odd, blocks - tall - tall * m, tall * m)
            mine_ok = [jnp.where(odd, blocks - 1 - row - a, row + a) < mine for a in range(tall)]
            others = side[...]
            used = [[p & (theirs >= q) for q in slots] for p in mine_ok]
            inner = product(x_ref[span(row, tall), :], others)
            weight = weights(inner, inv_ref[span(row, tall), :], inv_row[...], used)
            add_tile(acc_ref, sums_ref, row, weight, others, tall)
            return carry

        if tall == 4:
            tile(0, 0)
        else:
            lax.fori_loop(0, lax.div(mine + 1, 2), tile, 0)

    if slots[0] > 2:
        slot = slots[0]

        @pl.when((theirs >= 5) & (mine >= slot - 2))
        def _():
            r = link_place(info, slot - 3, blocks)
            acc_ref[span(r), :] += got_refs[0][...].astype(F32)
            store_row(sums_ref, r, load_row(sums_ref, r) + load_row(got_sums, slot - 3))

    def is_done(r):
        k = jnp.where(odd, blocks - 1 - r, r)
        last = jnp.where(theirs >= 5, k + 3, jnp.maximum(theirs, 2))
        now = last == slots[0]
        for slot in slots[1:]:
            now = now | (last == slot)
        return (k < mine) & now

    dup_copies = [pltpu.make_async_copy(sums_ref, ref, sem.at[blocks]) for ref in dup_ref]
    for copy in dup_copies:
        copy.start()
    each(blocks, is_done, functools.partial(finish, acc_ref, sums_ref, out_ref, sem))
    each(blocks, is_done, lambda r: copy_out(acc_ref, out_ref, sem, r).wait())
    for copy in dup_copies:
        copy.wait()


def totals_shapes(x):
    length, width = x.shape
    return [
        jax.ShapeDtypeStruct((length, width), F32),
        jax.ShapeDtypeStruct((2 * length // BLK, LANES), F32),
        jax.ShapeDtypeStruct((length, width), F32),
    ]


def chip_pairs(info, x, inv, chip_x, acc, sums, after):
    length, width = x.shape
    blocks = length // BLK
    return pl.pallas_call(
        functools.partial(chip_kernel, blocks),
        in_specs=[SMEM] + [VMEM] * 3 + [ANY] + [VMEM] * 2,
        out_specs=[VMEM, VMEM, ANY],
        out_shape=totals_shapes(x),
        scratch_shapes=[pltpu.VMEM((2, 1, BLK), F32), pltpu.SemaphoreType.DMA((blocks,))],
        input_output_aliases={5: 0, 6: 1},
        compiler_params=params(8),
        cost_estimate=pair_cost(12, width),
        name="chip_pairs",
    )(info, x, inv, chip_x, after, acc, sums)


def link_pairs(slots, info, x, inv, got_sums, got, acc, sums, out, last=False):
    length, width = x.shape
    blocks = length // BLK
    n = len(slots)
    return pl.pallas_call(
        functools.partial(link_kernel, blocks, slots),
        in_specs=[SMEM] + [VMEM] * (5 + n) + [ANY],
        out_specs=[VMEM, VMEM, ANY] + [ANY] * last,
        out_shape=totals_shapes(x) + totals_shapes(x)[1:2] * last,
        scratch_shapes=[
            pltpu.VMEM((n * BLK, width), BF16),
            pltpu.VMEM((1, n * BLK), F32),
            pltpu.SemaphoreType.DMA((blocks + 1,)),
        ],
        input_output_aliases={4 + n: 0, 5 + n: 1, 6 + n: 2},
        compiler_params=params(8),
        cost_estimate=pair_cost(6 * n, width),
        name="link_pairs",
    )(info, x, inv, got_sums, *got, acc, sums, out)


def per_device(embeddings, pair_blocks, pair_count):
    length, width = embeddings.shape
    blocks = length // BLK
    axes = ("rows", "sub")
    devices = lax.axis_size(axes)
    edges = [(i, i + 1) for i in range(1, devices - 1, 2)]
    edges += [(j, i) for i, j in edges]

    def over_link(array):
        return lax.ppermute(array, axes, edges)

    def over_chip(array):
        return lax.ppermute(array, "sub", [(0, 1), (1, 0)])

    x = embeddings
    counts, first, second = prepare(axes, pair_blocks, pair_count, x)
    one = over_link(first)
    two = over_link(second)
    chip_x = over_chip(x)
    chip_list = over_chip(pair_blocks)
    acc, sums, inv = local_pairs(counts, x, chip_list)
    third, shared, info = third_payload(axes, counts, chip_list, x, one, sums)
    three = over_link(third)
    fourth, shared = fourth_payload(info, x, two, shared)
    four = over_link(fourth)
    got_sums = over_link(shared)
    acc, sums, out = chip_pairs(info, x, inv, chip_x, acc, sums, fourth)
    acc, sums, out = link_pairs((1, 2), info, x, inv, shared, (one, two), acc, sums, out)
    acc, sums, out = link_pairs((3,), info, x, inv, got_sums, (three,), acc, sums, out)
    acc, sums, out, dup = link_pairs(
        (4,), info, x, inv, got_sums, (four,), acc, sums, out, last=True
    )
    return dup.reshape(length), out


def solution(mesh):
    in_specs = (
        P(("groups", "rows", "sub"), None),
        P(None, ("groups", "rows", "sub")),
        P(("groups", "rows", "sub")),
    )
    out_specs = (P(("groups", "rows", "sub")), P(("groups", "rows", "sub"), None))
    return jax.shard_map(
        per_device, mesh=mesh, in_specs=in_specs, out_specs=out_specs, check_vma=False
    )
```

```python
import functools

import jax
import jax.numpy as jnp
from jax import lax
from jax.experimental import pallas as pl
from jax.experimental.pallas import tpu as pltpu
from jax.sharding import PartitionSpec as P

BLK = 256
EXTRA = 16
TEMPER = 4.0
LOG2_E = 1.4426950408889634
NEVER = 1e30
EPS = 1e-06
LANES = 128
MIB = 1024 * 1024

F32 = jnp.float32
BF16 = jnp.bfloat16

ODD, MINE_CHIP, THEIRS_CHIP, MINE_LINK, THEIRS_LINK = range(5)

VMEM = pl.BlockSpec(memory_space=pltpu.VMEM)
SMEM = pl.BlockSpec(memory_space=pltpu.SMEM)
ANY = pl.BlockSpec(memory_space=pl.ANY)
HBM = pl.BlockSpec(memory_space=pltpu.HBM)


def diagonal():
    return lax.broadcasted_iota(jnp.int32, (BLK, BLK), 0) == lax.broadcasted_iota(
        jnp.int32, (BLK, BLK), 1
    )


def to_row(column):
    return jnp.sum(jnp.where(diagonal(), column, 0.0), axis=0, keepdims=True)


def to_column(row):
    return jnp.sum(jnp.where(diagonal(), row, 0.0), axis=1, keepdims=True)


def inverse_norm(rows):
    wide = rows.astype(F32)
    return lax.rsqrt(jnp.sum(wide * wide, axis=1, keepdims=True) + EPS)


def store_row(ref, place, row):
    ref[pl.ds(2 * place, 1), :] = row[:, :LANES]
    ref[pl.ds(2 * place + 1, 1), :] = row[:, LANES:]


def load_row(ref, place):
    return jnp.concatenate([ref[pl.ds(2 * place, 1), :], ref[pl.ds(2 * place + 1, 1), :]], axis=1)


def span(place, n=1):
    return pl.ds(pl.multiple_of(place * BLK, BLK), n * BLK)


def product(rows, others):
    return lax.dot_general(rows, others, (((1,), (1,)), ((), ())), preferred_element_type=F32)


def weights(inner, row_inv, other_inv, used=None):
    scaled = inner * (TEMPER * LOG2_E * row_inv) * other_inv
    if used is None:
        return jnp.exp2(scaled - TEMPER * LOG2_E)
    return jnp.concatenate(
        [
            jnp.concatenate(
                [
                    jnp.exp2(
                        scaled[a * BLK : (a + 1) * BLK, b * BLK : (b + 1) * BLK]
                        - jnp.where(use, TEMPER * LOG2_E, NEVER)
                    )
                    for b, use in enumerate(line)
                ],
                axis=1,
            )
            for a, line in enumerate(used)
        ],
        axis=0,
    )


def total(weight, others):
    return jnp.dot(weight.astype(BF16), others, preferred_element_type=F32)


def pair_cost(pairs, width):
    return pl.CostEstimate(
        flops=pairs * 4 * BLK * BLK * width * 1,
        bytes_accessed=pairs * 2 * BLK * width,
        transcendentals=pairs * BLK * BLK,
    )


def params(mib):
    return pltpu.CompilerParams(vmem_limit_bytes=mib * MIB)


def link_place(info, k, blocks):
    return jnp.where(info[ODD] == 1, blocks - 1 - k, k)


def edge_kernel(blocks, x_hbm, one_ref, two_ref, sem):
    odd = lax.axis_index("sub") == 1
    copies = [
        pltpu.make_async_copy(
            x_hbm.at[span(jnp.where(odd, blocks - 1 - k, k)), :], ref, sem.at[k]
        )
        for k, ref in enumerate((one_ref, two_ref))
    ]
    for copy in copies:
        copy.start()
    for copy in copies:
        copy.wait()


def edge_blocks(x):
    length, width = x.shape
    return pl.pallas_call(
        functools.partial(edge_kernel, length // BLK),
        in_specs=[HBM],
        out_specs=[VMEM, VMEM],
        out_shape=[jax.ShapeDtypeStruct((BLK, width), BF16)] * 2,
        scratch_shapes=[pltpu.SemaphoreType.DMA((2,))],
        compiler_params=params(56),
        cost_estimate=pl.CostEstimate(
            flops=0, bytes_accessed=4 * BLK * width, transcendentals=0
        ),
        name="edge_blocks",
    )(x)


def same_clusters(counts, blocks, row, col):
    return [
        [counts[blocks + 1 + row + a] == counts[blocks + 1 + col + b] for b in range(2)]
        for a in range(2)
    ]


def local_tile(x_ref, inv_ref, inv_row, row, col, same):
    others = x_ref[span(col, 2), :]
    other_inv = jnp.concatenate([inv_row[col], inv_row[col + 1]], axis=1)
    inner = product(x_ref[span(row, 2), :], others)
    return weights(inner, inv_ref[span(row, 2), :], other_inv, same), others


def count_pairs(blocks, axes, pairs, live, counts):
    base = lax.axis_index(axes) * blocks
    for r in range(blocks):
        counts[r] = 0

    def count(s, carry):
        r = pairs[0, s] - base
        counts[r] = counts[r] + 1
        return carry

    lax.fori_loop(0, live[0], count, 0)
    tail = jnp.int32(0)
    start = jnp.int32(0)
    for r in range(blocks):
        tail += jnp.where(r + counts[r] > blocks, 1, 0)
        if r:
            start = jnp.where(r - 1 + counts[r - 1] == r, r, start)
        counts[blocks + 1 + r] = start
    counts[blocks] = tail


def local_kernel(
    blocks, axes, pairs, live, after, x_ref, acc_ref, sums_ref, inv_ref, counts, inv_row
):
    half = blocks // 2
    count_pairs(blocks, axes, pairs, live, counts)

    def norms(r, carry):
        inv = inverse_norm(x_ref[span(r), :])
        inv_ref[span(r), :] = inv
        inv_row[r] = to_row(inv)
        return carry

    lax.fori_loop(0, blocks, norms, 0)

    def diagonal_tile(k, carry):
        row = 2 * k
        same = same_clusters(counts, blocks, row, row)
        weight, others = local_tile(x_ref, inv_ref, inv_row, row, row, same)
        acc_ref[span(row, 2), :] = total(weight, others)
        sums = jnp.sum(weight, axis=1, keepdims=True)
        for a in range(2):
            store_row(sums_ref, row + a, to_row(sums[a * BLK : (a + 1) * BLK]))
        return carry

    lax.fori_loop(0, half, diagonal_tile, 0)

    def other_tile(k, carry):
        row = lax.div(k, half - 1) * 2
        col = lax.rem(lax.div(k, half - 1) + 1 + lax.rem(k, half - 1), half) * 2
        same = same_clusters(counts, blocks, row, col)

        @pl.when(same[0][0] | same[0][1] | same[1][0] | same[1][1])
        def _():
            weight, others = local_tile(x_ref, inv_ref, inv_row, row, col, same)
            add_tile(acc_ref, sums_ref, row, weight, others)

        return carry

    lax.fori_loop(0, half * (half - 1), other_tile, 0)


def local_pairs(axes, pairs, live, x, after):
    length, width = x.shape
    blocks = length // BLK
    return pl.pallas_call(
        functools.partial(local_kernel, blocks, axes),
        in_specs=[SMEM, SMEM, SMEM, VMEM],
        out_specs=[VMEM] * 3 + [SMEM],
        out_shape=totals_shapes(x)[:2]
        + [
            jax.ShapeDtypeStruct((length, 1), F32),
            jax.ShapeDtypeStruct((2 * blocks + 1,), jnp.int32),
        ],
        scratch_shapes=[pltpu.VMEM((blocks, 1, BLK), F32)],
        compiler_params=params(12),
        cost_estimate=pair_cost(blocks * blocks, width),
        name="local_pairs",
    )(pairs, live, after, x)


def write_payload(blocks, slot, info, x_ref, link_ref, pay_ref, sums_ref, acc):
    mine, theirs = info[MINE_LINK], info[THEIRS_LINK]
    shares = (mine >= 5) & (theirs >= slot - 2)

    @pl.when(jnp.logical_not(shares))
    def _():
        pay_ref[:BLK, :] = x_ref[span(link_place(info, slot - 1, blocks)), :]
        store_row(sums_ref, slot - 3, jnp.zeros((1, BLK), F32))

    @pl.when(shares)
    def _():
        link = link_ref[:BLK, :]
        link_inv = inverse_norm(link)
        acc[...] = jnp.zeros_like(acc)

        def add(k, sums):
            others = x_ref[span(link_place(info, k, blocks)), :]
            weight = weights(product(link, others), link_inv, to_row(inverse_norm(others)))
            acc[...] += total(weight, others)
            return sums + to_row(jnp.sum(weight, axis=1, keepdims=True))

        sums = lax.fori_loop(2, mine, add, jnp.zeros((1, BLK), F32))
        pay_ref[:BLK, :] = acc[...].astype(BF16)
        store_row(sums_ref, slot - 3, sums)


def third_kernel(
    blocks, axes, counts, before, x_ref, link_ref, pay_ref, sums_ref, info, acc
):
    odd = lax.axis_index("sub") == 1
    base = lax.axis_index(axes) * blocks
    slots = before.shape[1]
    head_theirs = lax.fori_loop(
        0, slots, lambda s, n: n + jnp.where(before[1, s] == base, 1, 0), jnp.int32(0)
    )
    head_theirs = jnp.where(base > 0, head_theirs, 0)
    head_mine = jnp.where(head_theirs > 0, counts[0], 0)
    tail_mine = counts[blocks]
    tail_theirs = counts[blocks - 1] - 1
    info[ODD] = jnp.where(odd, 1, 0)
    info[MINE_CHIP] = jnp.where(odd, head_mine, tail_mine)
    info[THEIRS_CHIP] = jnp.where(odd, head_theirs, tail_theirs)
    info[MINE_LINK] = jnp.where(odd, tail_mine, head_mine)
    info[THEIRS_LINK] = jnp.where(odd, tail_theirs, head_theirs)
    store_row(sums_ref, 1, jnp.zeros((1, BLK), F32))
    write_payload(blocks, 3, info, x_ref, link_ref, pay_ref, sums_ref, acc)


def third_payload(axes, counts, before, x, link_block, after):
    length, width = x.shape
    blocks = length // BLK

    def kernel(counts, before, x_ref, link_ref, after_ref, *refs):
        third_kernel(blocks, axes, counts, before, x_ref, link_ref, *refs)

    return pl.pallas_call(
        kernel,
        in_specs=[SMEM, SMEM, VMEM, VMEM, ANY],
        out_specs=[VMEM, VMEM, SMEM],
        out_shape=[
            jax.ShapeDtypeStruct((BLK, width), BF16),
            jax.ShapeDtypeStruct((4, LANES), F32),
            jax.ShapeDtypeStruct((8,), jnp.int32),
        ],
        scratch_shapes=[pltpu.VMEM((BLK, width), F32)],
        compiler_params=params(8),
        cost_estimate=pair_cost(2, width),
        name="third_payload",
    )(counts, before, x, link_block, after)


def fourth_kernel(blocks, info, x_ref, link_ref, after_ref, sums_in, pay_ref, sums_ref, acc):
    write_payload(blocks, 4, info, x_ref, link_ref, pay_ref, sums_ref, acc)
    place = lax.broadcasted_iota(jnp.int32, (EXTRA, BLK), 0)
    parts = jnp.zeros((EXTRA, BLK), F32)
    for slot in range(2):
        rest = load_row(sums_ref, slot)
        for k in range(3):
            part = rest.astype(BF16).astype(F32)
            parts = jnp.where(place == 3 * slot + k, part, parts)
            rest = rest - part
    pay_ref[BLK:, :BLK] = parts.astype(BF16)
    pay_ref[BLK:, BLK:] = jnp.zeros((EXTRA, x_ref.shape[1] - BLK), BF16)


def fourth_payload(info, x, link_block, after, sums):
    length, width = x.shape
    return pl.pallas_call(
        functools.partial(fourth_kernel, length // BLK),
        in_specs=[SMEM, VMEM, VMEM, ANY, VMEM],
        out_specs=[VMEM, VMEM],
        out_shape=[
            jax.ShapeDtypeStruct((BLK + EXTRA, width), BF16),
            jax.ShapeDtypeStruct((4, LANES), F32),
        ],
        input_output_aliases={4: 1},
        scratch_shapes=[pltpu.VMEM((BLK, width), F32)],
        compiler_params=params(8),
        cost_estimate=pair_cost(2, width),
        name="fourth_payload",
    )(info, x, link_block, after, sums)[0]


def copy_out(acc_ref, out_ref, sem, r):
    return pltpu.make_async_copy(acc_ref.at[span(r), :], out_ref.at[span(r), :], sem.at[r])


def finish(acc_ref, sums_ref, out_ref, sem, r):
    acc_ref[span(r), :] = acc_ref[span(r), :] * (1.0 / to_column(load_row(sums_ref, r)))
    copy_out(acc_ref, out_ref, sem, r).start()


def each(blocks, chosen, body):
    def step(r, carry):
        @pl.when(chosen(r))
        def _():
            body(r)

        return carry

    lax.fori_loop(0, blocks, step, 0)


def add_tile(acc_ref, sums_ref, row, weight, others, tall=2):
    acc_ref[span(row, tall), :] += total(weight, others)
    sums = jnp.sum(weight, axis=1, keepdims=True)
    for a in range(tall):
        more = to_row(sums[a * BLK : (a + 1) * BLK])
        store_row(sums_ref, row + a, load_row(sums_ref, row + a) + more)


def chip_kernel(
    blocks,
    info,
    x_ref,
    inv_ref,
    chip_ref,
    acc_in,
    sums_in,
    acc_ref,
    sums_ref,
    out_ref,
    inv_row,
    sem,
):
    odd = info[ODD] == 1
    mine, theirs = info[MINE_CHIP], info[THEIRS_CHIP]
    mine_link = info[MINE_LINK]

    def is_done(r):
        return jnp.where(odd, blocks - 1 - r, r) >= mine_link

    def column(n):
        col = jnp.where(odd, blocks - 2 - 2 * n, 2 * n)
        for b in range(2):
            inv_row[b] = to_row(inverse_norm(chip_ref[span(col + b), :]))
        theirs_ok = [jnp.where(odd, blocks - 1 - col - b, col + b) < theirs for b in range(2)]

        def tile(m, carry):
            row = jnp.where(odd, 2 * m, blocks - 2 - 2 * m)
            mine_ok = [jnp.where(odd, row + a, blocks - 1 - row - a) < mine for a in range(2)]
            others = chip_ref[span(col, 2), :]
            other_inv = jnp.concatenate([inv_row[0], inv_row[1]], axis=1)
            used = [[p & q for q in theirs_ok] for p in mine_ok]
            inner = product(x_ref[span(row, 2), :], others)
            weight = weights(inner, inv_ref[span(row, 2), :], other_inv, used)
            add_tile(acc_ref, sums_ref, row, weight, others)
            return carry

        lax.fori_loop(0, lax.div(mine + 1, 2), tile, 0)

    def columns(n, carry):
        column(n)
        return carry

    lax.fori_loop(0, lax.div(theirs + 1, 2), columns, 0)
    each(blocks, is_done, functools.partial(finish, acc_ref, sums_ref, out_ref, sem))
    each(blocks, is_done, lambda r: copy_out(acc_ref, out_ref, sem, r).wait())


def link_kernel(blocks, slots, info, x_ref, inv_ref, *refs):
    got_refs = refs[: len(slots)]
    tall = 4 if slots == (4,) else 2
    acc_in, sums_in, out_in, acc_ref, sums_ref, out_ref, *dup_ref, side, inv_row, sem = refs[
        len(slots) :
    ]
    mine, theirs = info[MINE_LINK], info[THEIRS_LINK]
    odd = info[ODD] == 1

    uses = theirs >= slots[0]
    if slots[0] > 2:
        uses = uses & (theirs <= 4)

    @pl.when(uses)
    def _():
        for k, got_ref in enumerate(got_refs):
            block = got_ref[:BLK, :]
            side[k * BLK : (k + 1) * BLK, :] = block
            inv_row[:, k * BLK : (k + 1) * BLK] = to_row(inverse_norm(block))

        def tile(m, carry):
            row = jnp.where(odd, blocks - tall - tall * m, tall * m)
            mine_ok = [jnp.where(odd, blocks - 1 - row - a, row + a) < mine for a in range(tall)]
            others = side[...]
            used = [[p & (theirs >= q) for q in slots] for p in mine_ok]
            inner = product(x_ref[span(row, tall), :], others)
            weight = weights(inner, inv_ref[span(row, tall), :], inv_row[...], used)
            add_tile(acc_ref, sums_ref, row, weight, others, tall)
            return carry

        if tall == 4:
            tile(0, 0)
        else:
            lax.fori_loop(0, lax.div(mine + 1, 2), tile, 0)

    if slots[0] > 2:
        slot = slots[0]

        @pl.when((theirs >= 5) & (mine >= slot - 2))
        def _():
            r = link_place(info, slot - 3, blocks)
            acc_ref[span(r), :] += got_refs[0][:BLK, :].astype(F32)

    if slots[0] == 4:
        for k in range(2):

            @pl.when((theirs >= 5) & (mine > k))
            def _(k=k):
                r = link_place(info, k, blocks)
                parts = got_refs[0][BLK:, :BLK].astype(F32)
                more = jnp.sum(parts[3 * k : 3 * k + 3], axis=0, keepdims=True)
                store_row(sums_ref, r, load_row(sums_ref, r) + more)

    def is_done(r):
        last = jnp.clip(theirs, 2, 4)
        now = last == slots[0]
        for slot in slots[1:]:
            now = now | (last == slot)
        return (jnp.where(odd, blocks - 1 - r, r) < mine) & now

    dup_copies = [pltpu.make_async_copy(sums_ref, ref, sem.at[blocks]) for ref in dup_ref]
    for copy in dup_copies:
        copy.start()
    each(blocks, is_done, functools.partial(finish, acc_ref, sums_ref, out_ref, sem))
    each(blocks, is_done, lambda r: copy_out(acc_ref, out_ref, sem, r).wait())
    for copy in dup_copies:
        copy.wait()


def totals_shapes(x):
    length, width = x.shape
    return [
        jax.ShapeDtypeStruct((length, width), F32),
        jax.ShapeDtypeStruct((2 * length // BLK, LANES), F32),
        jax.ShapeDtypeStruct((length, width), F32),
    ]


def chip_pairs(info, x, inv, chip_x, acc, sums):
    length, width = x.shape
    blocks = length // BLK
    return pl.pallas_call(
        functools.partial(chip_kernel, blocks),
        in_specs=[SMEM] + [VMEM] * 5,
        out_specs=[VMEM, VMEM, ANY],
        out_shape=totals_shapes(x),
        scratch_shapes=[pltpu.VMEM((2, 1, BLK), F32), pltpu.SemaphoreType.DMA((blocks,))],
        input_output_aliases={4: 0, 5: 1},
        compiler_params=params(8),
        cost_estimate=pair_cost(12, width),
        name="chip_pairs",
    )(info, x, inv, chip_x, acc, sums)


def link_pairs(slots, info, x, inv, got, acc, sums, out, last=False):
    length, width = x.shape
    blocks = length // BLK
    n = len(slots)
    return pl.pallas_call(
        functools.partial(link_kernel, blocks, slots),
        in_specs=[SMEM] + [VMEM] * (4 + n) + [ANY],
        out_specs=[VMEM, VMEM, ANY] + [ANY] * last,
        out_shape=totals_shapes(x) + totals_shapes(x)[1:2] * last,
        scratch_shapes=[
            pltpu.VMEM((n * BLK, width), BF16),
            pltpu.VMEM((1, n * BLK), F32),
            pltpu.SemaphoreType.DMA((blocks + 1,)),
        ],
        input_output_aliases={3 + n: 0, 4 + n: 1, 5 + n: 2},
        compiler_params=params(8),
        cost_estimate=pair_cost(6 * n, width),
        name="link_pairs",
    )(info, x, inv, *got, acc, sums, out)


def per_device(embeddings, pair_blocks, pair_count):
    length, width = embeddings.shape
    blocks = length // BLK
    axes = ("rows", "sub")
    devices = lax.axis_size(axes)
    edges = [(i, i + 1) for i in range(1, devices - 1, 2)]
    edges += [(j, i) for i, j in edges]

    def over_link(array):
        return lax.ppermute(array, axes, edges)

    x = embeddings
    first, second = edge_blocks(x)
    one = over_link(first)
    chip_x = lax.ppermute(x, "sub", [(0, 1), (1, 0)])
    pair_list, second = lax.optimization_barrier((pair_blocks, second))
    before = lax.ppermute(pair_list, axes, [(i, i + 1) for i in range(devices - 1)])
    two = over_link(second)
    acc, sums, inv, counts = local_pairs(axes, pair_blocks, pair_count, x, before)
    third, shared, info = third_payload(axes, counts, before, x, one, sums)
    three = over_link(third)
    acc, sums, out = chip_pairs(info, x, inv, chip_x, acc, sums)
    fourth = fourth_payload(info, x, two, sums, shared)
    four = over_link(fourth)
    acc, sums, out = link_pairs((1, 2), info, x, inv, (one, two), acc, sums, out)
    acc, sums, out = link_pairs((3,), info, x, inv, (three,), acc, sums, out)
    acc, sums, out, dup = link_pairs((4,), info, x, inv, (four,), acc, sums, out, last=True)
    return dup.reshape(length), out


def solution(mesh):
    in_specs = (
        P(("groups", "rows", "sub"), None),
        P(None, ("groups", "rows", "sub")),
        P(("groups", "rows", "sub")),
    )
    out_specs = (P(("groups", "rows", "sub")), P(("groups", "rows", "sub"), None))
    return jax.shard_map(
        per_device, mesh=mesh, in_specs=in_specs, out_specs=out_specs, check_vma=False
    )
```

```python
import functools

import jax
import jax.numpy as jnp
from jax import lax
from jax.experimental import pallas as pl
from jax.experimental.pallas import tpu as pltpu
from jax.sharding import PartitionSpec as P

BLK = 256
EXTRA = 16
TEMPER = 4.0
LOG2_E = 1.4426950408889634
NEVER = 1e30
EPS = 1e-06
LANES = 128
MIB = 1024 * 1024

F32 = jnp.float32
BF16 = jnp.bfloat16

ODD, MINE_CHIP, THEIRS_CHIP, MINE_LINK, THEIRS_LINK = range(5)

VMEM = pl.BlockSpec(memory_space=pltpu.VMEM)
SMEM = pl.BlockSpec(memory_space=pltpu.SMEM)
ANY = pl.BlockSpec(memory_space=pl.ANY)
HBM = pl.BlockSpec(memory_space=pltpu.HBM)


def diagonal():
    return lax.broadcasted_iota(jnp.int32, (BLK, BLK), 0) == lax.broadcasted_iota(
        jnp.int32, (BLK, BLK), 1
    )


def to_row(column):
    return jnp.sum(jnp.where(diagonal(), column, 0.0), axis=0, keepdims=True)


def to_column(row):
    return jnp.sum(jnp.where(diagonal(), row, 0.0), axis=1, keepdims=True)


def inverse_norm(rows):
    wide = rows.astype(F32)
    return lax.rsqrt(jnp.sum(wide * wide, axis=1, keepdims=True) + EPS)


def store_row(ref, place, row):
    ref[pl.ds(2 * place, 1), :] = row[:, :LANES]
    ref[pl.ds(2 * place + 1, 1), :] = row[:, LANES:]


def load_row(ref, place):
    return jnp.concatenate([ref[pl.ds(2 * place, 1), :], ref[pl.ds(2 * place + 1, 1), :]], axis=1)


def span(place, n=1):
    return pl.ds(pl.multiple_of(place * BLK, BLK), n * BLK)


def product(rows, others):
    return lax.dot_general(rows, others, (((1,), (1,)), ((), ())), preferred_element_type=F32)


def weights(inner, row_inv, other_inv, used=None):
    scaled = inner * (TEMPER * LOG2_E * row_inv) * other_inv
    if used is None:
        return jnp.exp2(scaled - TEMPER * LOG2_E)
    return jnp.concatenate(
        [
            jnp.concatenate(
                [
                    jnp.exp2(
                        scaled[a * BLK : (a + 1) * BLK, b * BLK : (b + 1) * BLK]
                        - jnp.where(use, TEMPER * LOG2_E, NEVER)
                    )
                    for b, use in enumerate(line)
                ],
                axis=1,
            )
            for a, line in enumerate(used)
        ],
        axis=0,
    )


def total(weight, others):
    return jnp.dot(weight.astype(BF16), others, preferred_element_type=F32)


def pair_cost(pairs, width):
    return pl.CostEstimate(
        flops=pairs * 4 * BLK * BLK * width,
        bytes_accessed=pairs * 2 * BLK * width,
        transcendentals=pairs * BLK * BLK,
    )


def params(mib):
    return pltpu.CompilerParams(vmem_limit_bytes=mib * MIB)


def link_place(info, k, blocks):
    return jnp.where(info[ODD] == 1, blocks - 1 - k, k)


def prep_kernel(blocks, axes, pairs_hbm, live_hbm, x_hbm, counts, pay_ref, pairs, live, sem):
    odd = lax.axis_index("sub") == 1
    base = lax.axis_index(axes) * blocks
    edge = jnp.where(odd, blocks - 1, 0)
    copies = [
        pltpu.make_async_copy(pairs_hbm, pairs, sem.at[0]),
        pltpu.make_async_copy(live_hbm, live, sem.at[1]),
        pltpu.make_async_copy(x_hbm.at[span(edge), :], pay_ref.at[:BLK, :], sem.at[2]),
    ]
    for copy in copies:
        copy.start()
    for r in range(blocks):
        counts[r] = 0
    copies[0].wait()
    copies[1].wait()

    def count(s, carry):
        r = pairs[0, s] - base
        counts[r] = counts[r] + 1
        return carry

    lax.fori_loop(0, live[0], count, 0)
    tail = jnp.int32(0)
    start = jnp.int32(0)
    for r in range(blocks):
        tail += jnp.where(r + counts[r] > blocks, 1, 0)
        if r:
            start = jnp.where(r - 1 + counts[r - 1] == r, r, start)
        counts[blocks + 1 + r] = start
    counts[blocks] = tail
    pay_ref[BLK:, :] = jnp.full((EXTRA, pay_ref.shape[1]), tail.astype(F32)).astype(BF16)
    copies[2].wait()


def prepare(axes, pair_blocks, pair_count, x):
    length, width = x.shape
    blocks = length // BLK
    return pl.pallas_call(
        functools.partial(prep_kernel, blocks, axes),
        in_specs=[HBM] * 3,
        out_specs=[SMEM, VMEM],
        out_shape=[
            jax.ShapeDtypeStruct((2 * blocks + 1,), jnp.int32),
            jax.ShapeDtypeStruct((BLK + EXTRA, width), BF16),
        ],
        scratch_shapes=[
            pltpu.SMEM(pair_blocks.shape, jnp.int32),
            pltpu.SMEM(pair_count.shape, jnp.int32),
            pltpu.SemaphoreType.DMA((3,)),
        ],
        compiler_params=params(56),
        cost_estimate=pl.CostEstimate(
            flops=0, bytes_accessed=4 * BLK * width, transcendentals=0
        ),
        name="prepare",
    )(pair_blocks, pair_count, x)


def same_clusters(counts, blocks, row, col):
    return [
        [counts[blocks + 1 + row + a] == counts[blocks + 1 + col + b] for b in range(2)]
        for a in range(2)
    ]


def local_tile(x_ref, inv_ref, inv_row, row, col, same):
    others = x_ref[span(col, 2), :]
    other_inv = jnp.concatenate([inv_row[col], inv_row[col + 1]], axis=1)
    inner = product(x_ref[span(row, 2), :], others)
    return weights(inner, inv_ref[span(row, 2), :], other_inv, same), others


def diagonal_kernel(blocks, counts, after, x_ref, acc_ref, sums_ref, inv_ref, inv_row, pay_ref):
    odd = lax.axis_index("sub") == 1
    pay_ref[...] = x_ref[span(jnp.where(odd, blocks - 2, 1)), :]

    def norms(r, carry):
        inv = inverse_norm(x_ref[span(r), :])
        inv_ref[span(r), :] = inv
        inv_row[r] = to_row(inv)
        return carry

    lax.fori_loop(0, blocks, norms, 0)

    def visit(k, carry):
        row = 2 * k
        same = same_clusters(counts, blocks, row, row)
        weight, others = local_tile(x_ref, inv_ref, inv_row, row, row, same)
        acc_ref[span(row, 2), :] = total(weight, others)
        sums = jnp.sum(weight, axis=0, keepdims=True)
        for a in range(2):
            store_row(sums_ref, row + a, sums[:, a * BLK : (a + 1) * BLK])
        return carry

    lax.fori_loop(0, blocks // 2, visit, 0)


def rest_kernel(blocks, counts, x_ref, inv_ref, inv_row, acc_in, sums_in, acc_ref, sums_ref):
    half = blocks // 2

    def visit(k, carry):
        row = 2 * lax.div(k, half)
        col = 2 * lax.rem(k, half)
        same = same_clusters(counts, blocks, row, col)

        @pl.when((row < col) & (same[0][0] | same[0][1] | same[1][0] | same[1][1]))
        def _():
            weight, others = local_tile(x_ref, inv_ref, inv_row, row, col, same)
            add_tile(acc_ref, sums_ref, row, weight, others)
            sums = jnp.sum(weight, axis=0, keepdims=True)
            acc_ref[span(col, 2), :] += lax.dot_general(
                weight.astype(BF16),
                x_ref[span(row, 2), :],
                (((0,), (0,)), ((), ())),
                preferred_element_type=F32,
            )
            for b in range(2):
                more = sums[:, b * BLK : (b + 1) * BLK]
                store_row(sums_ref, col + b, load_row(sums_ref, col + b) + more)

        return carry

    lax.fori_loop(0, half * half, visit, 0)


def diagonal_pairs(counts, x, after):
    length, width = x.shape
    blocks = length // BLK
    return pl.pallas_call(
        functools.partial(diagonal_kernel, blocks),
        in_specs=[SMEM, SMEM, VMEM],
        out_specs=[VMEM] * 5,
        out_shape=[
            jax.ShapeDtypeStruct((length, width), F32),
            jax.ShapeDtypeStruct((2 * blocks, LANES), F32),
            jax.ShapeDtypeStruct((length, 1), F32),
            jax.ShapeDtypeStruct((blocks, 1, BLK), F32),
            jax.ShapeDtypeStruct((BLK, width), BF16),
        ],
        compiler_params=params(12),
        cost_estimate=pair_cost(2 * blocks, width),
        name="diagonal_pairs",
    )(counts, after, x)


def rest_pairs(counts, x, inv, inv_row, acc, sums):
    length, width = x.shape
    blocks = length // BLK

    return pl.pallas_call(
        functools.partial(rest_kernel, blocks),
        in_specs=[SMEM] + [VMEM] * 5,
        out_specs=[VMEM] * 2,
        out_shape=totals_shapes(x)[:2],
        input_output_aliases={4: 0, 5: 1},
        compiler_params=params(12),
        cost_estimate=pair_cost(blocks * blocks - 2 * blocks, width),
        name="rest_pairs",
    )(counts, x, inv, inv_row, acc, sums)


def write_payload(blocks, slot, info, x_ref, link_ref, pay_ref, sums_ref, acc):
    mine, theirs = info[MINE_LINK], info[THEIRS_LINK]
    shares = (mine >= 5) & (theirs >= slot - 2)

    @pl.when(jnp.logical_not(shares))
    def _():
        pay_ref[:BLK, :] = x_ref[span(link_place(info, slot - 1, blocks)), :]
        store_row(sums_ref, slot - 3, jnp.zeros((1, BLK), F32))

    @pl.when(shares)
    def _():
        link = link_ref[:BLK, :]
        link_inv = inverse_norm(link)
        acc[...] = jnp.zeros_like(acc)

        def add(k, sums):
            others = x_ref[span(link_place(info, k, blocks)), :]
            weight = weights(product(link, others), link_inv, to_row(inverse_norm(others)))
            acc[...] += total(weight, others)
            return sums + to_row(jnp.sum(weight, axis=1, keepdims=True))

        sums = lax.fori_loop(2, mine, add, jnp.zeros((1, BLK), F32))
        pay_ref[:BLK, :] = acc[...].astype(BF16)
        store_row(sums_ref, slot - 3, sums)


def third_kernel(
    blocks, axes, counts, chip_pairs, x_ref, link_ref, pay_ref, sums_ref, info, acc
):
    odd = lax.axis_index("sub") == 1
    base = lax.axis_index(axes) * blocks
    slots = chip_pairs.shape[1]
    listed = lax.fori_loop(
        0, slots, lambda s, n: n + jnp.where(chip_pairs[1, s] == base, 1, 0), jnp.int32(0)
    )
    told = jnp.max(link_ref[BLK:, :LANES].astype(F32)).astype(jnp.int32)
    head_theirs = jnp.where(odd, listed, told)
    head_mine = jnp.where(head_theirs > 0, counts[0], 0)
    tail_mine = counts[blocks]
    tail_theirs = counts[blocks - 1] - 1
    info[ODD] = jnp.where(odd, 1, 0)
    info[MINE_CHIP] = jnp.where(odd, head_mine, tail_mine)
    info[THEIRS_CHIP] = jnp.where(odd, head_theirs, tail_theirs)
    info[MINE_LINK] = jnp.where(odd, tail_mine, head_mine)
    info[THEIRS_LINK] = jnp.where(odd, tail_theirs, head_theirs)
    store_row(sums_ref, 1, jnp.zeros((1, BLK), F32))
    write_payload(blocks, 3, info, x_ref, link_ref, pay_ref, sums_ref, acc)


def third_payload(axes, counts, chip_list, x, link_block, after):
    length, width = x.shape
    blocks = length // BLK

    def kernel(counts, chip_list, x_ref, link_ref, after_ref, *refs):
        third_kernel(blocks, axes, counts, chip_list, x_ref, link_ref, *refs)

    return pl.pallas_call(
        kernel,
        in_specs=[SMEM, SMEM, VMEM, VMEM, ANY],
        out_specs=[VMEM, VMEM, SMEM],
        out_shape=[
            jax.ShapeDtypeStruct((BLK, width), BF16),
            jax.ShapeDtypeStruct((4, LANES), F32),
            jax.ShapeDtypeStruct((8,), jnp.int32),
        ],
        scratch_shapes=[pltpu.VMEM((BLK, width), F32)],
        compiler_params=params(8),
        cost_estimate=pair_cost(2, width),
        name="third_payload",
    )(counts, chip_list, x, link_block, after)


def fourth_kernel(blocks, info, x_ref, link_ref, after_ref, sums_in, pay_ref, sums_ref, acc):
    write_payload(blocks, 4, info, x_ref, link_ref, pay_ref, sums_ref, acc)
    place = lax.broadcasted_iota(jnp.int32, (EXTRA, BLK), 0)
    parts = jnp.zeros((EXTRA, BLK), F32)
    for slot in range(2):
        rest = load_row(sums_ref, slot)
        for k in range(3):
            part = rest.astype(BF16).astype(F32)
            parts = jnp.where(place == 3 * slot + k, part, parts)
            rest = rest - part
    pay_ref[BLK:, :BLK] = parts.astype(BF16)
    pay_ref[BLK:, BLK:] = jnp.zeros((EXTRA, x_ref.shape[1] - BLK), BF16)


def fourth_payload(info, x, link_block, after, sums):
    length, width = x.shape
    return pl.pallas_call(
        functools.partial(fourth_kernel, length // BLK),
        in_specs=[SMEM, VMEM, VMEM, ANY, VMEM],
        out_specs=[VMEM, VMEM],
        out_shape=[
            jax.ShapeDtypeStruct((BLK + EXTRA, width), BF16),
            jax.ShapeDtypeStruct((4, LANES), F32),
        ],
        input_output_aliases={4: 1},
        scratch_shapes=[pltpu.VMEM((BLK, width), F32)],
        compiler_params=params(8),
        cost_estimate=pair_cost(2, width),
        name="fourth_payload",
    )(info, x, link_block, after, sums)[0]


def copy_out(acc_ref, out_ref, sem, r):
    return pltpu.make_async_copy(acc_ref.at[span(r), :], out_ref.at[span(r), :], sem.at[r])


def finish(acc_ref, sums_ref, out_ref, sem, r):
    acc_ref[span(r), :] = acc_ref[span(r), :] * (1.0 / to_column(load_row(sums_ref, r)))
    copy_out(acc_ref, out_ref, sem, r).start()


def each(blocks, chosen, body):
    def step(r, carry):
        @pl.when(chosen(r))
        def _():
            body(r)

        return carry

    lax.fori_loop(0, blocks, step, 0)


def add_tile(acc_ref, sums_ref, row, weight, others, tall=2):
    acc_ref[span(row, tall), :] += total(weight, others)
    sums = jnp.sum(weight, axis=1, keepdims=True)
    for a in range(tall):
        more = to_row(sums[a * BLK : (a + 1) * BLK])
        store_row(sums_ref, row + a, load_row(sums_ref, row + a) + more)


def chip_kernel(
    blocks,
    info,
    x_ref,
    inv_ref,
    chip_ref,
    acc_in,
    sums_in,
    acc_ref,
    sums_ref,
    out_ref,
    inv_row,
    sem,
):
    odd = info[ODD] == 1
    mine, theirs = info[MINE_CHIP], info[THEIRS_CHIP]
    mine_link = info[MINE_LINK]

    def is_done(r):
        return jnp.where(odd, blocks - 1 - r, r) >= mine_link

    def column(n):
        col = jnp.where(odd, blocks - 2 - 2 * n, 2 * n)
        for b in range(2):
            inv_row[b] = to_row(inverse_norm(chip_ref[span(col + b), :]))
        theirs_ok = [jnp.where(odd, blocks - 1 - col - b, col + b) < theirs for b in range(2)]

        def tile(m, carry):
            row = jnp.where(odd, 2 * m, blocks - 2 - 2 * m)
            mine_ok = [jnp.where(odd, row + a, blocks - 1 - row - a) < mine for a in range(2)]
            others = chip_ref[span(col, 2), :]
            other_inv = jnp.concatenate([inv_row[0], inv_row[1]], axis=1)
            used = [[p & q for q in theirs_ok] for p in mine_ok]
            inner = product(x_ref[span(row, 2), :], others)
            weight = weights(inner, inv_ref[span(row, 2), :], other_inv, used)
            add_tile(acc_ref, sums_ref, row, weight, others)
            return carry

        lax.fori_loop(0, lax.div(mine + 1, 2), tile, 0)

    def columns(n, carry):
        column(n)
        return carry

    lax.fori_loop(0, lax.div(theirs + 1, 2), columns, 0)
    each(blocks, is_done, functools.partial(finish, acc_ref, sums_ref, out_ref, sem))
    each(blocks, is_done, lambda r: copy_out(acc_ref, out_ref, sem, r).wait())


def link_kernel(blocks, slots, info, x_ref, inv_ref, *refs):
    got_refs = refs[: len(slots)]
    tall = 4 if slots == (4,) else 2
    acc_in, sums_in, out_in, acc_ref, sums_ref, out_ref, *dup_ref, side, inv_row, sem = refs[
        len(slots) :
    ]
    mine, theirs = info[MINE_LINK], info[THEIRS_LINK]
    odd = info[ODD] == 1

    uses = theirs >= slots[0]
    if slots[0] > 2:
        uses = uses & (theirs <= 4)

    @pl.when(uses)
    def _():
        for k, got_ref in enumerate(got_refs):
            block = got_ref[:BLK, :]
            side[k * BLK : (k + 1) * BLK, :] = block
            inv_row[:, k * BLK : (k + 1) * BLK] = to_row(inverse_norm(block))

        def tile(m, carry):
            row = jnp.where(odd, blocks - tall - tall * m, tall * m)
            mine_ok = [jnp.where(odd, blocks - 1 - row - a, row + a) < mine for a in range(tall)]
            others = side[...]
            used = [[p & (theirs >= q) for q in slots] for p in mine_ok]
            inner = product(x_ref[span(row, tall), :], others)
            weight = weights(inner, inv_ref[span(row, tall), :], inv_row[...], used)
            add_tile(acc_ref, sums_ref, row, weight, others, tall)
            return carry

        if tall == 4:
            tile(0, 0)
        else:
            lax.fori_loop(0, lax.div(mine + 1, 2), tile, 0)

    if slots[0] > 2:
        slot = slots[0]

        @pl.when((theirs >= 5) & (mine >= slot - 2))
        def _():
            r = link_place(info, slot - 3, blocks)
            acc_ref[span(r), :] += got_refs[0][:BLK, :].astype(F32)

    if slots[0] == 4:
        for k in range(2):

            @pl.when((theirs >= 5) & (mine > k))
            def _(k=k):
                r = link_place(info, k, blocks)
                parts = got_refs[0][BLK:, :BLK].astype(F32)
                more = jnp.sum(parts[3 * k : 3 * k + 3], axis=0, keepdims=True)
                store_row(sums_ref, r, load_row(sums_ref, r) + more)

    def is_done(r):
        last = jnp.clip(theirs, 2, 4)
        now = last == slots[0]
        for slot in slots[1:]:
            now = now | (last == slot)
        return (jnp.where(odd, blocks - 1 - r, r) < mine) & now

    dup_copies = [pltpu.make_async_copy(sums_ref, ref, sem.at[blocks]) for ref in dup_ref]
    for copy in dup_copies:
        copy.start()
    each(blocks, is_done, functools.partial(finish, acc_ref, sums_ref, out_ref, sem))
    each(blocks, is_done, lambda r: copy_out(acc_ref, out_ref, sem, r).wait())
    for copy in dup_copies:
        copy.wait()


def totals_shapes(x):
    length, width = x.shape
    return [
        jax.ShapeDtypeStruct((length, width), F32),
        jax.ShapeDtypeStruct((2 * length // BLK, LANES), F32),
        jax.ShapeDtypeStruct((length, width), F32),
    ]


def chip_pairs(info, x, inv, chip_x, acc, sums):
    length, width = x.shape
    blocks = length // BLK
    return pl.pallas_call(
        functools.partial(chip_kernel, blocks),
        in_specs=[SMEM] + [VMEM] * 5,
        out_specs=[VMEM, VMEM, ANY],
        out_shape=totals_shapes(x),
        scratch_shapes=[pltpu.VMEM((2, 1, BLK), F32), pltpu.SemaphoreType.DMA((blocks,))],
        input_output_aliases={4: 0, 5: 1},
        compiler_params=params(8),
        cost_estimate=pair_cost(12, width),
        name="chip_pairs",
    )(info, x, inv, chip_x, acc, sums)


def link_pairs(slots, info, x, inv, got, acc, sums, out, last=False):
    length, width = x.shape
    blocks = length // BLK
    n = len(slots)
    return pl.pallas_call(
        functools.partial(link_kernel, blocks, slots),
        in_specs=[SMEM] + [VMEM] * (4 + n) + [ANY],
        out_specs=[VMEM, VMEM, ANY] + [ANY] * last,
        out_shape=totals_shapes(x) + totals_shapes(x)[1:2] * last,
        scratch_shapes=[
            pltpu.VMEM((n * BLK, width), BF16),
            pltpu.VMEM((1, n * BLK), F32),
            pltpu.SemaphoreType.DMA((blocks + 1,)),
        ],
        input_output_aliases={3 + n: 0, 4 + n: 1, 5 + n: 2},
        compiler_params=params(8),
        cost_estimate=pair_cost(6 * n, width),
        name="link_pairs",
    )(info, x, inv, *got, acc, sums, out)


def per_device(embeddings, pair_blocks, pair_count):
    length, width = embeddings.shape
    blocks = length // BLK
    axes = ("rows", "sub")
    devices = lax.axis_size(axes)
    edges = [(i, i + 1) for i in range(1, devices - 1, 2)]
    edges += [(j, i) for i, j in edges]

    def over_link(array):
        return lax.ppermute(array, axes, edges)

    def over_chip(array):
        return lax.ppermute(array, "sub", [(0, 1), (1, 0)])

    x = embeddings
    counts, first = prepare(axes, pair_blocks, pair_count, x)
    one = over_link(first)
    chip_x = over_chip(x)
    chip_list = over_chip(pair_blocks)
    acc, sums, inv, inv_row, second = diagonal_pairs(counts, x, chip_list)
    two = over_link(second)
    acc, sums = rest_pairs(counts, x, inv, inv_row, acc, sums)
    third, shared, info = third_payload(axes, counts, chip_list, x, one, sums)
    three = over_link(third)
    acc, sums, out = chip_pairs(info, x, inv, chip_x, acc, sums)
    fourth = fourth_payload(info, x, two, sums, shared)
    four = over_link(fourth)
    acc, sums, out = link_pairs((1, 2), info, x, inv, (one, two), acc, sums, out)
    acc, sums, out = link_pairs((3,), info, x, inv, (three,), acc, sums, out)
    acc, sums, out, dup = link_pairs((4,), info, x, inv, (four,), acc, sums, out, last=True)
    return dup.reshape(length), out


def solution(mesh):
    in_specs = (
        P(("groups", "rows", "sub"), None),
        P(None, ("groups", "rows", "sub")),
        P(("groups", "rows", "sub")),
    )
    out_specs = (P(("groups", "rows", "sub")), P(("groups", "rows", "sub"), None))
    return jax.shard_map(
        per_device, mesh=mesh, in_specs=in_specs, out_specs=out_specs, check_vma=False
    )
```

```python
import functools

import jax
import jax.numpy as jnp
from jax import lax
from jax.experimental import pallas as pl
from jax.experimental.pallas import tpu as pltpu
from jax.sharding import PartitionSpec as P

BLK = 256
EXTRA = 16
TEMPER = 4.0
LOG2_E = 1.4426950408889634
NEVER = 1e30
EPS = 1e-06
LANES = 128
MIB = 1024 * 1024

F32 = jnp.float32
BF16 = jnp.bfloat16

ODD, MINE_CHIP, THEIRS_CHIP, MINE_LINK, THEIRS_LINK = range(5)

VMEM = pl.BlockSpec(memory_space=pltpu.VMEM)
SMEM = pl.BlockSpec(memory_space=pltpu.SMEM)
ANY = pl.BlockSpec(memory_space=pl.ANY)
HBM = pl.BlockSpec(memory_space=pltpu.HBM)


def diagonal():
    return lax.broadcasted_iota(jnp.int32, (BLK, BLK), 0) == lax.broadcasted_iota(
        jnp.int32, (BLK, BLK), 1
    )


def to_row(column):
    return jnp.sum(jnp.where(diagonal(), column, 0.0), axis=0, keepdims=True)


def to_column(row):
    return jnp.sum(jnp.where(diagonal(), row, 0.0), axis=1, keepdims=True)


def inverse_norm(rows):
    wide = rows.astype(F32)
    return lax.rsqrt(jnp.sum(wide * wide, axis=1, keepdims=True) + EPS)


def store_row(ref, place, row):
    ref[pl.ds(2 * place, 1), :] = row[:, :LANES]
    ref[pl.ds(2 * place + 1, 1), :] = row[:, LANES:]


def load_row(ref, place):
    return jnp.concatenate([ref[pl.ds(2 * place, 1), :], ref[pl.ds(2 * place + 1, 1), :]], axis=1)


def span(place, n=1):
    return pl.ds(pl.multiple_of(place * BLK, BLK), n * BLK)


def product(rows, others):
    return lax.dot_general(rows, others, (((1,), (1,)), ((), ())), preferred_element_type=F32)


def weights(inner, row_inv, other_inv, used=None):
    scaled = inner * (TEMPER * LOG2_E * row_inv) * other_inv
    if used is None:
        return jnp.exp2(scaled - TEMPER * LOG2_E)
    return jnp.concatenate(
        [
            jnp.concatenate(
                [
                    jnp.exp2(
                        scaled[a * BLK : (a + 1) * BLK, b * BLK : (b + 1) * BLK]
                        - jnp.where(use, TEMPER * LOG2_E, NEVER)
                    )
                    for b, use in enumerate(line)
                ],
                axis=1,
            )
            for a, line in enumerate(used)
        ],
        axis=0,
    )


def total(weight, others):
    return jnp.dot(weight.astype(BF16), others, preferred_element_type=F32)


def pair_cost(pairs, width):
    return pl.CostEstimate(
        flops=pairs * 4 * BLK * BLK * width,
        bytes_accessed=pairs * 2 * BLK * width,
        transcendentals=pairs * BLK * BLK,
    )


def params(mib):
    return pltpu.CompilerParams(vmem_limit_bytes=mib * MIB)


def link_place(info, k, blocks):
    return jnp.where(info[ODD] == 1, blocks - 1 - k, k)


def prep_kernel(blocks, axes, pairs_hbm, x_hbm, counts, pay_ref, pairs, sem):
    odd = lax.axis_index("sub") == 1
    base = lax.axis_index(axes) * blocks
    edge = jnp.where(odd, blocks - 1, 0)
    copies = [
        pltpu.make_async_copy(pairs_hbm, pairs, sem.at[0]),
        pltpu.make_async_copy(x_hbm.at[span(edge), :], pay_ref.at[:BLK, :], sem.at[1]),
    ]
    for copy in copies:
        copy.start()
    for r in range(blocks):
        counts[r] = 1
    copies[0].wait()

    def count(s, carry):
        r = pairs[0, s] - base
        counts[r] = counts[r] + jnp.where(pairs[1, s] > pairs[0, s], 1, 0)
        return carry

    lax.fori_loop(0, pairs.shape[1], count, 0)
    tail = jnp.int32(0)
    start = jnp.int32(0)
    for r in range(blocks):
        tail += jnp.where(r + counts[r] > blocks, 1, 0)
        if r:
            start = jnp.where(r - 1 + counts[r - 1] == r, r, start)
        counts[blocks + 1 + r] = start
    counts[blocks] = tail
    pay_ref[BLK:, :] = jnp.full((EXTRA, pay_ref.shape[1]), tail.astype(F32)).astype(BF16)
    copies[1].wait()


def prepare(axes, pair_blocks, x):
    length, width = x.shape
    blocks = length // BLK
    return pl.pallas_call(
        functools.partial(prep_kernel, blocks, axes),
        in_specs=[HBM] * 2,
        out_specs=[SMEM, VMEM],
        out_shape=[
            jax.ShapeDtypeStruct((2 * blocks + 1,), jnp.int32),
            jax.ShapeDtypeStruct((BLK + EXTRA, width), BF16),
        ],
        scratch_shapes=[
            pltpu.SMEM(pair_blocks.shape, jnp.int32),
            pltpu.SemaphoreType.DMA((2,)),
        ],
        compiler_params=params(56),
        cost_estimate=pl.CostEstimate(
            flops=0, bytes_accessed=4 * BLK * width, transcendentals=0
        ),
        name="prepare",
    )(pair_blocks, x)


def same_clusters(counts, blocks, row, col):
    return [
        [counts[blocks + 1 + row + a] == counts[blocks + 1 + col + b] for b in range(2)]
        for a in range(2)
    ]


def local_tile(x_ref, inv_ref, inv_row, row, col, same):
    others = x_ref[span(col, 2), :]
    other_inv = jnp.concatenate([inv_row[col], inv_row[col + 1]], axis=1)
    inner = product(x_ref[span(row, 2), :], others)
    return weights(inner, inv_ref[span(row, 2), :], other_inv, same), others


def diagonal_kernel(blocks, counts, after, x_ref, acc_ref, sums_ref, inv_ref, inv_row, pay_ref):
    odd = lax.axis_index("sub") == 1
    pay_ref[...] = x_ref[span(jnp.where(odd, blocks - 2, 1)), :]

    def norms(r, carry):
        inv = inverse_norm(x_ref[span(r), :])
        inv_ref[span(r), :] = inv
        inv_row[r] = to_row(inv)
        return carry

    lax.fori_loop(0, blocks, norms, 0)

    def visit(k, carry):
        row = 2 * k
        same = same_clusters(counts, blocks, row, row)
        weight, others = local_tile(x_ref, inv_ref, inv_row, row, row, same)
        acc_ref[span(row, 2), :] = total(weight, others)
        sums = jnp.sum(weight, axis=0, keepdims=True)
        for a in range(2):
            store_row(sums_ref, row + a, sums[:, a * BLK : (a + 1) * BLK])
        return carry

    lax.fori_loop(0, blocks // 2, visit, 0)


def rest_kernel(blocks, counts, x_ref, inv_ref, inv_row, acc_in, sums_in, acc_ref, sums_ref):
    half = blocks // 2

    def visit(k, carry):
        row = 2 * lax.div(k, half)
        col = 2 * lax.rem(k, half)
        same = same_clusters(counts, blocks, row, col)

        @pl.when((row < col) & (same[0][0] | same[0][1] | same[1][0] | same[1][1]))
        def _():
            weight, others = local_tile(x_ref, inv_ref, inv_row, row, col, same)
            add_tile(acc_ref, sums_ref, row, weight, others)
            sums = jnp.sum(weight, axis=0, keepdims=True)
            acc_ref[span(col, 2), :] += lax.dot_general(
                weight.astype(BF16),
                x_ref[span(row, 2), :],
                (((0,), (0,)), ((), ())),
                preferred_element_type=F32,
            )
            for b in range(2):
                more = sums[:, b * BLK : (b + 1) * BLK]
                store_row(sums_ref, col + b, load_row(sums_ref, col + b) + more)

        return carry

    lax.fori_loop(0, half * half, visit, 0)


def diagonal_pairs(counts, x, after):
    length, width = x.shape
    blocks = length // BLK
    return pl.pallas_call(
        functools.partial(diagonal_kernel, blocks),
        in_specs=[SMEM, SMEM, VMEM],
        out_specs=[VMEM] * 5,
        out_shape=[
            jax.ShapeDtypeStruct((length, width), F32),
            jax.ShapeDtypeStruct((2 * blocks, LANES), F32),
            jax.ShapeDtypeStruct((length, 1), F32),
            jax.ShapeDtypeStruct((blocks, 1, BLK), F32),
            jax.ShapeDtypeStruct((BLK, width), BF16),
        ],
        compiler_params=params(12),
        cost_estimate=pair_cost(2 * blocks, width),
        name="diagonal_pairs",
    )(counts, after, x)


def rest_pairs(counts, x, inv, inv_row, acc, sums):
    length, width = x.shape
    blocks = length // BLK

    return pl.pallas_call(
        functools.partial(rest_kernel, blocks),
        in_specs=[SMEM] + [VMEM] * 5,
        out_specs=[VMEM] * 2,
        out_shape=totals_shapes(x)[:2],
        input_output_aliases={4: 0, 5: 1},
        compiler_params=params(12),
        cost_estimate=pair_cost(blocks * blocks - 2 * blocks, width),
        name="rest_pairs",
    )(counts, x, inv, inv_row, acc, sums)


def write_payload(blocks, slot, info, x_ref, link_ref, pay_ref, sums_ref, acc):
    mine, theirs = info[MINE_LINK], info[THEIRS_LINK]
    shares = (mine >= 5) & (theirs >= slot - 2)

    @pl.when(jnp.logical_not(shares))
    def _():
        pay_ref[:BLK, :] = x_ref[span(link_place(info, slot - 1, blocks)), :]
        store_row(sums_ref, slot - 3, jnp.zeros((1, BLK), F32))

    @pl.when(shares)
    def _():
        link = link_ref[:BLK, :]
        link_inv = inverse_norm(link)
        acc[...] = jnp.zeros_like(acc)

        def add(k, sums):
            others = x_ref[span(link_place(info, k, blocks)), :]
            weight = weights(product(link, others), link_inv, to_row(inverse_norm(others)))
            acc[...] += total(weight, others)
            return sums + to_row(jnp.sum(weight, axis=1, keepdims=True))

        sums = lax.fori_loop(2, mine, add, jnp.zeros((1, BLK), F32))
        pay_ref[:BLK, :] = acc[...].astype(BF16)
        store_row(sums_ref, slot - 3, sums)


def third_kernel(
    blocks, axes, counts, chip_pairs, x_ref, link_ref, pay_ref, sums_ref, info, acc
):
    odd = lax.axis_index("sub") == 1
    base = lax.axis_index(axes) * blocks
    slots = chip_pairs.shape[1]
    listed = lax.fori_loop(
        0, slots, lambda s, n: n + jnp.where(chip_pairs[1, s] == base, 1, 0), jnp.int32(0)
    )
    told = jnp.max(link_ref[BLK:, :LANES].astype(F32)).astype(jnp.int32)
    head_theirs = jnp.where(odd, listed, told)
    head_mine = jnp.where(head_theirs > 0, counts[0], 0)
    tail_mine = counts[blocks]
    tail_theirs = counts[blocks - 1] - 1
    info[ODD] = jnp.where(odd, 1, 0)
    info[MINE_CHIP] = jnp.where(odd, head_mine, tail_mine)
    info[THEIRS_CHIP] = jnp.where(odd, head_theirs, tail_theirs)
    info[MINE_LINK] = jnp.where(odd, tail_mine, head_mine)
    info[THEIRS_LINK] = jnp.where(odd, tail_theirs, head_theirs)
    store_row(sums_ref, 1, jnp.zeros((1, BLK), F32))
    write_payload(blocks, 3, info, x_ref, link_ref, pay_ref, sums_ref, acc)


def third_payload(axes, counts, chip_list, x, link_block, after):
    length, width = x.shape
    blocks = length // BLK

    def kernel(counts, chip_list, x_ref, link_ref, after_ref, *refs):
        third_kernel(blocks, axes, counts, chip_list, x_ref, link_ref, *refs)

    return pl.pallas_call(
        kernel,
        in_specs=[SMEM, SMEM, VMEM, VMEM, ANY],
        out_specs=[VMEM, VMEM, SMEM],
        out_shape=[
            jax.ShapeDtypeStruct((BLK, width), BF16),
            jax.ShapeDtypeStruct((4, LANES), F32),
            jax.ShapeDtypeStruct((8,), jnp.int32),
        ],
        scratch_shapes=[pltpu.VMEM((BLK, width), F32)],
        compiler_params=params(8),
        cost_estimate=pair_cost(2, width),
        name="third_payload",
    )(counts, chip_list, x, link_block, after)


def fourth_kernel(blocks, info, x_ref, link_ref, after_ref, sums_in, pay_ref, sums_ref, acc):
    write_payload(blocks, 4, info, x_ref, link_ref, pay_ref, sums_ref, acc)
    place = lax.broadcasted_iota(jnp.int32, (EXTRA, BLK), 0)
    parts = jnp.zeros((EXTRA, BLK), F32)
    for slot in range(2):
        rest = load_row(sums_ref, slot)
        for k in range(3):
            part = rest.astype(BF16).astype(F32)
            parts = jnp.where(place == 3 * slot + k, part, parts)
            rest = rest - part
    pay_ref[BLK:, :BLK] = parts.astype(BF16)
    pay_ref[BLK:, BLK:] = jnp.zeros((EXTRA, x_ref.shape[1] - BLK), BF16)


def fourth_payload(info, x, link_block, after, sums):
    length, width = x.shape
    return pl.pallas_call(
        functools.partial(fourth_kernel, length // BLK),
        in_specs=[SMEM, VMEM, VMEM, ANY, VMEM],
        out_specs=[VMEM, VMEM],
        out_shape=[
            jax.ShapeDtypeStruct((BLK + EXTRA, width), BF16),
            jax.ShapeDtypeStruct((4, LANES), F32),
        ],
        input_output_aliases={4: 1},
        scratch_shapes=[pltpu.VMEM((BLK, width), F32)],
        compiler_params=params(8),
        cost_estimate=pair_cost(2, width),
        name="fourth_payload",
    )(info, x, link_block, after, sums)[0]


def copy_out(acc_ref, out_ref, sem, r):
    return pltpu.make_async_copy(acc_ref.at[span(r), :], out_ref.at[span(r), :], sem.at[r])


def finish(acc_ref, sums_ref, out_ref, sem, r):
    acc_ref[span(r), :] = acc_ref[span(r), :] * (1.0 / to_column(load_row(sums_ref, r)))
    copy_out(acc_ref, out_ref, sem, r).start()


def each(blocks, chosen, body):
    def step(r, carry):
        @pl.when(chosen(r))
        def _():
            body(r)

        return carry

    lax.fori_loop(0, blocks, step, 0)


def add_tile(acc_ref, sums_ref, row, weight, others, tall=2):
    acc_ref[span(row, tall), :] += total(weight, others)
    sums = jnp.sum(weight, axis=1, keepdims=True)
    for a in range(tall):
        more = to_row(sums[a * BLK : (a + 1) * BLK])
        store_row(sums_ref, row + a, load_row(sums_ref, row + a) + more)


def chip_kernel(
    blocks,
    info,
    x_ref,
    inv_ref,
    chip_ref,
    acc_in,
    sums_in,
    acc_ref,
    sums_ref,
    out_ref,
    inv_row,
    sem,
):
    odd = info[ODD] == 1
    mine, theirs = info[MINE_CHIP], info[THEIRS_CHIP]
    mine_link = info[MINE_LINK]

    def is_done(r):
        return jnp.where(odd, blocks - 1 - r, r) >= mine_link

    def column(n):
        col = jnp.where(odd, blocks - 2 - 2 * n, 2 * n)
        for b in range(2):
            inv_row[b] = to_row(inverse_norm(chip_ref[span(col + b), :]))
        theirs_ok = [jnp.where(odd, blocks - 1 - col - b, col + b) < theirs for b in range(2)]

        def tile(m, carry):
            row = jnp.where(odd, 2 * m, blocks - 2 - 2 * m)
            mine_ok = [jnp.where(odd, row + a, blocks - 1 - row - a) < mine for a in range(2)]
            others = chip_ref[span(col, 2), :]
            other_inv = jnp.concatenate([inv_row[0], inv_row[1]], axis=1)
            used = [[p & q for q in theirs_ok] for p in mine_ok]
            inner = product(x_ref[span(row, 2), :], others)
            weight = weights(inner, inv_ref[span(row, 2), :], other_inv, used)
            add_tile(acc_ref, sums_ref, row, weight, others)
            return carry

        lax.fori_loop(0, lax.div(mine + 1, 2), tile, 0)

    def columns(n, carry):
        column(n)
        return carry

    lax.fori_loop(0, lax.div(theirs + 1, 2), columns, 0)
    each(blocks, is_done, functools.partial(finish, acc_ref, sums_ref, out_ref, sem))
    each(blocks, is_done, lambda r: copy_out(acc_ref, out_ref, sem, r).wait())


def link_kernel(blocks, slots, info, x_ref, inv_ref, *refs):
    got_refs = refs[: len(slots)]
    acc_in, sums_in, out_in, acc_ref, sums_ref, out_ref, side, inv_row, sem = refs[len(slots) :]
    mine, theirs = info[MINE_LINK], info[THEIRS_LINK]
    odd = info[ODD] == 1

    uses = theirs >= slots[0]
    if slots[0] > 2:
        uses = uses & (theirs <= 4)

    @pl.when(uses)
    def _():
        for k, got_ref in enumerate(got_refs):
            block = got_ref[:BLK, :]
            side[k * BLK : (k + 1) * BLK, :] = block
            inv_row[:, k * BLK : (k + 1) * BLK] = to_row(inverse_norm(block))

        def tile(m, carry):
            row = jnp.where(odd, blocks - 2 - 2 * m, 2 * m)
            mine_ok = [jnp.where(odd, blocks - 1 - row - a, row + a) < mine for a in range(2)]
            others = side[...]
            used = [[p & (theirs >= q) for q in slots] for p in mine_ok]
            inner = product(x_ref[span(row, 2), :], others)
            weight = weights(inner, inv_ref[span(row, 2), :], inv_row[...], used)
            add_tile(acc_ref, sums_ref, row, weight, others)
            return carry

        lax.fori_loop(0, lax.div(mine + 1, 2), tile, 0)

    if slots[0] > 2:

        @pl.when((theirs >= 5) & (mine >= 1))
        def _():
            r = link_place(info, 0, blocks)
            acc_ref[span(r), :] += got_refs[0][...].astype(F32)

    def is_done(r):
        last = jnp.clip(theirs, 2, 4)
        now = last == slots[0]
        for slot in slots[1:]:
            now = now | (last == slot)
        return (jnp.where(odd, blocks - 1 - r, r) < mine) & now

    each(blocks, is_done, functools.partial(finish, acc_ref, sums_ref, out_ref, sem))
    each(blocks, is_done, lambda r: copy_out(acc_ref, out_ref, sem, r).wait())


def last_kernel(
    blocks, info, x_ref, inv_ref, got_ref, acc_in, sums_in, out_in, acc_ref, sums_ref, out_ref, dup_ref, inv_row, sem
):
    mine, theirs = info[MINE_LINK], info[THEIRS_LINK]

    def shift(r):
        return pltpu.make_async_copy(acc_ref.at[span(r), :], out_ref.at[span(r), :], sem.at[r])

    def close(r, more, term):
        sums = load_row(sums_ref, r) + more
        store_row(sums_ref, r, sums)
        acc_ref[span(r), :] = (acc_ref[span(r), :] + term) * (1.0 / to_column(sums))
        shift(r).start()

    @pl.when(theirs == 4)
    def _():
        inv_row[...] = to_row(inverse_norm(got_ref[:BLK, :]))

        def visit(k, carry):
            r = link_place(info, k, blocks)
            others = got_ref[:BLK, :]
            inner = product(x_ref[span(r), :], others)
            weight = weights(inner, inv_ref[span(r), :], inv_row[...])
            more = to_row(jnp.sum(weight, axis=1, keepdims=True))
            close(r, more, total(weight, others))
            return carry

        lax.fori_loop(0, mine, visit, 0)

    for k in range(2):

        @pl.when((theirs >= 5) & (mine > k))
        def _(k=k):
            parts = got_ref[BLK:, :BLK].astype(F32)
            more = jnp.sum(parts[3 * k : 3 * k + 3], axis=0, keepdims=True)
            term = got_ref[:BLK, :].astype(F32) if k else 0.0
            close(link_place(info, k, blocks), more, term)

    dup_copy = pltpu.make_async_copy(sums_ref, dup_ref, sem.at[blocks])
    dup_copy.start()

    def wait(k, carry):
        @pl.when(theirs >= 4)
        def _():
            shift(link_place(info, k, blocks)).wait()

        return carry

    lax.fori_loop(0, mine, wait, 0)
    dup_copy.wait()


def totals_shapes(x):
    length, width = x.shape
    return [
        jax.ShapeDtypeStruct((length, width), F32),
        jax.ShapeDtypeStruct((2 * length // BLK, LANES), F32),
        jax.ShapeDtypeStruct((length, width), F32),
    ]


def chip_pairs(info, x, inv, chip_x, acc, sums):
    length, width = x.shape
    blocks = length // BLK
    return pl.pallas_call(
        functools.partial(chip_kernel, blocks),
        in_specs=[SMEM] + [VMEM] * 5,
        out_specs=[VMEM, VMEM, ANY],
        out_shape=totals_shapes(x),
        scratch_shapes=[pltpu.VMEM((2, 1, BLK), F32), pltpu.SemaphoreType.DMA((blocks,))],
        input_output_aliases={4: 0, 5: 1},
        compiler_params=params(8),
        cost_estimate=pair_cost(12, width),
        name="chip_pairs",
    )(info, x, inv, chip_x, acc, sums)


def link_pairs(slots, info, x, inv, got, acc, sums, out):
    length, width = x.shape
    blocks = length // BLK
    n = len(slots)
    return pl.pallas_call(
        functools.partial(link_kernel, blocks, slots),
        in_specs=[SMEM] + [VMEM] * (4 + n) + [ANY],
        out_specs=[VMEM, VMEM, ANY],
        out_shape=totals_shapes(x),
        scratch_shapes=[
            pltpu.VMEM((n * BLK, width), BF16),
            pltpu.VMEM((1, n * BLK), F32),
            pltpu.SemaphoreType.DMA((blocks,)),
        ],
        input_output_aliases={3 + n: 0, 4 + n: 1, 5 + n: 2},
        compiler_params=params(8),
        cost_estimate=pair_cost(6 * n, width),
        name="link_pairs",
    )(info, x, inv, *got, acc, sums, out)


def last_pairs(info, x, inv, got, acc, sums, out):
    length, width = x.shape
    blocks = length // BLK
    return pl.pallas_call(
        functools.partial(last_kernel, blocks),
        in_specs=[SMEM] + [VMEM] * 5 + [ANY],
        out_specs=[VMEM, VMEM, ANY, ANY],
        out_shape=totals_shapes(x) + totals_shapes(x)[1:2],
        scratch_shapes=[pltpu.VMEM((1, BLK), F32), pltpu.SemaphoreType.DMA((blocks + 1,))],
        input_output_aliases={4: 0, 5: 1, 6: 2},
        compiler_params=params(8),
        cost_estimate=pair_cost(3, width),
        name="last_pairs",
    )(info, x, inv, got, acc, sums, out)[2:]


def per_device(embeddings, pair_blocks, pair_count):
    length, width = embeddings.shape
    blocks = length // BLK
    axes = ("rows", "sub")
    devices = lax.axis_size(axes)
    edges = [(i, i + 1) for i in range(1, devices - 1, 2)]
    edges += [(j, i) for i, j in edges]

    def over_link(array):
        return lax.ppermute(array, axes, edges)

    def over_chip(array):
        return lax.ppermute(array, "sub", [(0, 1), (1, 0)])

    x = embeddings
    counts, first = prepare(axes, pair_blocks, x)
    one = over_link(first)
    chip_x = over_chip(x)
    chip_list = over_chip(pair_blocks)
    acc, sums, inv, inv_row, second = diagonal_pairs(counts, x, chip_list)
    two = over_link(second)
    acc, sums = rest_pairs(counts, x, inv, inv_row, acc, sums)
    third, shared, info = third_payload(axes, counts, chip_list, x, one, sums)
    three = over_link(third)
    acc, sums, out = chip_pairs(info, x, inv, chip_x, acc, sums)
    fourth = fourth_payload(info, x, two, sums, shared)
    four = over_link(fourth)
    acc, sums, out = link_pairs((1, 2), info, x, inv, (one, two), acc, sums, out)
    acc, sums, out = link_pairs((3,), info, x, inv, (three,), acc, sums, out)
    out, dup = last_pairs(info, x, inv, four, acc, sums, out)
    return dup.reshape(length), out


def solution(mesh):
    in_specs = (
        P(("groups", "rows", "sub"), None),
        P(None, ("groups", "rows", "sub")),
        P(("groups", "rows", "sub")),
    )
    out_specs = (P(("groups", "rows", "sub")), P(("groups", "rows", "sub"), None))
    return jax.shard_map(
        per_device, mesh=mesh, in_specs=in_specs, out_specs=out_specs, check_vma=False
    )
```

```python
import functools

import jax
import jax.numpy as jnp
from jax import lax
from jax.experimental import pallas as pl
from jax.experimental.pallas import tpu as pltpu
from jax.sharding import PartitionSpec as P

BLK = 256
EXTRA = 16
TEMPER = 4.0
LOG2_E = 1.4426950408889634
NEVER = 1e30
EPS = 1e-06
LANES = 128
MIB = 1024 * 1024

F32 = jnp.float32
BF16 = jnp.bfloat16

ODD, MINE_CHIP, THEIRS_CHIP, MINE_LINK, THEIRS_LINK = range(5)

VMEM = pl.BlockSpec(memory_space=pltpu.VMEM)
SMEM = pl.BlockSpec(memory_space=pltpu.SMEM)
ANY = pl.BlockSpec(memory_space=pl.ANY)
HBM = pl.BlockSpec(memory_space=pltpu.HBM)


def diagonal():
    return lax.broadcasted_iota(jnp.int32, (BLK, BLK), 0) == lax.broadcasted_iota(
        jnp.int32, (BLK, BLK), 1
    )


def to_row(column):
    return jnp.sum(jnp.where(diagonal(), column, 0.0), axis=0, keepdims=True)


def to_column(row):
    return jnp.sum(jnp.where(diagonal(), row, 0.0), axis=1, keepdims=True)


def inverse_norm(rows):
    wide = rows.astype(F32)
    return lax.rsqrt(jnp.sum(wide * wide, axis=1, keepdims=True) + EPS)


def store_row(ref, place, row):
    ref[pl.ds(2 * place, 1), :] = row[:, :LANES]
    ref[pl.ds(2 * place + 1, 1), :] = row[:, LANES:]


def load_row(ref, place):
    return jnp.concatenate([ref[pl.ds(2 * place, 1), :], ref[pl.ds(2 * place + 1, 1), :]], axis=1)


def span(place, n=1):
    return pl.ds(pl.multiple_of(place * BLK, BLK), n * BLK)


def product(rows, others):
    return lax.dot_general(rows, others, (((1,), (1,)), ((), ())), preferred_element_type=F32)


def weights(inner, row_inv, other_inv, used=None):
    scaled = inner * (TEMPER * LOG2_E * row_inv) * other_inv
    if used is None:
        return jnp.exp2(scaled - TEMPER * LOG2_E)
    return jnp.concatenate(
        [
            jnp.concatenate(
                [
                    jnp.exp2(
                        scaled[a * BLK : (a + 1) * BLK, b * BLK : (b + 1) * BLK]
                        - jnp.where(use, TEMPER * LOG2_E, NEVER)
                    )
                    for b, use in enumerate(line)
                ],
                axis=1,
            )
            for a, line in enumerate(used)
        ],
        axis=0,
    )


def total(weight, others):
    return jnp.dot(weight.astype(BF16), others, preferred_element_type=F32)


def pair_cost(pairs, width):
    return pl.CostEstimate(
        flops=pairs * 4 * BLK * BLK * width,
        bytes_accessed=pairs * 2 * BLK * width,
        transcendentals=pairs * BLK * BLK,
    )


def params(mib):
    return pltpu.CompilerParams(vmem_limit_bytes=mib * MIB)


def link_place(info, k, blocks):
    return jnp.where(info[ODD] == 1, blocks - 1 - k, k)


def prep_kernel(blocks, axes, pairs_hbm, x_hbm, counts, pay_ref, pairs, sem):
    odd = lax.axis_index("sub") == 1
    base = lax.axis_index(axes) * blocks
    edge = jnp.where(odd, blocks - 1, 0)
    copies = [
        pltpu.make_async_copy(pairs_hbm, pairs, sem.at[0]),
        pltpu.make_async_copy(x_hbm.at[span(edge), :], pay_ref.at[:BLK, :], sem.at[1]),
    ]
    for copy in copies:
        copy.start()
    for r in range(blocks):
        counts[r] = 1
    copies[0].wait()

    def count(s, carry):
        r = pairs[0, s] - base
        counts[r] = counts[r] + jnp.where(pairs[1, s] > pairs[0, s], 1, 0)
        return carry

    lax.fori_loop(0, pairs.shape[1], count, 0)
    tail = jnp.int32(0)
    start = jnp.int32(0)
    for r in range(blocks):
        tail += jnp.where(r + counts[r] > blocks, 1, 0)
        if r:
            start = jnp.where(r - 1 + counts[r - 1] == r, r, start)
        counts[blocks + 1 + r] = start
    counts[blocks] = tail
    pay_ref[BLK:, :] = jnp.full((EXTRA, pay_ref.shape[1]), tail.astype(F32)).astype(BF16)
    copies[1].wait()


def prepare(axes, pair_blocks, x):
    length, width = x.shape
    blocks = length // BLK
    return pl.pallas_call(
        functools.partial(prep_kernel, blocks, axes),
        in_specs=[HBM] * 2,
        out_specs=[SMEM, VMEM],
        out_shape=[
            jax.ShapeDtypeStruct((2 * blocks + 1,), jnp.int32),
            jax.ShapeDtypeStruct((BLK + EXTRA, width), BF16),
        ],
        scratch_shapes=[
            pltpu.SMEM(pair_blocks.shape, jnp.int32),
            pltpu.SemaphoreType.DMA((2,)),
        ],
        compiler_params=params(56),
        cost_estimate=pl.CostEstimate(
            flops=0, bytes_accessed=4 * BLK * width, transcendentals=0
        ),
        name="prepare",
    )(pair_blocks, x)


def same_clusters(counts, blocks, row, col):
    return [
        [counts[blocks + 1 + row + a] == counts[blocks + 1 + col + b] for b in range(2)]
        for a in range(2)
    ]


def local_tile(x_ref, inv_ref, inv_row, row, col, same):
    others = x_ref[span(col, 2), :]
    other_inv = jnp.concatenate([inv_row[col], inv_row[col + 1]], axis=1)
    inner = product(x_ref[span(row, 2), :], others)
    return weights(inner, inv_ref[span(row, 2), :], other_inv, same), others


def diagonal_kernel(blocks, counts, after, x_ref, acc_ref, sums_ref, inv_ref, inv_row, pay_ref):
    odd = lax.axis_index("sub") == 1
    pay_ref[...] = x_ref[span(jnp.where(odd, blocks - 2, 1)), :]

    def norms(r, carry):
        inv = inverse_norm(x_ref[span(r), :])
        inv_ref[span(r), :] = inv
        inv_row[r] = to_row(inv)
        return carry

    lax.fori_loop(0, blocks, norms, 0)

    def visit(k, carry):
        row = 2 * k
        same = same_clusters(counts, blocks, row, row)
        weight, others = local_tile(x_ref, inv_ref, inv_row, row, row, same)
        acc_ref[span(row, 2), :] = total(weight, others)
        sums = jnp.sum(weight, axis=0, keepdims=True)
        for a in range(2):
            store_row(sums_ref, row + a, sums[:, a * BLK : (a + 1) * BLK])
        return carry

    lax.fori_loop(0, blocks // 2, visit, 0)


def rest_kernel(blocks, counts, x_ref, inv_ref, inv_row, acc_in, sums_in, acc_ref, sums_ref):
    half = blocks // 2

    def visit(k, carry):
        row = 2 * lax.div(k, half)
        col = 2 * lax.rem(k, half)
        same = same_clusters(counts, blocks, row, col)

        @pl.when((row < col) & (same[0][0] | same[0][1] | same[1][0] | same[1][1]))
        def _():
            weight, others = local_tile(x_ref, inv_ref, inv_row, row, col, same)
            add_tile(acc_ref, sums_ref, row, weight, others)
            sums = jnp.sum(weight, axis=0, keepdims=True)
            acc_ref[span(col, 2), :] += lax.dot_general(
                weight.astype(BF16),
                x_ref[span(row, 2), :],
                (((0,), (0,)), ((), ())),
                preferred_element_type=F32,
            )
            for b in range(2):
                more = sums[:, b * BLK : (b + 1) * BLK]
                store_row(sums_ref, col + b, load_row(sums_ref, col + b) + more)

        return carry

    lax.fori_loop(0, half * half, visit, 0)


def diagonal_pairs(counts, x, after):
    length, width = x.shape
    blocks = length // BLK
    return pl.pallas_call(
        functools.partial(diagonal_kernel, blocks),
        in_specs=[SMEM, SMEM, VMEM],
        out_specs=[VMEM] * 5,
        out_shape=[
            jax.ShapeDtypeStruct((length, width), F32),
            jax.ShapeDtypeStruct((2 * blocks, LANES), F32),
            jax.ShapeDtypeStruct((length, 1), F32),
            jax.ShapeDtypeStruct((blocks, 1, BLK), F32),
            jax.ShapeDtypeStruct((BLK, width), BF16),
        ],
        compiler_params=params(12),
        cost_estimate=pair_cost(2 * blocks, width),
        name="diagonal_pairs",
    )(counts, after, x)


def rest_pairs(counts, x, inv, inv_row, acc, sums):
    length, width = x.shape
    blocks = length // BLK

    return pl.pallas_call(
        functools.partial(rest_kernel, blocks),
        in_specs=[SMEM] + [VMEM] * 5,
        out_specs=[VMEM] * 2,
        out_shape=totals_shapes(x)[:2],
        input_output_aliases={4: 0, 5: 1},
        compiler_params=params(12),
        cost_estimate=pair_cost(blocks * blocks - 2 * blocks, width),
        name="rest_pairs",
    )(counts, x, inv, inv_row, acc, sums)


def write_payload(blocks, slot, info, x_ref, link_ref, pay_ref, sums_ref, acc):
    mine, theirs = info[MINE_LINK], info[THEIRS_LINK]
    shares = (mine >= 5) & (theirs >= slot - 2)

    @pl.when(jnp.logical_not(shares))
    def _():
        pay_ref[:BLK, :] = x_ref[span(link_place(info, slot - 1, blocks)), :]
        store_row(sums_ref, slot - 3, jnp.zeros((1, BLK), F32))

    @pl.when(shares)
    def _():
        link = link_ref[:BLK, :]
        link_inv = inverse_norm(link)
        acc[...] = jnp.zeros_like(acc)

        def add(k, sums):
            others = x_ref[span(link_place(info, k, blocks)), :]
            weight = weights(product(link, others), link_inv, to_row(inverse_norm(others)))
            acc[...] += total(weight, others)
            return sums + to_row(jnp.sum(weight, axis=1, keepdims=True))

        sums = lax.fori_loop(2, mine, add, jnp.zeros((1, BLK), F32))
        pay_ref[:BLK, :] = acc[...].astype(BF16)
        store_row(sums_ref, slot - 3, sums)


def third_kernel(
    blocks, axes, counts, chip_pairs, x_ref, link_ref, pay_ref, sums_ref, info, acc
):
    odd = lax.axis_index("sub") == 1
    base = lax.axis_index(axes) * blocks
    slots = chip_pairs.shape[1]
    listed = lax.fori_loop(
        0, slots, lambda s, n: n + jnp.where(chip_pairs[1, s] == base, 1, 0), jnp.int32(0)
    )
    told = jnp.max(link_ref[BLK:, :LANES].astype(F32)).astype(jnp.int32)
    head_theirs = jnp.where(odd, listed, told)
    head_mine = jnp.where(head_theirs > 0, counts[0], 0)
    tail_mine = counts[blocks]
    tail_theirs = counts[blocks - 1] - 1
    info[ODD] = jnp.where(odd, 1, 0)
    info[MINE_CHIP] = jnp.where(odd, head_mine, tail_mine)
    info[THEIRS_CHIP] = jnp.where(odd, head_theirs, tail_theirs)
    info[MINE_LINK] = jnp.where(odd, tail_mine, head_mine)
    info[THEIRS_LINK] = jnp.where(odd, tail_theirs, head_theirs)
    store_row(sums_ref, 1, jnp.zeros((1, BLK), F32))
    write_payload(blocks, 3, info, x_ref, link_ref, pay_ref, sums_ref, acc)


def third_payload(axes, counts, chip_list, x, link_block, after):
    length, width = x.shape
    blocks = length // BLK

    def kernel(counts, chip_list, x_ref, link_ref, after_ref, *refs):
        third_kernel(blocks, axes, counts, chip_list, x_ref, link_ref, *refs)

    return pl.pallas_call(
        kernel,
        in_specs=[SMEM, SMEM, VMEM, VMEM, ANY],
        out_specs=[VMEM, VMEM, SMEM],
        out_shape=[
            jax.ShapeDtypeStruct((BLK, width), BF16),
            jax.ShapeDtypeStruct((4, LANES), F32),
            jax.ShapeDtypeStruct((8,), jnp.int32),
        ],
        scratch_shapes=[pltpu.VMEM((BLK, width), F32)],
        compiler_params=params(8),
        cost_estimate=pair_cost(2, width),
        name="third_payload",
    )(counts, chip_list, x, link_block, after)


def fourth_kernel(blocks, info, x_ref, link_ref, after_ref, sums_in, pay_ref, sums_ref, acc):
    write_payload(blocks, 4, info, x_ref, link_ref, pay_ref, sums_ref, acc)
    place = lax.broadcasted_iota(jnp.int32, (EXTRA, BLK), 0)
    parts = jnp.zeros((EXTRA, BLK), F32)
    for slot in range(2):
        rest = load_row(sums_ref, slot)
        for k in range(3):
            part = rest.astype(BF16).astype(F32)
            parts = jnp.where(place == 3 * slot + k, part, parts)
            rest = rest - part
    pay_ref[BLK:, :BLK] = parts.astype(BF16)
    pay_ref[BLK:, BLK:] = jnp.zeros((EXTRA, x_ref.shape[1] - BLK), BF16)


def fourth_payload(info, x, link_block, after, sums):
    length, width = x.shape
    return pl.pallas_call(
        functools.partial(fourth_kernel, length // BLK),
        in_specs=[SMEM, VMEM, VMEM, ANY, VMEM],
        out_specs=[VMEM, VMEM],
        out_shape=[
            jax.ShapeDtypeStruct((BLK + EXTRA, width), BF16),
            jax.ShapeDtypeStruct((4, LANES), F32),
        ],
        input_output_aliases={4: 1},
        scratch_shapes=[pltpu.VMEM((BLK, width), F32)],
        compiler_params=params(8),
        cost_estimate=pair_cost(2, width),
        name="fourth_payload",
    )(info, x, link_block, after, sums)[0]


def copy_out(acc_ref, out_ref, sem, r):
    return pltpu.make_async_copy(acc_ref.at[span(r), :], out_ref.at[span(r), :], sem.at[r])


def finish(acc_ref, sums_ref, out_ref, sem, r):
    acc_ref[span(r), :] = acc_ref[span(r), :] * (1.0 / to_column(load_row(sums_ref, r)))
    copy_out(acc_ref, out_ref, sem, r).start()


def each(blocks, chosen, body):
    def step(r, carry):
        @pl.when(chosen(r))
        def _():
            body(r)

        return carry

    lax.fori_loop(0, blocks, step, 0)


def add_tile(acc_ref, sums_ref, row, weight, others, tall=2):
    acc_ref[span(row, tall), :] += total(weight, others)
    sums = jnp.sum(weight, axis=1, keepdims=True)
    for a in range(tall):
        more = to_row(sums[a * BLK : (a + 1) * BLK])
        store_row(sums_ref, row + a, load_row(sums_ref, row + a) + more)


def chip_kernel(
    blocks,
    info,
    x_ref,
    inv_ref,
    chip_ref,
    acc_in,
    sums_in,
    acc_ref,
    sums_ref,
    out_ref,
    inv_row,
    sem,
):
    odd = info[ODD] == 1
    mine, theirs = info[MINE_CHIP], info[THEIRS_CHIP]
    mine_link = info[MINE_LINK]

    def is_done(r):
        return jnp.where(odd, blocks - 1 - r, r) >= mine_link

    def column(n):
        col = jnp.where(odd, blocks - 2 - 2 * n, 2 * n)
        for b in range(2):
            inv_row[b] = to_row(inverse_norm(chip_ref[span(col + b), :]))
        theirs_ok = [jnp.where(odd, blocks - 1 - col - b, col + b) < theirs for b in range(2)]

        def tile(m, carry):
            row = jnp.where(odd, 2 * m, blocks - 2 - 2 * m)
            mine_ok = [jnp.where(odd, row + a, blocks - 1 - row - a) < mine for a in range(2)]
            others = chip_ref[span(col, 2), :]
            other_inv = jnp.concatenate([inv_row[0], inv_row[1]], axis=1)
            used = [[p & q for q in theirs_ok] for p in mine_ok]
            inner = product(x_ref[span(row, 2), :], others)
            weight = weights(inner, inv_ref[span(row, 2), :], other_inv, used)
            add_tile(acc_ref, sums_ref, row, weight, others)
            return carry

        lax.fori_loop(0, lax.div(mine + 1, 2), tile, 0)

    def columns(n, carry):
        column(n)
        return carry

    lax.fori_loop(0, lax.div(theirs + 1, 2), columns, 0)
    each(blocks, is_done, functools.partial(finish, acc_ref, sums_ref, out_ref, sem))
    each(blocks, is_done, lambda r: copy_out(acc_ref, out_ref, sem, r).wait())


def link_kernel(blocks, slots, info, x_ref, inv_ref, *refs):
    got_refs = refs[: len(slots)]
    acc_in, sums_in, out_in, acc_ref, sums_ref, out_ref, side, inv_row, sem = refs[len(slots) :]
    mine, theirs = info[MINE_LINK], info[THEIRS_LINK]
    odd = info[ODD] == 1

    uses = theirs >= slots[0]
    if slots[0] > 2:
        uses = uses & (theirs <= 4)

    @pl.when(uses)
    def _():
        for k, got_ref in enumerate(got_refs):
            block = got_ref[:BLK, :]
            side[k * BLK : (k + 1) * BLK, :] = block
            inv_row[:, k * BLK : (k + 1) * BLK] = to_row(inverse_norm(block))

        def tile(m, carry):
            row = jnp.where(odd, blocks - 2 - 2 * m, 2 * m)
            mine_ok = [jnp.where(odd, blocks - 1 - row - a, row + a) < mine for a in range(2)]
            others = side[...]
            used = [[p & (theirs >= q) for q in slots] for p in mine_ok]
            inner = product(x_ref[span(row, 2), :], others)
            weight = weights(inner, inv_ref[span(row, 2), :], inv_row[...], used)
            add_tile(acc_ref, sums_ref, row, weight, others)
            return carry

        lax.fori_loop(0, lax.div(mine + 1, 2), tile, 0)

    if slots[0] > 2:

        @pl.when((theirs >= 5) & (mine >= 1))
        def _():
            r = link_place(info, 0, blocks)
            acc_ref[span(r), :] += got_refs[0][...].astype(F32)

    def is_done(r):
        last = jnp.clip(theirs, 2, 4)
        now = last == slots[0]
        for slot in slots[1:]:
            now = now | (last == slot)
        return (jnp.where(odd, blocks - 1 - r, r) < mine) & now

    each(blocks, is_done, functools.partial(finish, acc_ref, sums_ref, out_ref, sem))
    each(blocks, is_done, lambda r: copy_out(acc_ref, out_ref, sem, r).wait())


def last_kernel(
    blocks,
    info,
    x_ref,
    inv_ref,
    got_ref,
    acc_in,
    sums_in,
    out_in,
    acc_ref,
    sums_ref,
    out_ref,
    dup_ref,
    terms,
    sem,
):
    mine, theirs = info[MINE_LINK], info[THEIRS_LINK]
    odd = info[ODD] == 1
    most = 3

    def shift(r):
        return pltpu.make_async_copy(acc_ref.at[span(r), :], out_ref.at[span(r), :], sem.at[r])

    def close(r, more, term):
        sums = load_row(sums_ref, r) + more
        store_row(sums_ref, r, sums)
        acc_ref[span(r), :] = (acc_ref[span(r), :] + term) * (1.0 / to_column(sums))
        shift(r).start()

    @pl.when(theirs == 4)
    def _():
        others = got_ref[:BLK, :]
        low = jnp.where(odd, blocks - most, 0)
        inner = product(x_ref[span(low, most), :], others)
        weight = weights(inner, inv_ref[span(low, most), :], to_row(inverse_norm(others)))
        sums = jnp.sum(weight, axis=1, keepdims=True)
        terms[...] = total(weight, others)
        for k in range(most):
            r = low + k

            @pl.when(jnp.where(odd, blocks - 1 - r, r) < mine)
            def _(k=k, r=r):
                place = slice(k * BLK, (k + 1) * BLK)
                close(r, to_row(sums[place]), terms[place, :])

    for k in range(2):

        @pl.when((theirs >= 5) & (mine > k))
        def _(k=k):
            parts = got_ref[BLK:, :BLK].astype(F32)
            more = jnp.sum(parts[3 * k : 3 * k + 3], axis=0, keepdims=True)
            term = got_ref[:BLK, :].astype(F32) if k else 0.0
            close(link_place(info, k, blocks), more, term)

    dup_copy = pltpu.make_async_copy(sums_ref, dup_ref, sem.at[blocks])
    dup_copy.start()

    def wait(k, carry):
        @pl.when(theirs >= 4)
        def _():
            shift(link_place(info, k, blocks)).wait()

        return carry

    lax.fori_loop(0, mine, wait, 0)
    dup_copy.wait()


def totals_shapes(x):
    length, width = x.shape
    return [
        jax.ShapeDtypeStruct((length, width), F32),
        jax.ShapeDtypeStruct((2 * length // BLK, LANES), F32),
        jax.ShapeDtypeStruct((length, width), F32),
    ]


def chip_pairs(info, x, inv, chip_x, acc, sums):
    length, width = x.shape
    blocks = length // BLK
    return pl.pallas_call(
        functools.partial(chip_kernel, blocks),
        in_specs=[SMEM] + [VMEM] * 5,
        out_specs=[VMEM, VMEM, ANY],
        out_shape=totals_shapes(x),
        scratch_shapes=[pltpu.VMEM((2, 1, BLK), F32), pltpu.SemaphoreType.DMA((blocks,))],
        input_output_aliases={4: 0, 5: 1},
        compiler_params=params(8),
        cost_estimate=pair_cost(12, width),
        name="chip_pairs",
    )(info, x, inv, chip_x, acc, sums)


def link_pairs(slots, info, x, inv, got, acc, sums, out):
    length, width = x.shape
    blocks = length // BLK
    n = len(slots)
    return pl.pallas_call(
        functools.partial(link_kernel, blocks, slots),
        in_specs=[SMEM] + [VMEM] * (4 + n) + [ANY],
        out_specs=[VMEM, VMEM, ANY],
        out_shape=totals_shapes(x),
        scratch_shapes=[
            pltpu.VMEM((n * BLK, width), BF16),
            pltpu.VMEM((1, n * BLK), F32),
            pltpu.SemaphoreType.DMA((blocks,)),
        ],
        input_output_aliases={3 + n: 0, 4 + n: 1, 5 + n: 2},
        compiler_params=params(8),
        cost_estimate=pair_cost(6 * n, width),
        name="link_pairs",
    )(info, x, inv, *got, acc, sums, out)


def last_pairs(info, x, inv, got, acc, sums, out):
    length, width = x.shape
    blocks = length // BLK
    return pl.pallas_call(
        functools.partial(last_kernel, blocks),
        in_specs=[SMEM] + [VMEM] * 5 + [ANY],
        out_specs=[VMEM, VMEM, ANY, ANY],
        out_shape=totals_shapes(x) + totals_shapes(x)[1:2],
        scratch_shapes=[pltpu.VMEM((3 * BLK, width), F32), pltpu.SemaphoreType.DMA((blocks + 1,))],
        input_output_aliases={4: 0, 5: 1, 6: 2},
        compiler_params=params(12),
        cost_estimate=pair_cost(3, width),
        name="last_pairs",
    )(info, x, inv, got, acc, sums, out)[2:]


def per_device(embeddings, pair_blocks, pair_count):
    length, width = embeddings.shape
    blocks = length // BLK
    axes = ("rows", "sub")
    devices = lax.axis_size(axes)
    edges = [(i, i + 1) for i in range(1, devices - 1, 2)]
    edges += [(j, i) for i, j in edges]

    def over_link(array):
        return lax.ppermute(array, axes, edges)

    def over_chip(array):
        return lax.ppermute(array, "sub", [(0, 1), (1, 0)])

    x = embeddings
    counts, first = prepare(axes, pair_blocks, x)
    one = over_link(first)
    chip_x = over_chip(x)
    chip_list = over_chip(pair_blocks)
    acc, sums, inv, inv_row, second = diagonal_pairs(counts, x, chip_list)
    two = over_link(second)
    acc, sums = rest_pairs(counts, x, inv, inv_row, acc, sums)
    third, shared, info = third_payload(axes, counts, chip_list, x, one, sums)
    three = over_link(third)
    acc, sums, out = chip_pairs(info, x, inv, chip_x, acc, sums)
    fourth = fourth_payload(info, x, two, sums, shared)
    four = over_link(fourth)
    acc, sums, out = link_pairs((1, 2), info, x, inv, (one, two), acc, sums, out)
    acc, sums, out = link_pairs((3,), info, x, inv, (three,), acc, sums, out)
    out, dup = last_pairs(info, x, inv, four, acc, sums, out)
    return dup.reshape(length), out


def solution(mesh):
    in_specs = (
        P(("groups", "rows", "sub"), None),
        P(None, ("groups", "rows", "sub")),
        P(("groups", "rows", "sub")),
    )
    out_specs = (P(("groups", "rows", "sub")), P(("groups", "rows", "sub"), None))
    return jax.shard_map(
        per_device, mesh=mesh, in_specs=in_specs, out_specs=out_specs, check_vma=False
    )
```

```python
import functools

import jax
import jax.numpy as jnp
from jax import lax
from jax.experimental import pallas as pl
from jax.experimental.pallas import tpu as pltpu
from jax.sharding import PartitionSpec as P

BLK = 256
EXTRA = 16
TEMPER = 4.0
LOG2_E = 1.4426950408889634
NEVER = 1e30
EPS = 1e-06
LANES = 128
MIB = 1024 * 1024

F32 = jnp.float32
BF16 = jnp.bfloat16

ODD, MINE_CHIP, THEIRS_CHIP, MINE_LINK, THEIRS_LINK = range(5)

VMEM = pl.BlockSpec(memory_space=pltpu.VMEM)
SMEM = pl.BlockSpec(memory_space=pltpu.SMEM)
ANY = pl.BlockSpec(memory_space=pl.ANY)
HBM = pl.BlockSpec(memory_space=pltpu.HBM)


def diagonal():
    return lax.broadcasted_iota(jnp.int32, (BLK, BLK), 0) == lax.broadcasted_iota(
        jnp.int32, (BLK, BLK), 1
    )


def to_row(column):
    return jnp.sum(jnp.where(diagonal(), column, 0.0), axis=0, keepdims=True)


def to_column(row):
    return jnp.sum(jnp.where(diagonal(), row, 0.0), axis=1, keepdims=True)


def inverse_norm(rows):
    wide = rows.astype(F32)
    return lax.rsqrt(jnp.sum(wide * wide, axis=1, keepdims=True) + EPS)


def store_row(ref, place, row):
    ref[pl.ds(2 * place, 1), :] = row[:, :LANES]
    ref[pl.ds(2 * place + 1, 1), :] = row[:, LANES:]


def load_row(ref, place):
    return jnp.concatenate([ref[pl.ds(2 * place, 1), :], ref[pl.ds(2 * place + 1, 1), :]], axis=1)


def span(place, n=1):
    return pl.ds(pl.multiple_of(place * BLK, BLK), n * BLK)


def product(rows, others):
    return lax.dot_general(rows, others, (((1,), (1,)), ((), ())), preferred_element_type=F32)


def weights(inner, row_inv, other_inv, used=None):
    scaled = inner * (TEMPER * LOG2_E * row_inv) * other_inv
    if used is None:
        return jnp.exp2(scaled - TEMPER * LOG2_E)
    return jnp.concatenate(
        [
            jnp.concatenate(
                [
                    jnp.exp2(
                        scaled[a * BLK : (a + 1) * BLK, b * BLK : (b + 1) * BLK]
                        - jnp.where(use, TEMPER * LOG2_E, NEVER)
                    )
                    for b, use in enumerate(line)
                ],
                axis=1,
            )
            for a, line in enumerate(used)
        ],
        axis=0,
    )


def total(weight, others):
    return jnp.dot(weight.astype(BF16), others, preferred_element_type=F32)


def pair_cost(pairs, width):
    return pl.CostEstimate(
        flops=pairs * 4 * BLK * BLK * width,
        bytes_accessed=pairs * 2 * BLK * width,
        transcendentals=pairs * BLK * BLK,
    )


def params(mib):
    return pltpu.CompilerParams(vmem_limit_bytes=mib * MIB)


def link_place(info, k, blocks):
    return jnp.where(info[ODD] == 1, blocks - 1 - k, k)


def prep_kernel(blocks, axes, pairs_hbm, x_hbm, counts, pay_ref, pairs, sem):
    odd = lax.axis_index("sub") == 1
    base = lax.axis_index(axes) * blocks
    edge = jnp.where(odd, blocks - 1, 0)
    copies = [
        pltpu.make_async_copy(pairs_hbm, pairs, sem.at[0]),
        pltpu.make_async_copy(x_hbm.at[span(edge), :], pay_ref.at[:BLK, :], sem.at[1]),
    ]
    for copy in copies:
        copy.start()
    for r in range(blocks):
        counts[r] = 1
    copies[0].wait()

    def count(s, carry):
        r = pairs[0, s] - base
        counts[r] = counts[r] + jnp.where(pairs[1, s] > pairs[0, s], 1, 0)
        return carry

    lax.fori_loop(0, pairs.shape[1], count, 0)
    tail = jnp.int32(0)
    start = jnp.int32(0)
    for r in range(blocks):
        tail += jnp.where(r + counts[r] > blocks, 1, 0)
        if r:
            start = jnp.where(r - 1 + counts[r - 1] == r, r, start)
        counts[blocks + 1 + r] = start
    counts[blocks] = tail
    pay_ref[BLK:, :] = jnp.full((EXTRA, pay_ref.shape[1]), tail.astype(F32)).astype(BF16)
    copies[1].wait()


def prepare(axes, pair_blocks, x):
    length, width = x.shape
    blocks = length // BLK
    return pl.pallas_call(
        functools.partial(prep_kernel, blocks, axes),
        in_specs=[HBM] * 2,
        out_specs=[SMEM, VMEM],
        out_shape=[
            jax.ShapeDtypeStruct((2 * blocks + 1,), jnp.int32),
            jax.ShapeDtypeStruct((BLK + EXTRA, width), BF16),
        ],
        scratch_shapes=[
            pltpu.SMEM(pair_blocks.shape, jnp.int32),
            pltpu.SemaphoreType.DMA((2,)),
        ],
        compiler_params=params(56),
        cost_estimate=pl.CostEstimate(
            flops=0, bytes_accessed=4 * BLK * width, transcendentals=0
        ),
        name="prepare",
    )(pair_blocks, x)


def same_clusters(counts, blocks, row, col):
    return [
        [counts[blocks + 1 + row + a] == counts[blocks + 1 + col + b] for b in range(2)]
        for a in range(2)
    ]


def local_tile(x_ref, inv_ref, inv_row, row, col, same):
    others = x_ref[span(col, 2), :]
    other_inv = jnp.concatenate([inv_row[col], inv_row[col + 1]], axis=1)
    inner = product(x_ref[span(row, 2), :], others)
    return weights(inner, inv_ref[span(row, 2), :], other_inv, same), others


def diagonal_kernel(blocks, counts, after, x_ref, acc_ref, sums_ref, inv_ref, inv_row, pay_ref):
    odd = lax.axis_index("sub") == 1
    pay_ref[...] = x_ref[span(jnp.where(odd, blocks - 2, 1)), :]

    def norms(r, carry):
        inv = inverse_norm(x_ref[span(r), :])
        inv_ref[span(r), :] = inv
        inv_row[r] = to_row(inv)
        return carry

    lax.fori_loop(0, blocks, norms, 0)

    def visit(k, carry):
        row = 2 * k
        same = same_clusters(counts, blocks, row, row)
        weight, others = local_tile(x_ref, inv_ref, inv_row, row, row, same)
        acc_ref[span(row, 2), :] = total(weight, others)
        sums = jnp.sum(weight, axis=0, keepdims=True)
        for a in range(2):
            store_row(sums_ref, row + a, sums[:, a * BLK : (a + 1) * BLK])
        return carry

    lax.fori_loop(0, blocks // 2, visit, 0)


def rest_kernel(blocks, counts, x_ref, inv_ref, inv_row, acc_in, sums_in, acc_ref, sums_ref):
    half = blocks // 2

    def visit(k, carry):
        row = 2 * lax.div(k, half)
        col = 2 * lax.rem(k, half)
        same = same_clusters(counts, blocks, row, col)

        @pl.when((row < col) & (same[0][0] | same[0][1] | same[1][0] | same[1][1]))
        def _():
            weight, others = local_tile(x_ref, inv_ref, inv_row, row, col, same)
            add_tile(acc_ref, sums_ref, row, weight, others)
            sums = jnp.sum(weight, axis=0, keepdims=True)
            acc_ref[span(col, 2), :] += lax.dot_general(
                weight.astype(BF16),
                x_ref[span(row, 2), :],
                (((0,), (0,)), ((), ())),
                preferred_element_type=F32,
            )
            for b in range(2):
                more = sums[:, b * BLK : (b + 1) * BLK]
                store_row(sums_ref, col + b, load_row(sums_ref, col + b) + more)

        return carry

    lax.fori_loop(0, half * half, visit, 0)


def diagonal_pairs(counts, x, after):
    length, width = x.shape
    blocks = length // BLK
    return pl.pallas_call(
        functools.partial(diagonal_kernel, blocks),
        in_specs=[SMEM, SMEM, VMEM],
        out_specs=[VMEM] * 5,
        out_shape=[
            jax.ShapeDtypeStruct((length, width), F32),
            jax.ShapeDtypeStruct((2 * blocks, LANES), F32),
            jax.ShapeDtypeStruct((length, 1), F32),
            jax.ShapeDtypeStruct((blocks, 1, BLK), F32),
            jax.ShapeDtypeStruct((BLK, width), BF16),
        ],
        compiler_params=params(12),
        cost_estimate=pair_cost(2 * blocks, width),
        name="diagonal_pairs",
    )(counts, after, x)


def rest_pairs(counts, x, inv, inv_row, acc, sums):
    length, width = x.shape
    blocks = length // BLK

    return pl.pallas_call(
        functools.partial(rest_kernel, blocks),
        in_specs=[SMEM] + [VMEM] * 5,
        out_specs=[VMEM] * 2,
        out_shape=totals_shapes(x)[:2],
        input_output_aliases={4: 0, 5: 1},
        compiler_params=params(12),
        cost_estimate=pair_cost(blocks * blocks - 2 * blocks, width),
        name="rest_pairs",
    )(counts, x, inv, inv_row, acc, sums)


def write_payload(blocks, slot, info, x_ref, inv_row, link_ref, pay_ref, sums_ref, acc):
    mine, theirs = info[MINE_LINK], info[THEIRS_LINK]
    shares = (mine >= 5) & (theirs >= slot - 2)

    @pl.when(jnp.logical_not(shares))
    def _():
        pay_ref[:BLK, :] = x_ref[span(link_place(info, slot - 1, blocks)), :]
        store_row(sums_ref, slot - 3, jnp.zeros((1, BLK), F32))

    @pl.when(shares)
    def _():
        link = link_ref[:BLK, :]
        link_inv = inverse_norm(link)
        acc[...] = jnp.zeros_like(acc)

        def add(m, sums):
            low = jnp.where(info[ODD] == 1, blocks - 4 - 2 * m, 2 + 2 * m)
            others = x_ref[span(low, 2), :]
            other_inv = jnp.concatenate([inv_row[low], inv_row[low + 1]], axis=1)
            used = [[link_place(info, low + b, blocks) < mine for b in range(2)]]
            weight = weights(product(link, others), link_inv, other_inv, used)
            acc[...] += total(weight, others)
            return sums + to_row(jnp.sum(weight, axis=1, keepdims=True))

        sums = lax.fori_loop(0, lax.div(mine - 1, 2), add, jnp.zeros((1, BLK), F32))
        pay_ref[:BLK, :] = acc[...].astype(BF16)
        store_row(sums_ref, slot - 3, sums)


def third_kernel(
    blocks, axes, counts, chip_pairs, x_ref, inv_row, link_ref, pay_ref, sums_ref, info, acc
):
    odd = lax.axis_index("sub") == 1
    base = lax.axis_index(axes) * blocks
    slots = chip_pairs.shape[1]
    listed = lax.fori_loop(
        0, slots, lambda s, n: n + jnp.where(chip_pairs[1, s] == base, 1, 0), jnp.int32(0)
    )
    told = jnp.max(link_ref[BLK:, :LANES].astype(F32)).astype(jnp.int32)
    head_theirs = jnp.where(odd, listed, told)
    head_mine = jnp.where(head_theirs > 0, counts[0], 0)
    tail_mine = counts[blocks]
    tail_theirs = counts[blocks - 1] - 1
    info[ODD] = jnp.where(odd, 1, 0)
    info[MINE_CHIP] = jnp.where(odd, head_mine, tail_mine)
    info[THEIRS_CHIP] = jnp.where(odd, head_theirs, tail_theirs)
    info[MINE_LINK] = jnp.where(odd, tail_mine, head_mine)
    info[THEIRS_LINK] = jnp.where(odd, tail_theirs, head_theirs)
    store_row(sums_ref, 1, jnp.zeros((1, BLK), F32))
    write_payload(blocks, 3, info, x_ref, inv_row, link_ref, pay_ref, sums_ref, acc)


def third_payload(axes, counts, chip_list, x, inv_row, link_block, after):
    length, width = x.shape
    blocks = length // BLK

    def kernel(counts, chip_list, x_ref, inv_row, link_ref, after_ref, *refs):
        third_kernel(blocks, axes, counts, chip_list, x_ref, inv_row, link_ref, *refs)

    return pl.pallas_call(
        kernel,
        in_specs=[SMEM, SMEM, VMEM, VMEM, VMEM, ANY],
        out_specs=[VMEM, VMEM, SMEM],
        out_shape=[
            jax.ShapeDtypeStruct((BLK, width), BF16),
            jax.ShapeDtypeStruct((4, LANES), F32),
            jax.ShapeDtypeStruct((8,), jnp.int32),
        ],
        scratch_shapes=[pltpu.VMEM((BLK, width), F32)],
        compiler_params=params(8),
        cost_estimate=pair_cost(2, width),
        name="third_payload",
    )(counts, chip_list, x, inv_row, link_block, after)


def fourth_kernel(
    blocks, info, x_ref, inv_row, link_ref, after_ref, sums_in, pay_ref, sums_ref, acc
):
    write_payload(blocks, 4, info, x_ref, inv_row, link_ref, pay_ref, sums_ref, acc)
    place = lax.broadcasted_iota(jnp.int32, (EXTRA, BLK), 0)
    parts = jnp.zeros((EXTRA, BLK), F32)
    for slot in range(2):
        rest = load_row(sums_ref, slot)
        for k in range(3):
            part = rest.astype(BF16).astype(F32)
            parts = jnp.where(place == 3 * slot + k, part, parts)
            rest = rest - part
    pay_ref[BLK:, :BLK] = parts.astype(BF16)
    pay_ref[BLK:, BLK:] = jnp.zeros((EXTRA, x_ref.shape[1] - BLK), BF16)


def fourth_payload(info, x, inv_row, link_block, after, sums):
    length, width = x.shape
    return pl.pallas_call(
        functools.partial(fourth_kernel, length // BLK),
        in_specs=[SMEM, VMEM, VMEM, VMEM, ANY, VMEM],
        out_specs=[VMEM, VMEM],
        out_shape=[
            jax.ShapeDtypeStruct((BLK + EXTRA, width), BF16),
            jax.ShapeDtypeStruct((4, LANES), F32),
        ],
        input_output_aliases={5: 1},
        scratch_shapes=[pltpu.VMEM((BLK, width), F32)],
        compiler_params=params(8),
        cost_estimate=pair_cost(2, width),
        name="fourth_payload",
    )(info, x, inv_row, link_block, after, sums)[0]


def copy_out(acc_ref, out_ref, sem, r):
    return pltpu.make_async_copy(acc_ref.at[span(r), :], out_ref.at[span(r), :], sem.at[r])


def finish(acc_ref, sums_ref, out_ref, sem, r):
    acc_ref[span(r), :] = acc_ref[span(r), :] * (1.0 / to_column(load_row(sums_ref, r)))
    copy_out(acc_ref, out_ref, sem, r).start()


def each(blocks, chosen, body):
    def step(r, carry):
        @pl.when(chosen(r))
        def _():
            body(r)

        return carry

    lax.fori_loop(0, blocks, step, 0)


def add_tile(acc_ref, sums_ref, row, weight, others, tall=2):
    acc_ref[span(row, tall), :] += total(weight, others)
    sums = jnp.sum(weight, axis=1, keepdims=True)
    for a in range(tall):
        more = to_row(sums[a * BLK : (a + 1) * BLK])
        store_row(sums_ref, row + a, load_row(sums_ref, row + a) + more)


def chip_kernel(
    blocks,
    info,
    x_ref,
    inv_ref,
    chip_ref,
    acc_in,
    sums_in,
    acc_ref,
    sums_ref,
    out_ref,
    inv_row,
    sem,
):
    odd = info[ODD] == 1
    mine, theirs = info[MINE_CHIP], info[THEIRS_CHIP]
    mine_link = info[MINE_LINK]

    def is_done(r):
        return jnp.where(odd, blocks - 1 - r, r) >= mine_link

    def column(n):
        col = jnp.where(odd, blocks - 2 - 2 * n, 2 * n)
        for b in range(2):
            inv_row[b] = to_row(inverse_norm(chip_ref[span(col + b), :]))
        theirs_ok = [jnp.where(odd, blocks - 1 - col - b, col + b) < theirs for b in range(2)]

        def tile(m, carry):
            row = jnp.where(odd, 2 * m, blocks - 2 - 2 * m)
            mine_ok = [jnp.where(odd, row + a, blocks - 1 - row - a) < mine for a in range(2)]
            others = chip_ref[span(col, 2), :]
            other_inv = jnp.concatenate([inv_row[0], inv_row[1]], axis=1)
            used = [[p & q for q in theirs_ok] for p in mine_ok]
            inner = product(x_ref[span(row, 2), :], others)
            weight = weights(inner, inv_ref[span(row, 2), :], other_inv, used)
            add_tile(acc_ref, sums_ref, row, weight, others)
            return carry

        lax.fori_loop(0, lax.div(mine + 1, 2), tile, 0)

    def columns(n, carry):
        column(n)
        return carry

    lax.fori_loop(0, lax.div(theirs + 1, 2), columns, 0)
    each(blocks, is_done, functools.partial(finish, acc_ref, sums_ref, out_ref, sem))
    each(blocks, is_done, lambda r: copy_out(acc_ref, out_ref, sem, r).wait())


def link_kernel(blocks, slots, info, x_ref, inv_ref, *refs):
    got_refs = refs[: len(slots)]
    acc_in, sums_in, out_in, acc_ref, sums_ref, out_ref, side, inv_row, sem = refs[len(slots) :]
    mine, theirs = info[MINE_LINK], info[THEIRS_LINK]
    odd = info[ODD] == 1

    uses = theirs >= slots[0]
    if slots[0] > 2:
        uses = uses & (theirs <= 4)

    @pl.when(uses)
    def _():
        for k, got_ref in enumerate(got_refs):
            block = got_ref[:BLK, :]
            side[k * BLK : (k + 1) * BLK, :] = block
            inv_row[:, k * BLK : (k + 1) * BLK] = to_row(inverse_norm(block))

        def tile(m, carry):
            row = jnp.where(odd, blocks - 2 - 2 * m, 2 * m)
            mine_ok = [jnp.where(odd, blocks - 1 - row - a, row + a) < mine for a in range(2)]
            others = side[...]
            used = [[p & (theirs >= q) for q in slots] for p in mine_ok]
            inner = product(x_ref[span(row, 2), :], others)
            weight = weights(inner, inv_ref[span(row, 2), :], inv_row[...], used)
            add_tile(acc_ref, sums_ref, row, weight, others)
            return carry

        lax.fori_loop(0, lax.div(mine + 1, 2), tile, 0)

    if slots[0] > 2:

        @pl.when((theirs >= 5) & (mine >= 1))
        def _():
            r = link_place(info, 0, blocks)
            acc_ref[span(r), :] += got_refs[0][...].astype(F32)

    def is_done(r):
        last = jnp.clip(theirs, 2, 4)
        now = last == slots[0]
        for slot in slots[1:]:
            now = now | (last == slot)
        return (jnp.where(odd, blocks - 1 - r, r) < mine) & now

    each(blocks, is_done, functools.partial(finish, acc_ref, sums_ref, out_ref, sem))
    each(blocks, is_done, lambda r: copy_out(acc_ref, out_ref, sem, r).wait())


def last_kernel(
    blocks, info, x_ref, inv_ref, got_ref, acc_in, sums_in, out_in, acc_ref, sums_ref, out_ref, dup_ref, inv_row, sem
):
    mine, theirs = info[MINE_LINK], info[THEIRS_LINK]

    def shift(r):
        return pltpu.make_async_copy(acc_ref.at[span(r), :], out_ref.at[span(r), :], sem.at[r])

    def close(r, more, term):
        sums = load_row(sums_ref, r) + more
        store_row(sums_ref, r, sums)
        acc_ref[span(r), :] = (acc_ref[span(r), :] + term) * (1.0 / to_column(sums))
        shift(r).start()

    @pl.when(theirs == 4)
    def _():
        inv_row[...] = to_row(inverse_norm(got_ref[:BLK, :]))

        def visit(k, carry):
            r = link_place(info, k, blocks)
            others = got_ref[:BLK, :]
            inner = product(x_ref[span(r), :], others)
            weight = weights(inner, inv_ref[span(r), :], inv_row[...])
            more = to_row(jnp.sum(weight, axis=1, keepdims=True))
            close(r, more, total(weight, others))
            return carry

        lax.fori_loop(0, mine, visit, 0)

    for k in range(2):

        @pl.when((theirs >= 5) & (mine > k))
        def _(k=k):
            parts = got_ref[BLK:, :BLK].astype(F32)
            more = jnp.sum(parts[3 * k : 3 * k + 3], axis=0, keepdims=True)
            term = got_ref[:BLK, :].astype(F32) if k else 0.0
            close(link_place(info, k, blocks), more, term)

    dup_copy = pltpu.make_async_copy(sums_ref, dup_ref, sem.at[blocks])
    dup_copy.start()

    def wait(k, carry):
        @pl.when(theirs >= 4)
        def _():
            shift(link_place(info, k, blocks)).wait()

        return carry

    lax.fori_loop(0, mine, wait, 0)
    dup_copy.wait()


def totals_shapes(x):
    length, width = x.shape
    return [
        jax.ShapeDtypeStruct((length, width), F32),
        jax.ShapeDtypeStruct((2 * length // BLK, LANES), F32),
        jax.ShapeDtypeStruct((length, width), F32),
    ]


def chip_pairs(info, x, inv, chip_x, acc, sums):
    length, width = x.shape
    blocks = length // BLK
    return pl.pallas_call(
        functools.partial(chip_kernel, blocks),
        in_specs=[SMEM] + [VMEM] * 5,
        out_specs=[VMEM, VMEM, ANY],
        out_shape=totals_shapes(x),
        scratch_shapes=[pltpu.VMEM((2, 1, BLK), F32), pltpu.SemaphoreType.DMA((blocks,))],
        input_output_aliases={4: 0, 5: 1},
        compiler_params=params(8),
        cost_estimate=pair_cost(12, width),
        name="chip_pairs",
    )(info, x, inv, chip_x, acc, sums)


def link_pairs(slots, info, x, inv, got, acc, sums, out):
    length, width = x.shape
    blocks = length // BLK
    n = len(slots)
    return pl.pallas_call(
        functools.partial(link_kernel, blocks, slots),
        in_specs=[SMEM] + [VMEM] * (4 + n) + [ANY],
        out_specs=[VMEM, VMEM, ANY],
        out_shape=totals_shapes(x),
        scratch_shapes=[
            pltpu.VMEM((n * BLK, width), BF16),
            pltpu.VMEM((1, n * BLK), F32),
            pltpu.SemaphoreType.DMA((blocks,)),
        ],
        input_output_aliases={3 + n: 0, 4 + n: 1, 5 + n: 2},
        compiler_params=params(8),
        cost_estimate=pair_cost(6 * n, width),
        name="link_pairs",
    )(info, x, inv, *got, acc, sums, out)


def last_pairs(info, x, inv, got, acc, sums, out):
    length, width = x.shape
    blocks = length // BLK
    return pl.pallas_call(
        functools.partial(last_kernel, blocks),
        in_specs=[SMEM] + [VMEM] * 5 + [ANY],
        out_specs=[VMEM, VMEM, ANY, ANY],
        out_shape=totals_shapes(x) + totals_shapes(x)[1:2],
        scratch_shapes=[pltpu.VMEM((1, BLK), F32), pltpu.SemaphoreType.DMA((blocks + 1,))],
        input_output_aliases={4: 0, 5: 1, 6: 2},
        compiler_params=params(8),
        cost_estimate=pair_cost(3, width),
        name="last_pairs",
    )(info, x, inv, got, acc, sums, out)[2:]


def per_device(embeddings, pair_blocks, pair_count):
    length, width = embeddings.shape
    blocks = length // BLK
    axes = ("rows", "sub")
    devices = lax.axis_size(axes)
    edges = [(i, i + 1) for i in range(1, devices - 1, 2)]
    edges += [(j, i) for i, j in edges]

    def over_link(array):
        return lax.ppermute(array, axes, edges)

    def over_chip(array):
        return lax.ppermute(array, "sub", [(0, 1), (1, 0)])

    x = embeddings
    counts, first = prepare(axes, pair_blocks, x)
    one = over_link(first)
    chip_x = over_chip(x)
    chip_list = over_chip(pair_blocks)
    acc, sums, inv, inv_row, second = diagonal_pairs(counts, x, chip_list)
    two = over_link(second)
    acc, sums = rest_pairs(counts, x, inv, inv_row, acc, sums)
    third, shared, info = third_payload(axes, counts, chip_list, x, inv_row, one, sums)
    three = over_link(third)
    acc, sums, out = chip_pairs(info, x, inv, chip_x, acc, sums)
    fourth = fourth_payload(info, x, inv_row, two, sums, shared)
    four = over_link(fourth)
    acc, sums, out = link_pairs((1, 2), info, x, inv, (one, two), acc, sums, out)
    acc, sums, out = link_pairs((3,), info, x, inv, (three,), acc, sums, out)
    out, dup = last_pairs(info, x, inv, four, acc, sums, out)
    return dup.reshape(length), out


def solution(mesh):
    in_specs = (
        P(("groups", "rows", "sub"), None),
        P(None, ("groups", "rows", "sub")),
        P(("groups", "rows", "sub")),
    )
    out_specs = (P(("groups", "rows", "sub")), P(("groups", "rows", "sub"), None))
    return jax.shard_map(
        per_device, mesh=mesh, in_specs=in_specs, out_specs=out_specs, check_vma=False
    )
```

```python
import functools

import jax
import jax.numpy as jnp
from jax import lax
from jax.experimental import pallas as pl
from jax.experimental.pallas import tpu as pltpu
from jax.sharding import PartitionSpec as P

BLK = 256
EXTRA = 16
TEMPER = 4.0
LOG2_E = 1.4426950408889634
NEVER = 1e30
EPS = 1e-06
LANES = 128
MIB = 1024 * 1024

F32 = jnp.float32
BF16 = jnp.bfloat16

ODD, MINE_CHIP, THEIRS_CHIP, MINE_LINK, THEIRS_LINK = range(5)

VMEM = pl.BlockSpec(memory_space=pltpu.VMEM)
SMEM = pl.BlockSpec(memory_space=pltpu.SMEM)
ANY = pl.BlockSpec(memory_space=pl.ANY)
HBM = pl.BlockSpec(memory_space=pltpu.HBM)


def diagonal():
    return lax.broadcasted_iota(jnp.int32, (BLK, BLK), 0) == lax.broadcasted_iota(
        jnp.int32, (BLK, BLK), 1
    )


def to_row(column):
    return jnp.sum(jnp.where(diagonal(), column, 0.0), axis=0, keepdims=True)


def to_column(row):
    return jnp.sum(jnp.where(diagonal(), row, 0.0), axis=1, keepdims=True)


def inverse_norm(rows):
    wide = rows.astype(F32)
    return lax.rsqrt(jnp.sum(wide * wide, axis=1, keepdims=True) + EPS)


def store_row(ref, place, row):
    ref[pl.ds(2 * place, 1), :] = row[:, :LANES]
    ref[pl.ds(2 * place + 1, 1), :] = row[:, LANES:]


def load_row(ref, place):
    return jnp.concatenate([ref[pl.ds(2 * place, 1), :], ref[pl.ds(2 * place + 1, 1), :]], axis=1)


def span(place, n=1):
    return pl.ds(pl.multiple_of(place * BLK, BLK), n * BLK)


def product(rows, others):
    return lax.dot_general(rows, others, (((1,), (1,)), ((), ())), preferred_element_type=F32)


def weights(inner, row_inv, other_inv, used=None):
    scaled = inner * (TEMPER * LOG2_E * row_inv) * other_inv
    if used is None:
        return jnp.exp2(scaled - TEMPER * LOG2_E)
    return jnp.concatenate(
        [
            jnp.concatenate(
                [
                    jnp.exp2(
                        scaled[a * BLK : (a + 1) * BLK, b * BLK : (b + 1) * BLK]
                        - jnp.where(use, TEMPER * LOG2_E, NEVER)
                    )
                    for b, use in enumerate(line)
                ],
                axis=1,
            )
            for a, line in enumerate(used)
        ],
        axis=0,
    )


def total(weight, others):
    return jnp.dot(weight.astype(BF16), others, preferred_element_type=F32)


def pair_cost(pairs, width):
    return pl.CostEstimate(
        flops=pairs * 4 * BLK * BLK * width,
        bytes_accessed=pairs * 2 * BLK * width,
        transcendentals=pairs * BLK * BLK,
    )


def params(mib):
    return pltpu.CompilerParams(vmem_limit_bytes=mib * MIB)


def link_place(info, k, blocks):
    return jnp.where(info[ODD] == 1, blocks - 1 - k, k)


def prep_kernel(blocks, axes, pairs_hbm, x_hbm, pay_ref, pairs, sem):
    base = lax.axis_index(axes) * blocks
    edge = jnp.where(lax.axis_index("sub") == 1, blocks - 1, 0)
    copies = [
        pltpu.make_async_copy(pairs_hbm, pairs, sem.at[0]),
        pltpu.make_async_copy(x_hbm.at[span(edge), :], pay_ref.at[:BLK, :], sem.at[1]),
    ]
    for copy in copies:
        copy.start()
    copies[0].wait()
    tail = lax.fori_loop(
        0,
        pairs.shape[1],
        lambda s, n: n + jnp.where(pairs[1, s] == base + blocks, 1, 0),
        jnp.int32(0),
    )
    pay_ref[BLK:, :] = jnp.full((EXTRA, pay_ref.shape[1]), tail.astype(F32)).astype(BF16)
    copies[1].wait()


def prepare(axes, pair_blocks, x):
    length, width = x.shape
    return pl.pallas_call(
        functools.partial(prep_kernel, length // BLK, axes),
        in_specs=[HBM] * 2,
        out_specs=VMEM,
        out_shape=jax.ShapeDtypeStruct((BLK + EXTRA, width), BF16),
        scratch_shapes=[
            pltpu.SMEM(pair_blocks.shape, jnp.int32),
            pltpu.SemaphoreType.DMA((2,)),
        ],
        compiler_params=params(56),
        cost_estimate=pl.CostEstimate(
            flops=0, bytes_accessed=4 * BLK * width, transcendentals=0
        ),
        name="prepare",
    )(pair_blocks, x)


def count_pairs(blocks, axes, pairs, counts):
    base = lax.axis_index(axes) * blocks
    for r in range(blocks):
        counts[r] = 1

    def count(s, carry):
        r = pairs[0, s] - base
        counts[r] = counts[r] + jnp.where(pairs[1, s] > pairs[0, s], 1, 0)
        return carry

    lax.fori_loop(0, pairs.shape[1], count, 0)
    tail = jnp.int32(0)
    start = jnp.int32(0)
    for r in range(blocks):
        tail += jnp.where(r + counts[r] > blocks, 1, 0)
        if r:
            start = jnp.where(r - 1 + counts[r - 1] == r, r, start)
        counts[blocks + 1 + r] = start
    counts[blocks] = tail


def same_clusters(counts, blocks, row, col):
    return [
        [counts[blocks + 1 + row + a] == counts[blocks + 1 + col + b] for b in range(2)]
        for a in range(2)
    ]


def local_tile(x_ref, inv_ref, inv_row, row, col, same):
    others = x_ref[span(col, 2), :]
    other_inv = jnp.concatenate([inv_row[col], inv_row[col + 1]], axis=1)
    inner = product(x_ref[span(row, 2), :], others)
    return weights(inner, inv_ref[span(row, 2), :], other_inv, same), others


def diagonal_kernel(
    blocks, axes, pairs, after, x_ref, acc_ref, sums_ref, inv_ref, inv_row, pay_ref, counts
):
    odd = lax.axis_index("sub") == 1
    count_pairs(blocks, axes, pairs, counts)
    pay_ref[...] = x_ref[span(jnp.where(odd, blocks - 2, 1)), :]

    def norms(r, carry):
        inv = inverse_norm(x_ref[span(r), :])
        inv_ref[span(r), :] = inv
        inv_row[r] = to_row(inv)
        return carry

    lax.fori_loop(0, blocks, norms, 0)

    def visit(k, carry):
        row = 2 * k
        same = same_clusters(counts, blocks, row, row)
        weight, others = local_tile(x_ref, inv_ref, inv_row, row, row, same)
        acc_ref[span(row, 2), :] = total(weight, others)
        sums = jnp.sum(weight, axis=0, keepdims=True)
        for a in range(2):
            store_row(sums_ref, row + a, sums[:, a * BLK : (a + 1) * BLK])
        return carry

    lax.fori_loop(0, blocks // 2, visit, 0)


def rest_kernel(blocks, counts, x_ref, inv_ref, inv_row, acc_in, sums_in, acc_ref, sums_ref):
    half = blocks // 2

    def visit(k, carry):
        row = 2 * lax.div(k, half)
        col = 2 * lax.rem(k, half)
        same = same_clusters(counts, blocks, row, col)

        @pl.when((row < col) & (same[0][0] | same[0][1] | same[1][0] | same[1][1]))
        def _():
            weight, others = local_tile(x_ref, inv_ref, inv_row, row, col, same)
            add_tile(acc_ref, sums_ref, row, weight, others)
            sums = jnp.sum(weight, axis=0, keepdims=True)
            acc_ref[span(col, 2), :] += lax.dot_general(
                weight.astype(BF16),
                x_ref[span(row, 2), :],
                (((0,), (0,)), ((), ())),
                preferred_element_type=F32,
            )
            for b in range(2):
                more = sums[:, b * BLK : (b + 1) * BLK]
                store_row(sums_ref, col + b, load_row(sums_ref, col + b) + more)

        return carry

    lax.fori_loop(0, half * half, visit, 0)


def diagonal_pairs(axes, pairs, x, after):
    length, width = x.shape
    blocks = length // BLK
    return pl.pallas_call(
        functools.partial(diagonal_kernel, blocks, axes),
        in_specs=[SMEM, SMEM, VMEM],
        out_specs=[VMEM] * 5 + [SMEM],
        out_shape=[
            jax.ShapeDtypeStruct((length, width), F32),
            jax.ShapeDtypeStruct((2 * blocks, LANES), F32),
            jax.ShapeDtypeStruct((length, 1), F32),
            jax.ShapeDtypeStruct((blocks, 1, BLK), F32),
            jax.ShapeDtypeStruct((BLK, width), BF16),
            jax.ShapeDtypeStruct((2 * blocks + 1,), jnp.int32),
        ],
        compiler_params=params(12),
        cost_estimate=pair_cost(2 * blocks, width),
        name="diagonal_pairs",
    )(pairs, after, x)


def rest_pairs(counts, x, inv, inv_row, acc, sums):
    length, width = x.shape
    blocks = length // BLK

    return pl.pallas_call(
        functools.partial(rest_kernel, blocks),
        in_specs=[SMEM] + [VMEM] * 5,
        out_specs=[VMEM] * 2,
        out_shape=totals_shapes(x)[:2],
        input_output_aliases={4: 0, 5: 1},
        compiler_params=params(12),
        cost_estimate=pair_cost(blocks * blocks - 2 * blocks, width),
        name="rest_pairs",
    )(counts, x, inv, inv_row, acc, sums)


def write_payload(blocks, slot, info, x_ref, inv_row, link_ref, pay_ref, sums_ref, acc):
    mine, theirs = info[MINE_LINK], info[THEIRS_LINK]
    shares = (mine >= 5) & (theirs >= slot - 2)

    @pl.when(jnp.logical_not(shares))
    def _():
        pay_ref[:BLK, :] = x_ref[span(link_place(info, slot - 1, blocks)), :]
        store_row(sums_ref, slot - 3, jnp.zeros((1, BLK), F32))

    @pl.when(shares)
    def _():
        link = link_ref[:BLK, :]
        link_inv = inverse_norm(link)
        acc[...] = jnp.zeros_like(acc)

        def add(m, sums):
            low = jnp.where(info[ODD] == 1, blocks - 4 - 2 * m, 2 + 2 * m)
            others = x_ref[span(low, 2), :]
            other_inv = jnp.concatenate([inv_row[low], inv_row[low + 1]], axis=1)
            used = [[link_place(info, low + b, blocks) < mine for b in range(2)]]
            weight = weights(product(link, others), link_inv, other_inv, used)
            acc[...] += total(weight, others)
            return sums + to_row(jnp.sum(weight, axis=1, keepdims=True))

        sums = lax.fori_loop(0, lax.div(mine - 1, 2), add, jnp.zeros((1, BLK), F32))
        pay_ref[:BLK, :] = acc[...].astype(BF16)
        store_row(sums_ref, slot - 3, sums)


def third_kernel(
    blocks, axes, counts, chip_pairs, x_ref, inv_row, link_ref, pay_ref, sums_ref, info, acc
):
    odd = lax.axis_index("sub") == 1
    base = lax.axis_index(axes) * blocks
    slots = chip_pairs.shape[1]
    listed = lax.fori_loop(
        0, slots, lambda s, n: n + jnp.where(chip_pairs[1, s] == base, 1, 0), jnp.int32(0)
    )
    told = jnp.max(link_ref[BLK:, :LANES].astype(F32)).astype(jnp.int32)
    head_theirs = jnp.where(odd, listed, told)
    head_mine = jnp.where(head_theirs > 0, counts[0], 0)
    tail_mine = counts[blocks]
    tail_theirs = counts[blocks - 1] - 1
    info[ODD] = jnp.where(odd, 1, 0)
    info[MINE_CHIP] = jnp.where(odd, head_mine, tail_mine)
    info[THEIRS_CHIP] = jnp.where(odd, head_theirs, tail_theirs)
    info[MINE_LINK] = jnp.where(odd, tail_mine, head_mine)
    info[THEIRS_LINK] = jnp.where(odd, tail_theirs, head_theirs)
    store_row(sums_ref, 1, jnp.zeros((1, BLK), F32))
    write_payload(blocks, 3, info, x_ref, inv_row, link_ref, pay_ref, sums_ref, acc)


def third_payload(axes, counts, chip_list, x, inv_row, link_block, after):
    length, width = x.shape
    blocks = length // BLK

    def kernel(counts, chip_list, x_ref, inv_row, link_ref, after_ref, *refs):
        third_kernel(blocks, axes, counts, chip_list, x_ref, inv_row, link_ref, *refs)

    return pl.pallas_call(
        kernel,
        in_specs=[SMEM, SMEM, VMEM, VMEM, VMEM, ANY],
        out_specs=[VMEM, VMEM, SMEM],
        out_shape=[
            jax.ShapeDtypeStruct((BLK, width), BF16),
            jax.ShapeDtypeStruct((4, LANES), F32),
            jax.ShapeDtypeStruct((8,), jnp.int32),
        ],
        scratch_shapes=[pltpu.VMEM((BLK, width), F32)],
        compiler_params=params(8),
        cost_estimate=pair_cost(2, width),
        name="third_payload",
    )(counts, chip_list, x, inv_row, link_block, after)


def fourth_kernel(
    blocks, info, x_ref, inv_row, link_ref, after_ref, sums_in, pay_ref, sums_ref, acc
):
    write_payload(blocks, 4, info, x_ref, inv_row, link_ref, pay_ref, sums_ref, acc)
    place = lax.broadcasted_iota(jnp.int32, (EXTRA, BLK), 0)
    parts = jnp.zeros((EXTRA, BLK), F32)
    for slot in range(2):
        rest = load_row(sums_ref, slot)
        for k in range(3):
            part = rest.astype(BF16).astype(F32)
            parts = jnp.where(place == 3 * slot + k, part, parts)
            rest = rest - part
    pay_ref[BLK:, :BLK] = parts.astype(BF16)
    pay_ref[BLK:, BLK:] = jnp.zeros((EXTRA, x_ref.shape[1] - BLK), BF16)


def fourth_payload(info, x, inv_row, link_block, after, sums):
    length, width = x.shape
    return pl.pallas_call(
        functools.partial(fourth_kernel, length // BLK),
        in_specs=[SMEM, VMEM, VMEM, VMEM, ANY, VMEM],
        out_specs=[VMEM, VMEM],
        out_shape=[
            jax.ShapeDtypeStruct((BLK + EXTRA, width), BF16),
            jax.ShapeDtypeStruct((4, LANES), F32),
        ],
        input_output_aliases={5: 1},
        scratch_shapes=[pltpu.VMEM((BLK, width), F32)],
        compiler_params=params(8),
        cost_estimate=pair_cost(2, width),
        name="fourth_payload",
    )(info, x, inv_row, link_block, after, sums)[0]


def copy_out(acc_ref, out_ref, sem, r):
    return pltpu.make_async_copy(acc_ref.at[span(r), :], out_ref.at[span(r), :], sem.at[r])


def finish(acc_ref, sums_ref, out_ref, sem, r):
    acc_ref[span(r), :] = acc_ref[span(r), :] * (1.0 / to_column(load_row(sums_ref, r)))
    copy_out(acc_ref, out_ref, sem, r).start()


def each(blocks, chosen, body):
    def step(r, carry):
        @pl.when(chosen(r))
        def _():
            body(r)

        return carry

    lax.fori_loop(0, blocks, step, 0)


def add_tile(acc_ref, sums_ref, row, weight, others, tall=2):
    acc_ref[span(row, tall), :] += total(weight, others)
    sums = jnp.sum(weight, axis=1, keepdims=True)
    for a in range(tall):
        more = to_row(sums[a * BLK : (a + 1) * BLK])
        store_row(sums_ref, row + a, load_row(sums_ref, row + a) + more)


def chip_kernel(
    blocks,
    info,
    x_ref,
    inv_ref,
    chip_ref,
    acc_in,
    sums_in,
    acc_ref,
    sums_ref,
    out_ref,
    inv_row,
    sem,
):
    odd = info[ODD] == 1
    mine, theirs = info[MINE_CHIP], info[THEIRS_CHIP]
    mine_link = info[MINE_LINK]

    def is_done(r):
        return jnp.where(odd, blocks - 1 - r, r) >= mine_link

    def column(n):
        col = jnp.where(odd, blocks - 2 - 2 * n, 2 * n)
        for b in range(2):
            inv_row[b] = to_row(inverse_norm(chip_ref[span(col + b), :]))
        theirs_ok = [jnp.where(odd, blocks - 1 - col - b, col + b) < theirs for b in range(2)]

        def tile(m, carry):
            row = jnp.where(odd, 2 * m, blocks - 2 - 2 * m)
            mine_ok = [jnp.where(odd, row + a, blocks - 1 - row - a) < mine for a in range(2)]
            others = chip_ref[span(col, 2), :]
            other_inv = jnp.concatenate([inv_row[0], inv_row[1]], axis=1)
            used = [[p & q for q in theirs_ok] for p in mine_ok]
            inner = product(x_ref[span(row, 2), :], others)
            weight = weights(inner, inv_ref[span(row, 2), :], other_inv, used)
            add_tile(acc_ref, sums_ref, row, weight, others)
            return carry

        lax.fori_loop(0, lax.div(mine + 1, 2), tile, 0)

    def columns(n, carry):
        column(n)
        return carry

    lax.fori_loop(0, lax.div(theirs + 1, 2), columns, 0)
    each(blocks, is_done, functools.partial(finish, acc_ref, sums_ref, out_ref, sem))
    each(blocks, is_done, lambda r: copy_out(acc_ref, out_ref, sem, r).wait())


def link_kernel(blocks, slots, info, x_ref, inv_ref, *refs):
    got_refs = refs[: len(slots)]
    acc_in, sums_in, out_in, acc_ref, sums_ref, out_ref, *dup_ref, side, inv_row, sem = refs[
        len(slots) :
    ]
    mine, theirs = info[MINE_LINK], info[THEIRS_LINK]
    odd = info[ODD] == 1

    uses = theirs >= slots[0]
    if slots[0] > 2:
        uses = uses & (theirs <= 4)

    @pl.when(uses)
    def _():
        for k, got_ref in enumerate(got_refs):
            block = got_ref[:BLK, :]
            side[k * BLK : (k + 1) * BLK, :] = block
            inv_row[:, k * BLK : (k + 1) * BLK] = to_row(inverse_norm(block))

        def tile(m, carry):
            row = jnp.where(odd, blocks - 2 - 2 * m, 2 * m)
            mine_ok = [jnp.where(odd, blocks - 1 - row - a, row + a) < mine for a in range(2)]
            others = side[...]
            used = [[p & (theirs >= q) for q in slots] for p in mine_ok]
            inner = product(x_ref[span(row, 2), :], others)
            weight = weights(inner, inv_ref[span(row, 2), :], inv_row[...], used)
            add_tile(acc_ref, sums_ref, row, weight, others)
            return carry

        lax.fori_loop(0, lax.div(mine + 1, 2), tile, 0)

    if slots[0] > 2:

        @pl.when((theirs >= 5) & (mine >= 1))
        def _():
            r = link_place(info, 0, blocks)
            acc_ref[span(r), :] += got_refs[0][...].astype(F32)

    def is_done(r):
        last = jnp.clip(theirs, 2, 4)
        now = last == slots[0]
        for slot in slots[1:]:
            now = now | (last == slot)
        return (jnp.where(odd, blocks - 1 - r, r) < mine) & now

    dup_copies = [pltpu.make_async_copy(sums_ref, ref, sem.at[blocks]) for ref in dup_ref]
    for copy in dup_copies:
        copy.start()
    each(blocks, is_done, functools.partial(finish, acc_ref, sums_ref, out_ref, sem))
    each(blocks, is_done, lambda r: copy_out(acc_ref, out_ref, sem, r).wait())
    for copy in dup_copies:
        copy.wait()


def last_kernel(
    blocks, info, x_ref, inv_ref, got_ref, acc_in, sums_in, out_in, dup_in, acc_ref, sums_ref, out_ref, dup_ref, inv_row, sem
):
    mine, theirs = info[MINE_LINK], info[THEIRS_LINK]

    def shift(r):
        return pltpu.make_async_copy(acc_ref.at[span(r), :], out_ref.at[span(r), :], sem.at[r])

    def close(r, more, term):
        sums = load_row(sums_ref, r) + more
        store_row(sums_ref, r, sums)
        acc_ref[span(r), :] = (acc_ref[span(r), :] + term) * (1.0 / to_column(sums))
        shift(r).start()

    @pl.when(theirs == 4)
    def _():
        inv_row[...] = to_row(inverse_norm(got_ref[:BLK, :]))

        def visit(k, carry):
            r = link_place(info, k, blocks)
            others = got_ref[:BLK, :]
            inner = product(x_ref[span(r), :], others)
            weight = weights(inner, inv_ref[span(r), :], inv_row[...])
            more = to_row(jnp.sum(weight, axis=1, keepdims=True))
            close(r, more, total(weight, others))
            return carry

        lax.fori_loop(0, mine, visit, 0)

    for k in range(2):

        @pl.when((theirs >= 5) & (mine > k))
        def _(k=k):
            parts = got_ref[BLK:, :BLK].astype(F32)
            more = jnp.sum(parts[3 * k : 3 * k + 3], axis=0, keepdims=True)
            term = got_ref[:BLK, :].astype(F32) if k else 0.0
            close(link_place(info, k, blocks), more, term)

    @pl.when(theirs >= 4)
    def _():
        dup_copy = pltpu.make_async_copy(sums_ref, dup_ref, sem.at[blocks])
        dup_copy.start()

        def wait(k, carry):
            shift(link_place(info, k, blocks)).wait()
            return carry

        lax.fori_loop(0, mine, wait, 0)
        dup_copy.wait()


def totals_shapes(x):
    length, width = x.shape
    return [
        jax.ShapeDtypeStruct((length, width), F32),
        jax.ShapeDtypeStruct((2 * length // BLK, LANES), F32),
        jax.ShapeDtypeStruct((length, width), F32),
    ]


def chip_pairs(info, x, inv, chip_x, acc, sums):
    length, width = x.shape
    blocks = length // BLK
    return pl.pallas_call(
        functools.partial(chip_kernel, blocks),
        in_specs=[SMEM] + [VMEM] * 5,
        out_specs=[VMEM, VMEM, ANY],
        out_shape=totals_shapes(x),
        scratch_shapes=[pltpu.VMEM((2, 1, BLK), F32), pltpu.SemaphoreType.DMA((blocks,))],
        input_output_aliases={4: 0, 5: 1},
        compiler_params=params(8),
        cost_estimate=pair_cost(12, width),
        name="chip_pairs",
    )(info, x, inv, chip_x, acc, sums)


def link_pairs(slots, info, x, inv, got, acc, sums, out):
    length, width = x.shape
    blocks = length // BLK
    n = len(slots)
    dup = totals_shapes(x)[1:2] * (slots[-1] == 3)
    return pl.pallas_call(
        functools.partial(link_kernel, blocks, slots),
        in_specs=[SMEM] + [VMEM] * (4 + n) + [ANY],
        out_specs=[VMEM, VMEM, ANY] + [ANY] * len(dup),
        out_shape=totals_shapes(x) + dup,
        scratch_shapes=[
            pltpu.VMEM((n * BLK, width), BF16),
            pltpu.VMEM((1, n * BLK), F32),
            pltpu.SemaphoreType.DMA((blocks + 1,)),
        ],
        input_output_aliases={3 + n: 0, 4 + n: 1, 5 + n: 2},
        compiler_params=params(8),
        cost_estimate=pair_cost(6 * n, width),
        name="link_pairs",
    )(info, x, inv, *got, acc, sums, out)


def last_pairs(info, x, inv, got, acc, sums, out, dup):
    length, width = x.shape
    blocks = length // BLK
    return pl.pallas_call(
        functools.partial(last_kernel, blocks),
        in_specs=[SMEM] + [VMEM] * 5 + [ANY] * 2,
        out_specs=[VMEM, VMEM, ANY, ANY],
        out_shape=totals_shapes(x) + totals_shapes(x)[1:2],
        scratch_shapes=[pltpu.VMEM((1, BLK), F32), pltpu.SemaphoreType.DMA((blocks + 1,))],
        input_output_aliases={4: 0, 5: 1, 6: 2, 7: 3},
        compiler_params=params(8),
        cost_estimate=pair_cost(3, width),
        name="last_pairs",
    )(info, x, inv, got, acc, sums, out, dup)[2:]


def per_device(embeddings, pair_blocks, pair_count):
    length, width = embeddings.shape
    blocks = length // BLK
    axes = ("rows", "sub")
    devices = lax.axis_size(axes)
    edges = [(i, i + 1) for i in range(1, devices - 1, 2)]
    edges += [(j, i) for i, j in edges]

    def over_link(array):
        return lax.ppermute(array, axes, edges)

    def over_chip(array):
        return lax.ppermute(array, "sub", [(0, 1), (1, 0)])

    x = embeddings
    one = over_link(prepare(axes, pair_blocks, x))
    chip_x = over_chip(x)
    chip_list = over_chip(pair_blocks)
    acc, sums, inv, inv_row, second, counts = diagonal_pairs(axes, pair_blocks, x, chip_list)
    two = over_link(second)
    acc, sums = rest_pairs(counts, x, inv, inv_row, acc, sums)
    third, shared, info = third_payload(axes, counts, chip_list, x, inv_row, one, sums)
    three = over_link(third)
    acc, sums, out = chip_pairs(info, x, inv, chip_x, acc, sums)
    fourth = fourth_payload(info, x, inv_row, two, sums, shared)
    four = over_link(fourth)
    acc, sums, out = link_pairs((1, 2), info, x, inv, (one, two), acc, sums, out)
    acc, sums, out, dup = link_pairs((3,), info, x, inv, (three,), acc, sums, out)
    out, dup = last_pairs(info, x, inv, four, acc, sums, out, dup)
    return dup.reshape(length), out


def solution(mesh):
    in_specs = (
        P(("groups", "rows", "sub"), None),
        P(None, ("groups", "rows", "sub")),
        P(("groups", "rows", "sub")),
    )
    out_specs = (P(("groups", "rows", "sub")), P(("groups", "rows", "sub"), None))
    return jax.shard_map(
        per_device, mesh=mesh, in_specs=in_specs, out_specs=out_specs, check_vma=False
    )
```

```python
import functools

import jax
import jax.numpy as jnp
from jax import lax
from jax.experimental import pallas as pl
from jax.experimental.pallas import tpu as pltpu
from jax.sharding import PartitionSpec as P

BLK = 256
EXTRA = 16
TEMPER = 4.0
LOG2_E = 1.4426950408889634
NEVER = 1e30
EPS = 1e-06
LANES = 128
MIB = 1024 * 1024

F32 = jnp.float32
BF16 = jnp.bfloat16

ODD, MINE_CHIP, THEIRS_CHIP, MINE_LINK, THEIRS_LINK = range(5)

VMEM = pl.BlockSpec(memory_space=pltpu.VMEM)
SMEM = pl.BlockSpec(memory_space=pltpu.SMEM)
ANY = pl.BlockSpec(memory_space=pl.ANY)
HBM = pl.BlockSpec(memory_space=pltpu.HBM)


def diagonal():
    return lax.broadcasted_iota(jnp.int32, (BLK, BLK), 0) == lax.broadcasted_iota(
        jnp.int32, (BLK, BLK), 1
    )


def to_row(column):
    return jnp.sum(jnp.where(diagonal(), column, 0.0), axis=0, keepdims=True)


def to_column(row):
    return jnp.sum(jnp.where(diagonal(), row, 0.0), axis=1, keepdims=True)


def inverse_norm(rows):
    wide = rows.astype(F32)
    return lax.rsqrt(jnp.sum(wide * wide, axis=1, keepdims=True) + EPS)


def store_row(ref, place, row):
    ref[pl.ds(2 * place, 1), :] = row[:, :LANES]
    ref[pl.ds(2 * place + 1, 1), :] = row[:, LANES:]


def load_row(ref, place):
    return jnp.concatenate([ref[pl.ds(2 * place, 1), :], ref[pl.ds(2 * place + 1, 1), :]], axis=1)


def span(place, n=1):
    return pl.ds(pl.multiple_of(place * BLK, BLK), n * BLK)


def product(rows, others):
    return lax.dot_general(rows, others, (((1,), (1,)), ((), ())), preferred_element_type=F32)


def weights(inner, row_inv, other_inv, used=None):
    scaled = inner * (TEMPER * LOG2_E * row_inv) * other_inv
    if used is None:
        return jnp.exp2(scaled - TEMPER * LOG2_E)
    return jnp.concatenate(
        [
            jnp.concatenate(
                [
                    jnp.exp2(
                        scaled[a * BLK : (a + 1) * BLK, b * BLK : (b + 1) * BLK]
                        - jnp.where(use, TEMPER * LOG2_E, NEVER)
                    )
                    for b, use in enumerate(line)
                ],
                axis=1,
            )
            for a, line in enumerate(used)
        ],
        axis=0,
    )


def total(weight, others):
    return jnp.dot(weight.astype(BF16), others, preferred_element_type=F32)


def pair_cost(pairs, width):
    return pl.CostEstimate(
        flops=pairs * 4 * BLK * BLK * width,
        bytes_accessed=pairs * 2 * BLK * width,
        transcendentals=pairs * BLK * BLK,
    )


def params(mib):
    return pltpu.CompilerParams(vmem_limit_bytes=mib * MIB)


def link_place(info, k, blocks):
    return jnp.where(info[ODD] == 1, blocks - 1 - k, k)


def prep_kernel(blocks, axes, pairs_hbm, x_hbm, pay_ref, pairs, sem):
    base = lax.axis_index(axes) * blocks
    edge = jnp.where(lax.axis_index("sub") == 1, blocks - 1, 0)
    copies = [
        pltpu.make_async_copy(pairs_hbm, pairs, sem.at[0]),
        pltpu.make_async_copy(x_hbm.at[span(edge), :], pay_ref.at[:BLK, :], sem.at[1]),
    ]
    for copy in copies:
        copy.start()
    copies[0].wait()
    tail = lax.fori_loop(
        0,
        pairs.shape[1],
        lambda s, n: n + jnp.where(pairs[1, s] == base + blocks, 1, 0),
        jnp.int32(0),
    )
    pay_ref[BLK:, :] = jnp.full((EXTRA, pay_ref.shape[1]), tail.astype(F32)).astype(BF16)
    copies[1].wait()


def prepare(axes, pair_blocks, x):
    length, width = x.shape
    return pl.pallas_call(
        functools.partial(prep_kernel, length // BLK, axes),
        in_specs=[HBM] * 2,
        out_specs=VMEM,
        out_shape=jax.ShapeDtypeStruct((BLK + EXTRA, width), BF16),
        scratch_shapes=[
            pltpu.SMEM(pair_blocks.shape, jnp.int32),
            pltpu.SemaphoreType.DMA((2,)),
        ],
        compiler_params=params(52),
        cost_estimate=pl.CostEstimate(
            flops=0, bytes_accessed=4 * BLK * width, transcendentals=0
        ),
        name="prepare",
    )(pair_blocks, x)


def count_pairs(blocks, axes, pairs, counts):
    base = lax.axis_index(axes) * blocks
    for r in range(blocks):
        counts[r] = 1

    def count(s, carry):
        r = pairs[0, s] - base
        counts[r] = counts[r] + jnp.where(pairs[1, s] > pairs[0, s], 1, 0)
        return carry

    lax.fori_loop(0, pairs.shape[1], count, 0)
    tail = jnp.int32(0)
    start = jnp.int32(0)
    for r in range(blocks):
        tail += jnp.where(r + counts[r] > blocks, 1, 0)
        if r:
            start = jnp.where(r - 1 + counts[r - 1] == r, r, start)
        counts[blocks + 1 + r] = start
    counts[blocks] = tail


def same_clusters(counts, blocks, row, col):
    return [
        [counts[blocks + 1 + row + a] == counts[blocks + 1 + col + b] for b in range(2)]
        for a in range(2)
    ]


def local_tile(x_ref, inv_ref, inv_row, row, col, same):
    others = x_ref[span(col, 2), :]
    other_inv = jnp.concatenate([inv_row[col], inv_row[col + 1]], axis=1)
    inner = product(x_ref[span(row, 2), :], others)
    return weights(inner, inv_ref[span(row, 2), :], other_inv, same), others


def diagonal_kernel(
    blocks, axes, pairs, after, x_ref, acc_ref, sums_ref, inv_ref, inv_row, pay_ref, counts
):
    odd = lax.axis_index("sub") == 1
    count_pairs(blocks, axes, pairs, counts)
    pay_ref[...] = x_ref[span(jnp.where(odd, blocks - 2, 1)), :]

    def norms(r, carry):
        inv = inverse_norm(x_ref[span(r), :])
        inv_ref[span(r), :] = inv
        inv_row[r] = to_row(inv)
        return carry

    lax.fori_loop(0, blocks, norms, 0)

    def visit(k, carry):
        row = 2 * k
        same = same_clusters(counts, blocks, row, row)
        weight, others = local_tile(x_ref, inv_ref, inv_row, row, row, same)
        acc_ref[span(row, 2), :] = total(weight, others)
        sums = jnp.sum(weight, axis=0, keepdims=True)
        for a in range(2):
            store_row(sums_ref, row + a, sums[:, a * BLK : (a + 1) * BLK])
        return carry

    lax.fori_loop(0, blocks // 2, visit, 0)


def rest_kernel(blocks, counts, x_ref, inv_ref, inv_row, acc_in, sums_in, acc_ref, sums_ref):
    half = blocks // 2

    def visit(k, carry):
        row = 2 * lax.div(k, half)
        col = 2 * lax.rem(k, half)
        same = same_clusters(counts, blocks, row, col)

        @pl.when((row < col) & (same[0][0] | same[0][1] | same[1][0] | same[1][1]))
        def _():
            weight, others = local_tile(x_ref, inv_ref, inv_row, row, col, same)
            add_tile(acc_ref, sums_ref, row, weight, others)
            sums = jnp.sum(weight, axis=0, keepdims=True)
            acc_ref[span(col, 2), :] += lax.dot_general(
                weight.astype(BF16),
                x_ref[span(row, 2), :],
                (((0,), (0,)), ((), ())),
                preferred_element_type=F32,
            )
            for b in range(2):
                more = sums[:, b * BLK : (b + 1) * BLK]
                store_row(sums_ref, col + b, load_row(sums_ref, col + b) + more)

        return carry

    lax.fori_loop(0, half * half, visit, 0)


def diagonal_pairs(axes, pairs, x, after):
    length, width = x.shape
    blocks = length // BLK
    return pl.pallas_call(
        functools.partial(diagonal_kernel, blocks, axes),
        in_specs=[SMEM, SMEM, VMEM],
        out_specs=[VMEM] * 5 + [SMEM],
        out_shape=[
            jax.ShapeDtypeStruct((length, width), F32),
            jax.ShapeDtypeStruct((2 * blocks, LANES), F32),
            jax.ShapeDtypeStruct((length, 1), F32),
            jax.ShapeDtypeStruct((blocks, 1, BLK), F32),
            jax.ShapeDtypeStruct((BLK, width), BF16),
            jax.ShapeDtypeStruct((2 * blocks + 1,), jnp.int32),
        ],
        compiler_params=params(12),
        cost_estimate=pair_cost(2 * blocks, width),
        name="diagonal_pairs",
    )(pairs, after, x)


def rest_pairs(counts, x, inv, inv_row, acc, sums):
    length, width = x.shape
    blocks = length // BLK

    return pl.pallas_call(
        functools.partial(rest_kernel, blocks),
        in_specs=[SMEM] + [VMEM] * 5,
        out_specs=[VMEM] * 2,
        out_shape=totals_shapes(x)[:2],
        input_output_aliases={4: 0, 5: 1},
        compiler_params=params(12),
        cost_estimate=pair_cost(blocks * blocks - 2 * blocks, width),
        name="rest_pairs",
    )(counts, x, inv, inv_row, acc, sums)


def write_payload(blocks, slot, info, x_ref, inv_row, link_ref, pay_ref, sums_ref, acc):
    mine, theirs = info[MINE_LINK], info[THEIRS_LINK]
    shares = (mine >= 5) & (theirs >= slot - 2)

    @pl.when(jnp.logical_not(shares))
    def _():
        pay_ref[:BLK, :] = x_ref[span(link_place(info, slot - 1, blocks)), :]
        store_row(sums_ref, slot - 3, jnp.zeros((1, BLK), F32))

    @pl.when(shares)
    def _():
        link = link_ref[:BLK, :]
        link_inv = inverse_norm(link)
        acc[...] = jnp.zeros_like(acc)

        def add(m, sums):
            low = jnp.where(info[ODD] == 1, blocks - 4 - 2 * m, 2 + 2 * m)
            others = x_ref[span(low, 2), :]
            other_inv = jnp.concatenate([inv_row[low], inv_row[low + 1]], axis=1)
            used = [[link_place(info, low + b, blocks) < mine for b in range(2)]]
            weight = weights(product(link, others), link_inv, other_inv, used)
            acc[...] += total(weight, others)
            return sums + to_row(jnp.sum(weight, axis=1, keepdims=True))

        sums = lax.fori_loop(0, lax.div(mine - 1, 2), add, jnp.zeros((1, BLK), F32))
        pay_ref[:BLK, :] = acc[...].astype(BF16)
        store_row(sums_ref, slot - 3, sums)


def third_kernel(
    blocks, axes, counts, chip_pairs, x_ref, inv_row, link_ref, pay_ref, sums_ref, info, acc
):
    odd = lax.axis_index("sub") == 1
    base = lax.axis_index(axes) * blocks
    slots = chip_pairs.shape[1]
    listed = lax.fori_loop(
        0, slots, lambda s, n: n + jnp.where(chip_pairs[1, s] == base, 1, 0), jnp.int32(0)
    )
    told = jnp.max(link_ref[BLK:, :LANES].astype(F32)).astype(jnp.int32)
    head_theirs = jnp.where(odd, listed, told)
    head_mine = jnp.where(head_theirs > 0, counts[0], 0)
    tail_mine = counts[blocks]
    tail_theirs = counts[blocks - 1] - 1
    info[ODD] = jnp.where(odd, 1, 0)
    info[MINE_CHIP] = jnp.where(odd, head_mine, tail_mine)
    info[THEIRS_CHIP] = jnp.where(odd, head_theirs, tail_theirs)
    info[MINE_LINK] = jnp.where(odd, tail_mine, head_mine)
    info[THEIRS_LINK] = jnp.where(odd, tail_theirs, head_theirs)
    store_row(sums_ref, 1, jnp.zeros((1, BLK), F32))
    write_payload(blocks, 3, info, x_ref, inv_row, link_ref, pay_ref, sums_ref, acc)


def third_payload(axes, counts, chip_list, x, inv_row, link_block, after):
    length, width = x.shape
    blocks = length // BLK

    def kernel(counts, chip_list, x_ref, inv_row, link_ref, after_ref, *refs):
        third_kernel(blocks, axes, counts, chip_list, x_ref, inv_row, link_ref, *refs)

    return pl.pallas_call(
        kernel,
        in_specs=[SMEM, SMEM, VMEM, VMEM, VMEM, ANY],
        out_specs=[VMEM, VMEM, SMEM],
        out_shape=[
            jax.ShapeDtypeStruct((BLK, width), BF16),
            jax.ShapeDtypeStruct((4, LANES), F32),
            jax.ShapeDtypeStruct((8,), jnp.int32),
        ],
        scratch_shapes=[pltpu.VMEM((BLK, width), F32)],
        compiler_params=params(8),
        cost_estimate=pair_cost(2, width),
        name="third_payload",
    )(counts, chip_list, x, inv_row, link_block, after)


def fourth_kernel(
    blocks, info, x_ref, inv_row, link_ref, after_ref, sums_in, pay_ref, sums_ref, acc
):
    write_payload(blocks, 4, info, x_ref, inv_row, link_ref, pay_ref, sums_ref, acc)
    place = lax.broadcasted_iota(jnp.int32, (EXTRA, BLK), 0)
    parts = jnp.zeros((EXTRA, BLK), F32)
    for slot in range(2):
        rest = load_row(sums_ref, slot)
        for k in range(3):
            part = rest.astype(BF16).astype(F32)
            parts = jnp.where(place == 3 * slot + k, part, parts)
            rest = rest - part
    pay_ref[BLK:, :BLK] = parts.astype(BF16)
    pay_ref[BLK:, BLK:] = jnp.zeros((EXTRA, x_ref.shape[1] - BLK), BF16)


def fourth_payload(info, x, inv_row, link_block, after, sums):
    length, width = x.shape
    return pl.pallas_call(
        functools.partial(fourth_kernel, length // BLK),
        in_specs=[SMEM, VMEM, VMEM, VMEM, ANY, VMEM],
        out_specs=[VMEM, VMEM],
        out_shape=[
            jax.ShapeDtypeStruct((BLK + EXTRA, width), BF16),
            jax.ShapeDtypeStruct((4, LANES), F32),
        ],
        input_output_aliases={5: 1},
        scratch_shapes=[pltpu.VMEM((BLK, width), F32)],
        compiler_params=params(8),
        cost_estimate=pair_cost(2, width),
        name="fourth_payload",
    )(info, x, inv_row, link_block, after, sums)[0]


def copy_out(acc_ref, out_ref, sem, r):
    return pltpu.make_async_copy(acc_ref.at[span(r), :], out_ref.at[span(r), :], sem.at[r])


def finish(acc_ref, sums_ref, out_ref, sem, r):
    acc_ref[span(r), :] = acc_ref[span(r), :] * (1.0 / to_column(load_row(sums_ref, r)))
    copy_out(acc_ref, out_ref, sem, r).start()


def each(blocks, chosen, body):
    def step(r, carry):
        @pl.when(chosen(r))
        def _():
            body(r)

        return carry

    lax.fori_loop(0, blocks, step, 0)


def add_tile(acc_ref, sums_ref, row, weight, others, tall=2):
    acc_ref[span(row, tall), :] += total(weight, others)
    sums = jnp.sum(weight, axis=1, keepdims=True)
    for a in range(tall):
        more = to_row(sums[a * BLK : (a + 1) * BLK])
        store_row(sums_ref, row + a, load_row(sums_ref, row + a) + more)


def chip_kernel(
    blocks,
    info,
    x_ref,
    inv_ref,
    chip_ref,
    acc_in,
    sums_in,
    acc_ref,
    sums_ref,
    out_ref,
    inv_row,
    sem,
):
    odd = info[ODD] == 1
    mine, theirs = info[MINE_CHIP], info[THEIRS_CHIP]
    mine_link = info[MINE_LINK]

    def is_done(r):
        return jnp.where(odd, blocks - 1 - r, r) >= mine_link

    def column(n):
        col = jnp.where(odd, blocks - 2 - 2 * n, 2 * n)
        for b in range(2):
            inv_row[b] = to_row(inverse_norm(chip_ref[span(col + b), :]))
        theirs_ok = [jnp.where(odd, blocks - 1 - col - b, col + b) < theirs for b in range(2)]

        def tile(m, carry):
            row = jnp.where(odd, 2 * m, blocks - 2 - 2 * m)
            mine_ok = [jnp.where(odd, row + a, blocks - 1 - row - a) < mine for a in range(2)]
            others = chip_ref[span(col, 2), :]
            other_inv = jnp.concatenate([inv_row[0], inv_row[1]], axis=1)
            used = [[p & q for q in theirs_ok] for p in mine_ok]
            inner = product(x_ref[span(row, 2), :], others)
            weight = weights(inner, inv_ref[span(row, 2), :], other_inv, used)
            add_tile(acc_ref, sums_ref, row, weight, others)
            return carry

        lax.fori_loop(0, lax.div(mine + 1, 2), tile, 0)

    def columns(n, carry):
        column(n)
        return carry

    lax.fori_loop(0, lax.div(theirs + 1, 2), columns, 0)
    each(blocks, is_done, functools.partial(finish, acc_ref, sums_ref, out_ref, sem))
    each(blocks, is_done, lambda r: copy_out(acc_ref, out_ref, sem, r).wait())


def link_kernel(blocks, slots, info, x_ref, inv_ref, *refs):
    got_refs = refs[: len(slots)]
    acc_in, sums_in, out_in, acc_ref, sums_ref, out_ref, *dup_ref, side, inv_row, sem = refs[
        len(slots) :
    ]
    mine, theirs = info[MINE_LINK], info[THEIRS_LINK]
    odd = info[ODD] == 1

    uses = theirs >= slots[0]
    if slots[0] > 2:
        uses = uses & (theirs <= 4)

    @pl.when(uses)
    def _():
        for k, got_ref in enumerate(got_refs):
            block = got_ref[:BLK, :]
            side[k * BLK : (k + 1) * BLK, :] = block
            inv_row[:, k * BLK : (k + 1) * BLK] = to_row(inverse_norm(block))

        def tile(m, carry):
            row = jnp.where(odd, blocks - 2 - 2 * m, 2 * m)
            mine_ok = [jnp.where(odd, blocks - 1 - row - a, row + a) < mine for a in range(2)]
            others = side[...]
            used = [[p & (theirs >= q) for q in slots] for p in mine_ok]
            inner = product(x_ref[span(row, 2), :], others)
            weight = weights(inner, inv_ref[span(row, 2), :], inv_row[...], used)
            add_tile(acc_ref, sums_ref, row, weight, others)
            return carry

        lax.fori_loop(0, lax.div(mine + 1, 2), tile, 0)

    if slots[0] > 2:

        @pl.when((theirs >= 5) & (mine >= 1))
        def _():
            r = link_place(info, 0, blocks)
            acc_ref[span(r), :] += got_refs[0][...].astype(F32)

    def is_done(r):
        last = jnp.clip(theirs, 2, 4)
        now = last == slots[0]
        for slot in slots[1:]:
            now = now | (last == slot)
        return (jnp.where(odd, blocks - 1 - r, r) < mine) & now

    dup_copies = [pltpu.make_async_copy(sums_ref, ref, sem.at[blocks]) for ref in dup_ref]
    for copy in dup_copies:
        copy.start()
    each(blocks, is_done, functools.partial(finish, acc_ref, sums_ref, out_ref, sem))
    each(blocks, is_done, lambda r: copy_out(acc_ref, out_ref, sem, r).wait())
    for copy in dup_copies:
        copy.wait()


def last_kernel(
    blocks, info, x_ref, inv_ref, got_ref, acc_in, sums_in, out_in, dup_in, acc_ref, sums_ref, out_ref, dup_ref, inv_row, sem
):
    mine, theirs = info[MINE_LINK], info[THEIRS_LINK]

    def shift(r):
        return pltpu.make_async_copy(acc_ref.at[span(r), :], out_ref.at[span(r), :], sem.at[r])

    def close(r, more, term):
        sums = load_row(sums_ref, r) + more
        store_row(sums_ref, r, sums)
        acc_ref[span(r), :] = (acc_ref[span(r), :] + term) * (1.0 / to_column(sums))
        shift(r).start()

    @pl.when(theirs == 4)
    def _():
        inv_row[...] = to_row(inverse_norm(got_ref[:BLK, :]))

        def visit(k, carry):
            r = link_place(info, k, blocks)
            others = got_ref[:BLK, :]
            inner = product(x_ref[span(r), :], others)
            weight = weights(inner, inv_ref[span(r), :], inv_row[...])
            more = to_row(jnp.sum(weight, axis=1, keepdims=True))
            close(r, more, total(weight, others))
            return carry

        lax.fori_loop(0, mine, visit, 0)

    for k in range(2):

        @pl.when((theirs >= 5) & (mine > k))
        def _(k=k):
            parts = got_ref[BLK:, :BLK].astype(F32)
            more = jnp.sum(parts[3 * k : 3 * k + 3], axis=0, keepdims=True)
            term = got_ref[:BLK, :].astype(F32) if k else 0.0
            close(link_place(info, k, blocks), more, term)

    @pl.when(theirs >= 4)
    def _():
        dup_copy = pltpu.make_async_copy(sums_ref, dup_ref, sem.at[blocks])
        dup_copy.start()

        def wait(k, carry):
            shift(link_place(info, k, blocks)).wait()
            return carry

        lax.fori_loop(0, mine, wait, 0)
        dup_copy.wait()


def totals_shapes(x):
    length, width = x.shape
    return [
        jax.ShapeDtypeStruct((length, width), F32),
        jax.ShapeDtypeStruct((2 * length // BLK, LANES), F32),
        jax.ShapeDtypeStruct((length, width), F32),
    ]


def chip_pairs(info, x, inv, chip_x, acc, sums):
    length, width = x.shape
    blocks = length // BLK
    return pl.pallas_call(
        functools.partial(chip_kernel, blocks),
        in_specs=[SMEM] + [VMEM] * 5,
        out_specs=[VMEM, VMEM, ANY],
        out_shape=totals_shapes(x),
        scratch_shapes=[pltpu.VMEM((2, 1, BLK), F32), pltpu.SemaphoreType.DMA((blocks,))],
        input_output_aliases={4: 0, 5: 1},
        compiler_params=params(8),
        cost_estimate=pair_cost(12, width),
        name="chip_pairs",
    )(info, x, inv, chip_x, acc, sums)


def link_pairs(slots, info, x, inv, got, acc, sums, out):
    length, width = x.shape
    blocks = length // BLK
    n = len(slots)
    dup = totals_shapes(x)[1:2] * (slots[-1] == 3)
    return pl.pallas_call(
        functools.partial(link_kernel, blocks, slots),
        in_specs=[SMEM] + [VMEM] * (4 + n) + [ANY],
        out_specs=[VMEM, VMEM, ANY] + [ANY] * len(dup),
        out_shape=totals_shapes(x) + dup,
        scratch_shapes=[
            pltpu.VMEM((n * BLK, width), BF16),
            pltpu.VMEM((1, n * BLK), F32),
            pltpu.SemaphoreType.DMA((blocks + 1,)),
        ],
        input_output_aliases={3 + n: 0, 4 + n: 1, 5 + n: 2},
        compiler_params=params(8),
        cost_estimate=pair_cost(6 * n, width),
        name="link_pairs",
    )(info, x, inv, *got, acc, sums, out)


def last_pairs(info, x, inv, got, acc, sums, out, dup):
    length, width = x.shape
    blocks = length // BLK
    return pl.pallas_call(
        functools.partial(last_kernel, blocks),
        in_specs=[SMEM] + [VMEM] * 5 + [ANY] * 2,
        out_specs=[VMEM, VMEM, ANY, ANY],
        out_shape=totals_shapes(x) + totals_shapes(x)[1:2],
        scratch_shapes=[pltpu.VMEM((1, BLK), F32), pltpu.SemaphoreType.DMA((blocks + 1,))],
        input_output_aliases={4: 0, 5: 1, 6: 2, 7: 3},
        compiler_params=params(8),
        cost_estimate=pair_cost(3, width),
        name="last_pairs",
    )(info, x, inv, got, acc, sums, out, dup)[2:]


def per_device(embeddings, pair_blocks, pair_count):
    length, width = embeddings.shape
    blocks = length // BLK
    axes = ("rows", "sub")
    devices = lax.axis_size(axes)
    edges = [(i, i + 1) for i in range(1, devices - 1, 2)]
    edges += [(j, i) for i, j in edges]

    def over_link(array):
        return lax.ppermute(array, axes, edges)

    def over_chip(array):
        return lax.ppermute(array, "sub", [(0, 1), (1, 0)])

    x = embeddings
    one = over_link(prepare(axes, pair_blocks, x))
    chip_x = over_chip(x)
    chip_list = over_chip(pair_blocks)
    acc, sums, inv, inv_row, second, counts = diagonal_pairs(axes, pair_blocks, x, chip_list)
    two = over_link(second)
    acc, sums = rest_pairs(counts, x, inv, inv_row, acc, sums)
    third, shared, info = third_payload(axes, counts, chip_list, x, inv_row, one, sums)
    three = over_link(third)
    acc, sums, out = chip_pairs(info, x, inv, chip_x, acc, sums)
    fourth = fourth_payload(info, x, inv_row, two, sums, shared)
    four = over_link(fourth)
    acc, sums, out = link_pairs((1, 2), info, x, inv, (one, two), acc, sums, out)
    acc, sums, out, dup = link_pairs((3,), info, x, inv, (three,), acc, sums, out)
    out, dup = last_pairs(info, x, inv, four, acc, sums, out, dup)
    return dup.reshape(length), out


def solution(mesh):
    in_specs = (
        P(("groups", "rows", "sub"), None),
        P(None, ("groups", "rows", "sub")),
        P(("groups", "rows", "sub")),
    )
    out_specs = (P(("groups", "rows", "sub")), P(("groups", "rows", "sub"), None))
    return jax.shard_map(
        per_device, mesh=mesh, in_specs=in_specs, out_specs=out_specs, check_vma=False
    )
```
